256 devices in a mesh: lat: 16 (over z, core), lon: 16 (over x, y).
Axes of the slice: x: 4, y: 4, z: 8, core: 2. Of those that a mesh axis runs over, the one named last changes fastest.
Arguments:
- adjoint_state: float32 [3, 12, 256, 5760], P(None, None, 'lat', 'lon'), may hold values from -6 to 6
- innovation: float32 [3, 12, 256, 5760], P(None, None, 'lat', 'lon'), may hold values from -6 to 6
- coefficients: float32 [3, 5, 12, 256, 5760], P(None, None, None, 'lat', 'lon'), may hold values from 0.1 to 0.6
- polar_mask: int32 [256], P('lat'), may hold values from 0 to 1, as said below
- wave_cutoff: int32 [256], P('lat'), may hold values from 1 to 64, as said below
Outputs:
- adjoint_start: float32 [3, 12, 256, 5760], P(None, None, 'lat', 'lon')
The draws below stay inside these ranges and needn't reach their ends.
Inputs may be any that keep to these rules, and one draw needn't show every extreme that they name: polar_mask is 1 on every row within 8 rows of either pole, 0 on every row 16 or more rows from both poles, and either on the rows between. `wave_cutoff`: rows with polar_mask 0 have the cutoff 64.
All inputs are finite; a program needn't handle non-finite values.
Results may differ from the reference program's by a relative error of at most 0.00008.
Values sent between devices are 32-bit elements; how exact they have to be, the bound alone decides.
No kernel may reach another device: no remote copies, remote signals or barrier semaphores. Data moves between devices by JAX's collectives and lax.ppermute only.
A program may use at most 128 MiB of HBM per device.

```python
import math
import jax
import jax.numpy as jnp
from jax import lax

NLON = 5760
LEV = 12
LAT_DEV = 16
FIELDS = 3
KMAX = 64
NLAT = 256


def polar_tables(key):
    row_index = jnp.arange(NLAT, dtype=jnp.int32)
    distance = jnp.minimum(row_index, NLAT - 1 - row_index)
    coin = jax.random.randint(jax.random.fold_in(key, 11), (NLAT,), 0, 2)
    inner = (distance < LAT_DEV // 2).astype(jnp.int32)
    between = ((distance >= LAT_DEV // 2) & (distance < LAT_DEV)).astype(jnp.int32)
    row_mask = inner + between * coin
    jitter = jax.random.randint(jax.random.fold_in(key, 12), (NLAT,), 0, 8)
    cutoff = jnp.clip((distance + 1) * KMAX // LAT_DEV + jitter, 1, KMAX)
    cutoff = jnp.where(row_mask == 1, cutoff, KMAX).astype(jnp.int32)
    return (row_mask.astype(jnp.int32), cutoff)


def draw_polar_mask(key, part):
    return polar_tables(key)[0]


def draw_wave_cutoff(key, part):
    return polar_tables(key)[1]


def level_of(rng, dims, shards, low, high):
    def one(dim, parts):
        draws = jax.random.uniform(jax.random.fold_in(jax.random.fold_in(rng, 6), dim), (parts,), jnp.float32, low / len(shards), high / len(shards))
        return jnp.repeat(jnp.exp(draws), dims[dim] // parts).reshape((-1,) + (1,) * (len(dims) - dim - 1))

    loudness = one(*shards[0])
    for cut in shards[1:]:
        loudness = loudness * one(*cut)
    return loudness


def noise(rng, dims, deviation, reach, split=(), held_as=jnp.bfloat16):
    values = jax.random.normal(rng, dims, jnp.float32) * deviation
    if len(split) > 0:
        values = level_of(rng, dims, split, -0.22, 0.18) * values
    return jnp.clip(values, min=-reach, max=reach).astype(held_as)


def setup_inputs(seed: int = 0) -> dict:
    key_list = jax.random.split(jax.random.key(seed), 6)
    return {
        "adjoint_state": noise(key_list[0], (FIELDS, LEV, NLAT, NLON), 1.0, 6.0, ((2, 16), (3, 16)), jnp.float32),
        "innovation": noise(key_list[1], (FIELDS, LEV, NLAT, NLON), 1.0, 6.0, ((2, 16), (3, 16)), jnp.float32),
        "coefficients": jnp.clip(0.1 + 0.5 * jax.random.uniform(key_list[2], (FIELDS, 5, LEV, NLAT, NLON), jnp.float32) ** level_of(key_list[2], (FIELDS, 5, LEV, NLAT, NLON), ((3, 16), (4, 16)), -0.2, 0.2), 0.1, 0.6),
        "polar_mask": draw_polar_mask(jax.random.fold_in(key_list[5], 71), 0),
        "wave_cutoff": draw_wave_cutoff(jax.random.fold_in(key_list[5], 71), 0),
    }


def wave_tables(columns):
    wave_index = jnp.arange(KMAX, dtype=jnp.int32)
    phases = columns[:, None] * wave_index[None, :] % NLON
    radians = phases.astype(jnp.float32) * (2.0 * math.pi / NLON)
    return (jnp.cos(radians), jnp.sin(radians))

def spectral_response(cutoff_float):
    wave_float = jnp.arange(KMAX).astype(jnp.float32)
    cutoff_col = cutoff_float[:, None]
    ratio = cutoff_col / jnp.maximum(wave_float, 1.0)[None, :]
    response = jnp.where(wave_float[None, :] <= cutoff_col, 1.0, ratio * ratio)
    weights = jnp.where(wave_float == 0.0, 1.0 / NLON, 2.0 / NLON)
    return (response * weights[None, :]).astype(jnp.float32)

def polar_filter(field, polar_mask, wave_cutoff):
    highest = lax.Precision.HIGHEST
    cosines, sines = wave_tables(jnp.arange(NLON, dtype=jnp.int32))
    real_part = jnp.einsum('flrj,jk->flrk', field, cosines, precision=highest)
    imag_part = jnp.einsum('flrj,jk->flrk', field, sines, precision=highest)
    response = spectral_response(wave_cutoff.astype(jnp.float32))
    filtered = jnp.einsum('flrk,jk->flrj', real_part * response, cosines, precision=highest)
    filtered = filtered + jnp.einsum('flrk,jk->flrj', imag_part * response, sines, precision=highest)
    row_weight = polar_mask.astype(jnp.float32)[:, None]
    return field + row_weight * (filtered - field)

def stencil(field, coefficients):
    pole_sign = jnp.array([-1.0, -1.0, 1.0], dtype=jnp.float32).reshape(3, 1, 1, 1)
    across = jnp.roll(field, NLON // 2, axis=3)
    north_ghost = pole_sign * across[:, :, -1:]
    south_ghost = pole_sign * across[:, :, :1]
    north_val = jnp.concatenate([field[:, :, 1:], north_ghost], axis=2)
    south_val = jnp.concatenate([south_ghost, field[:, :, :-1]], axis=2)
    east_val = jnp.roll(field, -1, axis=3)
    west_val = jnp.roll(field, 1, axis=3)
    result = coefficients[:, 0] * field + coefficients[:, 1] * north_val
    result = result + coefficients[:, 2] * south_val + coefficients[:, 3] * east_val
    return result + coefficients[:, 4] * west_val

def stencil_adjoint(adjoint, coefficients):
    zeros_in = jnp.zeros_like(adjoint)
    pullback = jax.vjp(lambda field: stencil(field, coefficients), zeros_in)[1]
    return pullback(adjoint)[0]

def reference(adjoint_state, innovation, coefficients, polar_mask, wave_cutoff):
    middle = stencil_adjoint(polar_filter(adjoint_state, polar_mask, wave_cutoff), coefficients) + innovation
    return stencil_adjoint(polar_filter(middle, polar_mask, wave_cutoff), coefficients)
```

```python
import math

import jax
import jax.numpy as jnp
import numpy as np
from jax import lax
from jax.experimental import pallas as pl
from jax.experimental.pallas import tpu as pltpu
from jax.sharding import PartitionSpec as P

NLON = 5760
KMAX = 64
WAVES = 2 * KMAX
FIELDS = 3
LEV = 12
BAND = 16
LON_DEV = 16
LAT_DEV = 16
WIDTH = NLON // LON_DEV
WIDE = 384
SLABS = FIELDS * LEV
ROWS = SLABS * BAND
SHARE = WAVES // LON_DEV
HIGHEST = lax.Precision.HIGHEST


def wave_tables():
    columns = np.concatenate([np.arange(WIDTH), [WIDTH, -1]])
    phases = (np.arange(LON_DEV)[:, None] * WIDTH + columns[None, :]) % NLON
    phases = phases[:, None, :] * np.arange(KMAX)[None, :, None] % NLON
    radians = phases * (2.0 * math.pi / NLON)
    both = np.concatenate([np.cos(radians), np.sin(radians)], axis=1)
    return np.pad(both, ((0, 0), (0, 0), (0, WIDE - WIDTH - 2))).astype(np.float32)


def dot(left, right, left_dim, right_dim):
    return lax.dot_general(
        left,
        right,
        (((left_dim,), (right_dim,)), ((), ())),
        precision=HIGHEST,
        preferred_element_type=jnp.float32,
    )


def iota(shape, dim):
    return lax.broadcasted_iota(jnp.int32, shape, dim)


def whole(shape):
    return pl.BlockSpec(shape, lambda i, *_: (0,) * len(shape))


TABLE = pl.BlockSpec((1, WAVES, WIDE), lambda i, place, *_: (place[0], 0, 0))


def launch(kernel, scalars, operands, in_specs, out_shapes, scratch=(), flops=0):
    nbytes = sum(4 * math.prod(shape) for shape in out_shapes)
    nbytes += sum(4 * math.prod(spec.block_shape) for spec in in_specs)
    return pl.pallas_call(
        kernel,
        grid_spec=pltpu.PrefetchScalarGridSpec(
            num_scalar_prefetch=len(scalars),
            grid=(1,),
            in_specs=in_specs,
            out_specs=[whole(shape) for shape in out_shapes],
            scratch_shapes=list(scratch),
        ),
        out_shape=[jax.ShapeDtypeStruct(shape, jnp.float32) for shape in out_shapes],
        compiler_params=pltpu.CompilerParams(vmem_limit_bytes=50 * 2**20),
        cost_estimate=pl.CostEstimate(flops=flops, bytes_accessed=nbytes, transcendentals=0),
    )(*scalars, *operands)


FIELD = (FIELDS, LEV, BAND, WIDTH)
COEFF = (FIELDS, 5, LEV, BAND, WIDTH)
CHUNKS = (LON_DEV, SHARE, ROWS)
LINE = (SLABS, WIDTH)
EDGES = (8, ROWS)


def forward_kernel(place, table, field, send):
    waves = dot(table[0][:, :WIDTH], field[...].reshape(ROWS, WIDTH), 1, 1)
    send[...] = waves.reshape(CHUNKS)


def respond_kernel(place, cutoff, received, send):
    total = received[0]
    for source in range(1, LON_DEV):
        total = total + received[source]
    shape = (SHARE, ROWS)
    wave = (place[0] * SHARE + iota(shape, 0)) % KMAX
    row = iota(shape, 1) % BAND
    limit = jnp.zeros(shape, jnp.int32)
    for r in range(BAND):
        limit = jnp.where(row == r, cutoff[r], limit)
    ratio = limit.astype(jnp.float32) / jnp.maximum(wave, 1).astype(jnp.float32)
    response = jnp.where(wave <= limit, 1.0, ratio * ratio)
    response = response * jnp.where(wave == 0, 1.0 / NLON, 2.0 / NLON)
    total = total * response
    for target in range(LON_DEV):
        send[target] = total


def edge_kernel(place, west_field, east_field, to_east, to_west, north, south, edges, across):
    shape = (ROWS, 128)
    last = (WIDTH - 1) % 128
    first_x = west_field[...].reshape(shape)[:, 0:1]
    last_x = east_field[...].reshape(shape)[:, last : last + 1]
    last_c = to_east[...].reshape(shape)[:, last : last + 1]
    first_c = to_west[...].reshape(shape)[:, 0:1]
    lane = iota(shape, 1)
    packed = jnp.where(lane == 0, last_c * last_x, 0.0)
    packed = jnp.where(lane == 1, last_c, packed)
    packed = jnp.where(lane == 2, first_c * first_x, packed)
    packed = jnp.where(lane == 3, first_c, packed)
    edges[...] = packed.T[0:8]
    lat = place[1]

    def one(slab, _):
        field, level = slab // LEV, slab % LEV
        sign = jnp.where(field == FIELDS - 1, 1.0, -1.0)
        top = north[field, 0, level, BAND - 1 : BAND]
        bottom = south[field, 0, level, 0:1]
        line = jnp.where(lat == LAT_DEV - 1, top, jnp.where(lat == 0, bottom, 0.0))
        across[pl.ds(slab, 1)] = sign * line
        return 0

    lax.fori_loop(0, SLABS, one, 0)


def gather_terms(value, coeff, south_line, north_line, west_edge, east_edge):
    to_north, to_south = coeff[1] * value, coeff[2] * value
    total = coeff[0] * value
    total = total + jnp.concatenate([south_line, to_north[:-1]], axis=0)
    total = total + jnp.concatenate([to_south[1:], north_line], axis=0)
    total = total + jnp.concatenate([west_edge, (coeff[3] * value)[:, :-1]], axis=1)
    total = total + jnp.concatenate([(coeff[4] * value)[:, 1:], east_edge], axis=1)
    return total, to_north, to_south


def load_coeff(coeff, field, level):
    return [coeff[field, term, level] for term in range(5)]


def edge_columns(from_west, from_east):
    row = iota(EDGES, 0)
    return jnp.where(row < 2, from_west[...], from_east[...]).T


def line_kernel(place, field_ref, extra, coeff_ref, from_west, from_east, to_north, to_south, columns):
    columns[...] = edge_columns(from_west, from_east)

    def one(slab, _):
        field, level = slab // LEV, slab % LEV
        value = field_ref[field, level]
        coeff = load_coeff(coeff_ref, field, level)
        edge = columns[pl.ds(slab * BAND, BAND)]
        none = jnp.zeros((1, WIDTH), jnp.float32)
        total, north, south = gather_terms(value, coeff, none, none, edge[:, 0:1], edge[:, 2:3])
        total = total + extra[field, level]
        here = pl.ds(slab, 1)
        to_north[0, here] = total[BAND - 1 :]
        to_north[1, here] = coeff[1][BAND - 1 :]
        to_north[2, here] = north[BAND - 1 :]
        to_south[0, here] = total[0:1]
        to_south[1, here] = coeff[2][0:1]
        to_south[2, here] = south[0:1]
        return 0

    lax.fori_loop(0, SLABS, one, 0)


def row_weight(mask):
    row = iota((BAND, WIDTH), 0)
    weight = jnp.zeros((BAND, WIDTH), jnp.float32)
    for r in range(BAND):
        weight = jnp.where(row == r, mask[r].astype(jnp.float32), weight)
    return weight


def one_row(waves, table, row, opposite):
    picked = (iota((ROWS, 128), 0) == iota((ROWS, 128), 1) * BAND + row).astype(jnp.float32)
    chosen = dot(waves, picked, 1, 0)
    if opposite:
        chosen = jnp.where(iota((WAVES, 128), 0) % 2 == 1, -chosen, chosen)
    return dot(chosen, table, 0, 0)


def middle_kernel(
    place, mask, waves_ref, table, state, extra, coeff_ref, from_west, from_east,
    below, above, across,
    middle, send, row_out, kept, lines,
    filtered, opposite, columns,
):
    lat = place[1]
    top = lat == LAT_DEV - 1
    waves = waves_ref[...].reshape(WAVES, ROWS)
    filtered[...] = dot(waves, table[0], 0, 0)
    polar_row = jnp.where(top, BAND - 1, 0)
    opposite[...] = one_row(waves, table[0], polar_row, True)
    columns[...] = edge_columns(from_west, from_east)
    weight = row_weight(mask)
    row = iota((BAND, WIDTH), 0)

    def one(slab, _):
        field, level = slab // LEV, slab % LEV
        here = pl.ds(slab, 1)
        value = state[field, level]
        smooth = filtered[pl.ds(slab * BAND, BAND)]
        edge = columns[pl.ds(slab * BAND, BAND)]
        value = value + weight * (smooth[:, :WIDTH] - value)
        coeff = load_coeff(coeff_ref, field, level)
        edge_weight = weight[:, 0:1]
        west = edge[:, 0:1]
        west = west + edge_weight * (edge[:, 1:2] * smooth[:, WIDTH + 1 : WIDTH + 2] - west)
        east = edge[:, 2:3]
        east = east + edge_weight * (edge[:, 3:4] * smooth[:, WIDTH : WIDTH + 1] - east)
        total, north, south = gather_terms(value, coeff, below[2, here], above[2, here], west, east)
        pole = across[here] * opposite[here][:, :WIDTH]
        total = total + jnp.where(row == polar_row, pole, 0.0) + extra[field, level]
        middle[field, level] = total
        row_out[here] = jnp.where(top, south[0:1], north[BAND - 1 :])
        kept[0, here] = jnp.where(top, total[0:1], total[BAND - 1 :])
        kept[1, here] = jnp.where(top, coeff[2][0:1], coeff[1][BAND - 1 :])
        lines[0, here] = below[1, here] * (below[0, here] + south[0:1])
        lines[1, here] = above[1, here] * (above[0, here] + north[BAND - 1 :])
        return 0

    lax.fori_loop(0, SLABS, one, 0)
    waves = dot(table[0][:, :WIDTH], middle[...].reshape(ROWS, WIDTH), 1, 1)
    send[...] = waves.reshape(CHUNKS)


def mend_row(lat):
    return jnp.where(lat == 1, 0, BAND - 1)


def second_edge_kernel(place, west_field, east_field, to_east, to_west, line, edges, packed):
    row = iota((BAND, 128), 0)
    lane = iota((BAND, 128), 1)
    last = (WIDTH - 1) % 128
    mend = mend_row(place[1])

    def one(slab, _):
        field, level = slab // LEV, slab % LEV
        here = pl.ds(slab, 1)
        reached = line[here]
        fix = jnp.where(row == mend, reached[:, 0:128], 0.0)
        west = (west_field[field, level] + fix) * to_west[field, 0, level]
        tail = (WIDTH - 1) // 128 * 128
        pad = jnp.zeros((1, 128 - (WIDTH - tail)), jnp.float32)
        fix = jnp.where(row == mend, jnp.concatenate([reached[:, tail:WIDTH], pad], axis=1), 0.0)
        east = (east_field[field, level] + fix) * to_east[field, 0, level]
        both = jnp.where(lane == 0, east[:, last : last + 1], 0.0)
        both = jnp.where(lane == 2, west[:, 0:1], both)
        packed[pl.ds(slab * BAND, BAND)] = both
        return 0

    lax.fori_loop(0, SLABS, one, 0)
    edges[...] = packed[...].T[0:8]


def row_kernel(place, mask, waves_ref, table, kept, row_out):
    top = place[1] == LAT_DEV - 1
    waves = waves_ref[...].reshape(WAVES, ROWS)
    smooth = one_row(waves, table[0], jnp.where(top, 0, BAND - 1), False)[:SLABS, :WIDTH]
    weight = jnp.where(top, mask[0], mask[BAND - 1]).astype(jnp.float32)
    value = kept[0]
    row_out[...] = kept[1] * (value + weight * (smooth - value))


def final_kernel(
    place, mask, waves_ref, table, middle, mend_line, coeff_ref, first_west, first_east,
    from_west, from_east, lines, polar_line, across,
    out,
    filtered, opposite, columns, firsts,
):
    lat = place[1]
    waves = waves_ref[...].reshape(WAVES, ROWS)
    filtered[...] = dot(waves, table[0], 0, 0)
    polar_row = jnp.where(lat == LAT_DEV - 1, BAND - 1, 0)
    opposite[...] = one_row(waves, table[0], polar_row, True)
    columns[...] = edge_columns(from_west, from_east)
    firsts[...] = edge_columns(first_west, first_east)
    weight = row_weight(mask)
    row = iota((BAND, WIDTH), 0)
    mend = mend_row(lat)

    def one(slab, _):
        field, level = slab // LEV, slab % LEV
        here = pl.ds(slab, 1)
        value = middle[field, level] + jnp.where(row == mend, mend_line[here], 0.0)
        smooth = filtered[pl.ds(slab * BAND, BAND)]
        edge = columns[pl.ds(slab * BAND, BAND)]
        first = firsts[pl.ds(slab * BAND, BAND)]
        value = value + weight * (smooth[:, :WIDTH] - value)
        coeff = load_coeff(coeff_ref, field, level)
        edge_weight = weight[:, 0:1]
        west = edge[:, 0:1]
        west = west + edge_weight * (first[:, 1:2] * smooth[:, WIDTH + 1 : WIDTH + 2] - west)
        east = edge[:, 2:3]
        east = east + edge_weight * (first[:, 3:4] * smooth[:, WIDTH : WIDTH + 1] - east)
        total, _, _ = gather_terms(value, coeff, lines[0, here], lines[1, here], west, east)
        pole = across[here] * opposite[here][:, :WIDTH]
        total = total + jnp.where(row == polar_row, pole, 0.0)
        out[field, level] = total + jnp.where(row == mend, polar_line[here], 0.0)
        return 0

    lax.fori_loop(0, SLABS, one, 0)


def exchanged(chunks):
    return lax.all_to_all(chunks, "lon", split_axis=0, concat_axis=0, tiled=True)


def local(adjoint_state, innovation, coefficients, polar_mask, wave_cutoff):
    lon, lat = lax.axis_index("lon"), lax.axis_index("lat")
    place = jnp.stack([lon, lat]).astype(jnp.int32)
    table = jnp.asarray(wave_tables())
    field, coeff, chunks, line, edges = map(whole, (FIELD, COEFF, CHUNKS, LINE, EDGES))
    three, two = whole((3, *LINE)), whole((2, *LINE))
    wave_scratch = [pltpu.VMEM((ROWS, WIDE), jnp.float32), pltpu.VMEM((128, WIDE), jnp.float32)]
    column_scratch = pltpu.VMEM((ROWS, 8), jnp.float32)

    part = (FIELDS, LEV, BAND, 128)
    tail = (WIDTH - 1) // 128
    west_part = pl.BlockSpec(part, lambda i, *_: (0, 0, 0, 0))
    east_part = pl.BlockSpec(part, lambda i, *_: (0, 0, 0, tail))

    def term_part(term, lane):
        return pl.BlockSpec((FIELDS, 1, LEV, BAND, 128), lambda i, *_: (0, term, 0, 0, lane))

    def term_whole(term):
        return pl.BlockSpec((FIELDS, 1, LEV, BAND, WIDTH), lambda i, *_: (0, term, 0, 0, 0))

    eastward = [(i, (i + 1) % LON_DEV) for i in range(LON_DEV)]
    westward = [(target, source) for source, target in eastward]
    opposite = [(i, (i + LON_DEV // 2) % LON_DEV) for i in range(LON_DEV)]
    northward = [(i, i + 1) for i in range(1, LAT_DEV - 1)]
    southward = [(i, i - 1) for i in range(1, LAT_DEV - 1)]
    last = (LAT_DEV - 1) * LON_DEV
    from_polar = [(i, LON_DEV + i) for i in range(LON_DEV)]
    from_polar += [(last + i, last - LON_DEV + i) for i in range(LON_DEV)]

    (send,) = launch(forward_kernel, [place], [table, adjoint_state], [TABLE, field], [CHUNKS])
    received = exchanged(send)
    first_edges, cross = launch(
        edge_kernel,
        [place],
        [adjoint_state, adjoint_state, coefficients, coefficients, coefficients, coefficients],
        [west_part, east_part, term_part(3, tail), term_part(4, 0), term_whole(1), term_whole(2)],
        [EDGES, LINE],
    )
    first_west = lax.ppermute(first_edges, "lon", eastward)
    first_east = lax.ppermute(first_edges, "lon", westward)
    across = lax.ppermute(cross, "lon", opposite)
    (send,) = launch(respond_kernel, [place, wave_cutoff], [received], [chunks], [CHUNKS])
    waves = exchanged(send)
    to_north, to_south = launch(
        line_kernel,
        [place],
        [adjoint_state, innovation, coefficients, first_west, first_east],
        [field, field, coeff, edges, edges],
        [(3, *LINE), (3, *LINE)],
        [column_scratch],
    )
    below = lax.ppermute(to_north, "lat", northward)
    above = lax.ppermute(to_south, "lat", southward)
    middle, send, row, kept, lines = launch(
        middle_kernel,
        [place, polar_mask],
        [waves, table, adjoint_state, innovation, coefficients, first_west, first_east, below, above, across],
        [chunks, TABLE, field, field, coeff, edges, edges, three, three, line],
        [FIELD, CHUNKS, LINE, (2, *LINE), (2, *LINE)],
        [*wave_scratch, column_scratch],
    )
    received = exchanged(send)
    mend_line = lax.ppermute(row, ("lat", "lon"), from_polar)
    (second_edges,) = launch(
        second_edge_kernel,
        [place],
        [middle, middle, coefficients, coefficients, mend_line],
        [west_part, east_part, term_part(3, tail), term_part(4, 0), line],
        [EDGES],
        [pltpu.VMEM((ROWS, 128), jnp.float32)],
    )
    second_west = lax.ppermute(second_edges, "lon", eastward)
    second_east = lax.ppermute(second_edges, "lon", westward)
    (send,) = launch(respond_kernel, [place, wave_cutoff], [received], [chunks], [CHUNKS])
    waves = exchanged(send)
    (row,) = launch(row_kernel, [place, polar_mask], [waves, table, kept], [chunks, TABLE, two], [LINE])
    polar_line = lax.ppermute(row, ("lat", "lon"), from_polar)
    (out,) = launch(
        final_kernel,
        [place, polar_mask],
        [waves, table, middle, mend_line, coefficients, first_west, first_east, second_west, second_east, lines, polar_line, across],
        [chunks, TABLE, field, line, coeff, edges, edges, edges, edges, two, line, line],
        [FIELD],
        [*wave_scratch, column_scratch, column_scratch],
    )
    return out


def solution(mesh):
    return jax.shard_map(
        local,
        mesh=mesh,
        in_specs=(
            P(None, None, "lat", "lon"),
            P(None, None, "lat", "lon"),
            P(None, None, None, "lat", "lon"),
            P("lat"),
            P("lat"),
        ),
        out_specs=P(None, None, "lat", "lon"),
        check_vma=False,
    )
```

```python
import math

import jax
import jax.numpy as jnp
import numpy as np
from jax import lax
from jax.experimental import pallas as pl
from jax.experimental.pallas import tpu as pltpu
from jax.sharding import PartitionSpec as P

NLON = 5760
KMAX = 64
WAVES = 2 * KMAX
FIELDS = 3
LEV = 12
BAND = 16
HALF = BAND // 2
LON_DEV = 16
LAT_DEV = 16
TOP = LAT_DEV - 1
WIDTH = NLON // LON_DEV
WIDE = 384
SLABS = FIELDS * LEV
ROWS = SLABS * BAND
SHARE = WAVES // LON_DEV
UNROLL = 6
HIGHEST = lax.Precision.HIGHEST

FIELD = (FIELDS, LEV, BAND, WIDTH)
HALF_FIELD = (FIELDS, LEV, HALF, WIDTH)
COEFF = (FIELDS, 5, LEV, BAND, WIDTH)
CHUNKS = (LON_DEV, SHARE, ROWS + 64)
LINE = (SLABS, WIDTH)
LINES = (3, SLABS, WIDTH)
TILES = (2, HALF, 128)
EDGES = (2, BAND, 128)


def wave_tables():
    columns = np.concatenate([np.arange(WIDTH), [WIDTH, -1]])
    phases = (np.arange(LON_DEV)[:, None] * WIDTH + columns[None, :]) % NLON
    phases = phases[:, None, :] * np.arange(KMAX)[None, :, None] % NLON
    radians = phases * (2.0 * math.pi / NLON)
    both = np.concatenate([np.cos(radians), np.sin(radians)], axis=1)
    return np.pad(both, ((0, 0), (0, 0), (0, WIDE - WIDTH - 2))).astype(np.float32)


def dot(left, right, left_dim, right_dim):
    return lax.dot_general(
        left,
        right,
        (((left_dim,), (right_dim,)), ((), ())),
        precision=HIGHEST,
        preferred_element_type=jnp.float32,
    )


def iota(shape, dim):
    return lax.broadcasted_iota(jnp.int32, shape, dim)


def in_vmem(shape):
    return pltpu.VMEM(shape, jnp.float32)


def launch(kernel, operands, outs, far_outs=(), scratch=(), copies=0, aliases=None):
    shapes = [*outs, *far_outs]
    nbytes = sum(4 * math.prod(shape) for shape in shapes)
    nbytes += sum(4 * math.prod(operand.shape) for operand in operands)
    return pl.pallas_call(
        kernel,
        in_specs=[pl.BlockSpec(memory_space=pltpu.HBM)] * len(operands),
        out_specs=[pl.BlockSpec(memory_space=pltpu.VMEM)] * len(outs)
        + [pl.BlockSpec(memory_space=pltpu.HBM)] * len(far_outs),
        out_shape=[jax.ShapeDtypeStruct(shape, jnp.float32) for shape in shapes],
        scratch_shapes=[*scratch, pltpu.SemaphoreType.DMA((copies,))],
        input_output_aliases=aliases or {},
        compiler_params=pltpu.CompilerParams(vmem_limit_bytes=24 * 2**20),
        cost_estimate=pl.CostEstimate(flops=0, bytes_accessed=nbytes, transcendentals=0),
    )(*operands)


def begin(sems, *pairs):
    started = []
    for index, (source, target) in enumerate(pairs):
        copy = pltpu.make_async_copy(source, target, sems.at[index])
        copy.start()
        started.append(copy)
    return started


def finish(*started):
    for copy in started:
        copy.wait()


def for_slabs(one, carry=0):
    def some(step, carry):
        for slab in range(UNROLL):
            carry = one(step * UNROLL + slab, carry)
        return carry

    return lax.fori_loop(0, SLABS // UNROLL, some, carry)


def lane_of(tile, slab):
    return jnp.sum(jnp.where(iota(tile.shape, 1) == slab, tile, 0.0), axis=1, keepdims=True)


def with_lane(tile, slab, column):
    return jnp.where(iota(tile.shape, 1) == slab, column, tile)


def place():
    return lax.axis_index("lon"), lax.axis_index("lat")


def open_row(lat):
    return pl.multiple_of(jnp.where(lat == TOP, 0, HALF), HALF)


def row_weight(mask, first, shape):
    row = iota(shape, 0)
    weight = jnp.zeros(shape, jnp.float32)
    for r in range(shape[0]):
        weight = jnp.where(row == r, mask[first + r].astype(jnp.float32), weight)
    return weight


def forward_kernel(
    field_in, coeff_in, table_in, mask_in, send, field, table, to_east, to_west, mask, sems
):
    lon, lat = place()
    first = open_row(lat)
    rows = pl.ds(first, HALF)
    field_copy, table_copy, *rest = begin(
        sems,
        (field_in, field),
        (table_in.at[lon], table),
        (coeff_in.at[:, 3, :, rows], to_east),
        (coeff_in.at[:, 4, :, rows], to_west),
        (mask_in, mask),
    )
    finish(field_copy, table_copy)
    waves = dot(table[:, :WIDTH], field[...].reshape(ROWS, WIDTH), 1, 1)
    send[:, :, :ROWS] = waves.reshape(LON_DEV, SHARE, ROWS)
    finish(*rest)
    filtered = row_weight(mask, first, (HALF, 1)) > 0.5
    east = west = jnp.zeros((HALF, 128), jnp.float32)
    for slab in range(SLABS):
        at = slab // LEV, slab % LEV
        value = field[*at, rows]
        coeff = to_east[at][:, WIDTH - 1 :]
        east = with_lane(east, slab, jnp.where(filtered, coeff, coeff * value[:, WIDTH - 1 :]))
        coeff = to_west[at][:, 0:1]
        west = with_lane(west, slab, jnp.where(filtered, coeff, coeff * value[:, 0:1]))
    for target in range(LON_DEV):
        send[target, :, ROWS:] = jnp.where(target == (lon + 1) % LON_DEV, east, west)[:, :64]


def across_kernel(coeff_in, across, tiles, pole, to_east, to_west, sems):
    lon, lat = place()
    top = lat == TOP
    closed = pl.ds(pl.multiple_of(HALF - open_row(lat), HALF), HALF)
    term = jnp.where(top, 1, 2)
    finish(
        *begin(
            sems,
            (coeff_in.at[:, term, :, closed], pole),
            (coeff_in.at[:, 3, :, closed], to_east),
            (coeff_in.at[:, 4, :, closed], to_west),
        )
    )
    east = west = jnp.zeros((HALF, 128), jnp.float32)
    for slab in range(SLABS):
        at = slab // LEV, slab % LEV
        sign = 1.0 if at[0] == FIELDS - 1 else -1.0
        lines = pole[at]
        across[slab : slab + 1] = sign * jnp.where(top, lines[HALF - 1 :], lines[0:1])
        east = with_lane(east, slab, to_east[at][:, WIDTH - 1 :])
        west = with_lane(west, slab, to_west[at][:, 0:1])
    tiles[0] = east
    tiles[1] = west


def respond_kernel(received_in, cutoff_in, tiles_in, send, edges, received, cutoff, tiles, sems):
    lon, _ = place()
    main, *rest = begin(
        sems, (received_in, received), (cutoff_in, cutoff), (tiles_in, tiles)
    )
    finish(*rest)
    shape = (SHARE, ROWS)
    wave = (lon * SHARE + iota(shape, 0)) % KMAX
    row = iota(shape, 1) % BAND
    limit = jnp.zeros(shape, jnp.int32)
    for r in range(BAND):
        limit = jnp.where(row == r, cutoff[r], limit)
    ratio = limit.astype(jnp.float32) / jnp.maximum(wave, 1).astype(jnp.float32)
    response = jnp.where(wave <= limit, 1.0, ratio * ratio)
    response = response * jnp.where(wave == 0, 1.0 / NLON, 2.0 / NLON)
    finish(main)
    total = received[0, :, :ROWS]
    for source in range(1, LON_DEV):
        total = total + received[source, :, :ROWS]
    total = total * response
    for target in range(LON_DEV):
        send[target, :, :ROWS] = total
        tile = jnp.where(target == (lon + 1) % LON_DEV, tiles[0], tiles[1])
        send[target, :, ROWS:] = tile[:, :64]
    blank = jnp.zeros((HALF, 64), jnp.float32)
    west = received[(lon + LON_DEV - 1) % LON_DEV, :, ROWS:]
    east = received[(lon + 1) % LON_DEV, :, ROWS:]
    edges[0] = jnp.concatenate([west, blank], axis=1)
    edges[1] = jnp.concatenate([east, blank], axis=1)


def gather_terms(value, coeff, south_line, north_line, west_edge, east_edge):
    to_north, to_south = coeff[1] * value, coeff[2] * value
    total = coeff[0] * value
    total = total + jnp.concatenate([south_line, to_north[:-1]], axis=0)
    total = total + jnp.concatenate([to_south[1:], north_line], axis=0)
    total = total + jnp.concatenate([west_edge, (coeff[3] * value)[:, :-1]], axis=1)
    total = total + jnp.concatenate([(coeff[4] * value)[:, 1:], east_edge], axis=1)
    return total, to_north, to_south


def load_coeff(coeff, field, level):
    return [coeff[field, term, level] for term in range(5)]


def one_row(waves, table, row, opposite):
    picked = (iota((ROWS, 128), 0) == iota((ROWS, 128), 1) * BAND + row).astype(jnp.float32)
    chosen = dot(waves, picked, 1, 0)
    if opposite:
        chosen = jnp.where(iota((WAVES, 128), 0) % 2 == 1, -chosen, chosen)
    return dot(chosen, table, 0, 0)


def whole_band(closed, opened, top):
    return jnp.where(
        top, jnp.concatenate([opened, closed], axis=0), jnp.concatenate([closed, opened], axis=0)
    )


def middle_kernel(
    waves_in, table_in, mask_in, state_in, extra_in, coeff_in, opened_in, beyond_in, across_in,
    send, to_next, next_line, edges, middle_out,
    waves, table, mask, state, extra, coeff_ref, opened, beyond, across, middle,
    filtered, opposite, sems,
):
    lon, lat = place()
    top = lat == TOP
    waves_copy, table_copy, *rest = begin(
        sems,
        (waves_in, waves),
        (table_in.at[lon], table),
        (mask_in, mask),
        (state_in, state),
        (extra_in, extra),
        (coeff_in, coeff_ref),
        (opened_in, opened),
        (beyond_in, beyond),
        (across_in, across),
    )
    finish(waves_copy, table_copy)
    flat = waves[:, :, :ROWS].reshape(WAVES, ROWS)
    filtered[...] = dot(flat, table[...], 0, 0)
    polar_row = jnp.where(top, BAND - 1, 0)
    opposite[...] = one_row(flat, table[...], polar_row, True)
    finish(*rest)
    blank = jnp.zeros((HALF, 64), jnp.float32)
    sides = (lon + LON_DEV - 1) % LON_DEV, (lon + 1) % LON_DEV
    for side in range(2):
        closed = jnp.concatenate([waves[sides[side], :, ROWS:], blank], axis=1)
        edges[side] = whole_band(closed, opened[side], top)
    weight = row_weight(mask, 0, (BAND, WIDTH))
    is_filtered = weight[:, 0:1] > 0.5
    next_weight = jnp.where(top, weight[0:1], weight[BAND - 1 :])
    row = iota((BAND, WIDTH), 0)

    def one(slab, carry):
        east_tile, west_tile = carry
        field, level = slab // LEV, slab % LEV
        here = pl.ds(slab, 1)
        value = state[field, level]
        smooth = filtered[pl.ds(slab * BAND, BAND)]
        value = value + weight * (smooth[:, :WIDTH] - value)
        coeff = load_coeff(coeff_ref, field, level)
        west = lane_of(edges[0], slab)
        west = jnp.where(is_filtered, west * smooth[:, WIDTH + 1 : WIDTH + 2], west)
        east = lane_of(edges[1], slab)
        east = jnp.where(is_filtered, east * smooth[:, WIDTH : WIDTH + 1], east)
        halo = beyond[2, here]
        total, north, south = gather_terms(
            value, coeff, jnp.where(top, halo, 0.0), jnp.where(top, 0.0, halo), west, east
        )
        pole = across[here] * opposite[here][:, :WIDTH]
        total = total + jnp.where(row == polar_row, pole, 0.0) + extra[field, level]
        middle[field, level] = total
        product = jnp.where(top, south[0:1], north[BAND - 1 :])
        near = jnp.where(top, total[0:1], total[BAND - 1 :])
        near_coeff = jnp.where(top, coeff[2][0:1], coeff[1][BAND - 1 :])
        to_next[0, here] = product
        to_next[1, here] = (1.0 - next_weight) * near_coeff * near
        to_next[2, here] = next_weight * near_coeff
        next_line[here] = beyond[1, here] * (beyond[0, here] + product)
        column = (coeff[3] * total)[:, WIDTH - 1 :]
        east_tile = with_lane(east_tile, slab, jnp.where(top, column[:HALF], column[HALF:]))
        column = (coeff[4] * total)[:, 0:1]
        west_tile = with_lane(west_tile, slab, jnp.where(top, column[:HALF], column[HALF:]))
        return east_tile, west_tile

    none = jnp.zeros((HALF, 128), jnp.float32)
    east_tile, west_tile = for_slabs(one, (none, none))
    (out_copy,) = begin(sems, (middle, middle_out))
    sums = dot(table[:, :WIDTH], middle[...].reshape(ROWS, WIDTH), 1, 1)
    send[:, :, :ROWS] = sums.reshape(LON_DEV, SHARE, ROWS)
    for target in range(LON_DEV):
        tile = jnp.where(target == (lon + 1) % LON_DEV, east_tile, west_tile)
        send[target, :, ROWS:] = tile[:, :64]
    finish(out_copy)


def final_kernel(
    waves_in, table_in, mask_in, middle_in, coeff_in, edges_in, opened_in, line_in, across_in,
    out,
    waves, table, mask, middle, coeff_ref, edges, opened, next_line, across,
    filtered, opposite, sems,
):
    lon, lat = place()
    top = lat == TOP
    waves_copy, table_copy, *rest = begin(
        sems,
        (waves_in, waves),
        (table_in.at[lon], table),
        (mask_in, mask),
        (middle_in, middle),
        (coeff_in, coeff_ref),
        (edges_in, edges),
        (opened_in, opened),
        (line_in, next_line),
        (across_in, across),
    )
    finish(waves_copy, table_copy)
    flat = waves[:, :, :ROWS].reshape(WAVES, ROWS)
    filtered[...] = dot(flat, table[...], 0, 0)
    polar_row = jnp.where(top, BAND - 1, 0)
    opposite[...] = one_row(flat, table[...], polar_row, True)
    finish(*rest)
    weight = row_weight(mask, 0, (BAND, WIDTH))
    is_filtered = weight[:, 0:1] > 0.5
    row = iota((BAND, WIDTH), 0)
    none = jnp.zeros((HALF, 128), jnp.float32)
    west_band = whole_band(none, opened[0], top)
    east_band = whole_band(none, opened[1], top)

    def one(slab, carry):
        field, level = slab // LEV, slab % LEV
        here = pl.ds(slab, 1)
        value = middle[field, level]
        smooth = filtered[pl.ds(slab * BAND, BAND)]
        value = value + weight * (smooth[:, :WIDTH] - value)
        coeff = load_coeff(coeff_ref, field, level)
        west = lane_of(edges[0], slab) * smooth[:, WIDTH + 1 : WIDTH + 2]
        west = jnp.where(is_filtered, west, lane_of(west_band, slab))
        east = lane_of(edges[1], slab) * smooth[:, WIDTH : WIDTH + 1]
        east = jnp.where(is_filtered, east, lane_of(east_band, slab))
        halo = next_line[here]
        total, _, _ = gather_terms(
            value, coeff, jnp.where(top, halo, 0.0), jnp.where(top, 0.0, halo), west, east
        )
        pole = across[here] * opposite[here][:, :WIDTH]
        out[field, level] = total + jnp.where(row == polar_row, pole, 0.0)
        return carry

    for_slabs(one)


def edge_kernel(field_in, coeff_in, edges, field, to_east, to_west, sems):
    finish(
        *begin(
            sems,
            (field_in, field),
            (coeff_in.at[:, 3], to_east),
            (coeff_in.at[:, 4], to_west),
        )
    )
    east = west = jnp.zeros((BAND, 128), jnp.float32)
    for slab in range(SLABS):
        at = slab // LEV, slab % LEV
        value = field[at]
        east = with_lane(east, slab, (to_east[at] * value)[:, WIDTH - 1 :])
        west = with_lane(west, slab, (to_west[at] * value)[:, 0:1])
    edges[0] = east
    edges[1] = west


def line_kernel(
    field_in, extra_in, coeff_in, west_in, east_in,
    to_north, to_south, to_polar,
    field_ref, extra, coeff_ref, west_edge, east_edge, sems,
):
    _, lat = place()
    finish(
        *begin(
            sems,
            (field_in, field_ref),
            (extra_in, extra),
            (coeff_in, coeff_ref),
            (west_in, west_edge),
            (east_in, east_edge),
        )
    )
    none = jnp.zeros((1, WIDTH), jnp.float32)

    def one(slab, carry):
        field, level = slab // LEV, slab % LEV
        here = pl.ds(slab, 1)
        coeff = load_coeff(coeff_ref, field, level)
        west, east = lane_of(west_edge[...], slab), lane_of(east_edge[...], slab)
        total, north, south = gather_terms(field_ref[field, level], coeff, none, none, west, east)
        total = total + extra[field, level]
        norths = total[BAND - 1 :], coeff[1][BAND - 1 :], north[BAND - 1 :]
        souths = total[0:1], coeff[2][0:1], south[0:1]
        for part in range(3):
            to_north[part, here] = norths[part]
            to_south[part, here] = souths[part]
            to_polar[part, here] = jnp.where(lat == 1, souths[part], norths[part])
        return carry

    for_slabs(one)


def plain_middle_kernel(
    state_in, extra_in, coeff_in, west_in, east_in, below_in, above_in, polar_in,
    edges, lines, middle_out,
    state, extra, coeff_ref, west_edge, east_edge, below, above, polar, middle, sems,
):
    _, lat = place()
    finish(
        *begin(
            sems,
            (state_in, state),
            (extra_in, extra),
            (coeff_in, coeff_ref),
            (west_in, west_edge),
            (east_in, east_edge),
            (below_in, below),
            (above_in, above),
            (polar_in, polar),
        )
    )

    def one(slab, carry):
        east_tile, west_tile = carry
        field, level = slab // LEV, slab % LEV
        here = pl.ds(slab, 1)
        coeff = load_coeff(coeff_ref, field, level)
        west, east = lane_of(west_edge[...], slab), lane_of(east_edge[...], slab)
        reached = polar[0, here]
        total, north, south = gather_terms(
            state[field, level],
            coeff,
            jnp.where(lat == 1, reached, below[2, here]),
            jnp.where(lat == TOP - 1, reached, above[2, here]),
            west,
            east,
        )
        total = total + extra[field, level]
        middle[field, level] = total
        low = below[1, here] * (below[0, here] + south[0:1])
        high = above[1, here] * (above[0, here] + north[BAND - 1 :])
        lines[0, here] = jnp.where(lat == 1, 0.0, low)
        lines[1, here] = jnp.where(lat == TOP - 1, 0.0, high)
        east_tile = with_lane(east_tile, slab, (coeff[3] * total)[:, WIDTH - 1 :])
        west_tile = with_lane(west_tile, slab, (coeff[4] * total)[:, 0:1])
        return east_tile, west_tile

    none = jnp.zeros((BAND, 128), jnp.float32)
    edges[0], edges[1] = for_slabs(one, (none, none))
    finish(*begin(sems, (middle, middle_out)))


def plain_final_kernel(
    middle_in, coeff_in, west_in, east_in, lines_in,
    out,
    middle, coeff_ref, west_edge, east_edge, lines, sems,
):
    finish(
        *begin(
            sems,
            (middle_in, middle),
            (coeff_in, coeff_ref),
            (west_in, west_edge),
            (east_in, east_edge),
            (lines_in, lines),
        )
    )

    def one(slab, carry):
        field, level = slab // LEV, slab % LEV
        here = pl.ds(slab, 1)
        coeff = load_coeff(coeff_ref, field, level)
        west, east = lane_of(west_edge[...], slab), lane_of(east_edge[...], slab)
        value = middle[field, level]
        out[field, level] = gather_terms(value, coeff, lines[0, here], lines[1, here], west, east)[0]
        return carry

    for_slabs(one)


def reach_kernel(result_in, waves_in, table_in, polar_in, result_out, part, waves, table, polar, sems):
    lon, lat = place()
    next_to = (lat == 1) | (lat == TOP - 1)
    bottom = lat == 1
    rows = pl.ds(pl.multiple_of(jnp.where(bottom, 0, HALF), HALF), HALF)

    @pl.when(next_to)
    def _():
        finish(
            *begin(
                sems,
                (result_in.at[:, :, rows], part),
                (waves_in, waves),
                (table_in.at[lon], table),
                (polar_in, polar),
            )
        )
        flat = waves[:, :, :ROWS].reshape(WAVES, ROWS)
        smooth = one_row(flat, table[...], jnp.where(bottom, BAND - 1, 0), False)
        line = polar[1] + polar[2] * smooth[:SLABS, :WIDTH]
        row = iota((HALF, WIDTH), 0)
        mine = row == jnp.where(bottom, 0, HALF - 1)
        for slab in range(SLABS):
            at = slab // LEV, slab % LEV
            part[at] = part[at] + jnp.where(mine, line[slab : slab + 1], 0.0)
        finish(*begin(sems, (part, result_out.at[:, :, rows])))


def exchanged(chunks):
    return lax.all_to_all(chunks, "lon", split_axis=0, concat_axis=0, tiled=True)


def moved(value, lats, north, east):
    pairs = []
    for lat, lon in [(lat, lon) for lat in lats for lon in range(LON_DEV)]:
        pairs.append((lat * LON_DEV + lon, (lat + north) * LON_DEV + (lon + east) % LON_DEV))
    return lax.ppermute(value, ("lat", "lon"), pairs)


def next_to_pole(value, outward):
    pairs = []
    for lon in range(LON_DEV):
        for polar, other in ((0, 1), (TOP, TOP - 1)):
            pair = polar * LON_DEV + lon, other * LON_DEV + lon
            pairs.append(pair if outward else pair[::-1])
    return lax.ppermute(value, ("lat", "lon"), pairs)


def local(adjoint_state, innovation, coefficients, polar_mask, wave_cutoff):
    lat = lax.axis_index("lat")
    polar = (lat == 0) | (lat == TOP)
    table = jnp.asarray(wave_tables())
    small = pltpu.SMEM((BAND,), jnp.int32)
    plain = range(1, TOP)
    table_scratch = in_vmem((WAVES, WIDE))
    wave_scratch = [in_vmem((ROWS, WIDE)), in_vmem((128, WIDE))]
    one_edge = (BAND, 128)

    def blanks(*shapes):
        return tuple(jnp.zeros(shape, jnp.float32) for shape in shapes)

    def polar_first():
        half = in_vmem(HALF_FIELD)
        send, to_polar, to_north, to_south, edge = launch(
            forward_kernel_with_blanks,
            [adjoint_state, coefficients, table, polar_mask],
            [CHUNKS],
            [LINES, LINES, LINES, (2, *one_edge)],
            [in_vmem(FIELD), table_scratch, half, half, small],
            copies=5,
        )
        received = exchanged(send)
        cross, tiles = launch(
            across_kernel, [coefficients], [LINE, TILES], (), [half, half, half], copies=3
        )
        across = moved(cross, (0, TOP), 0, LON_DEV // 2)
        return received, across, tiles, to_polar, to_north, to_south, edge

    def plain_first():
        (edges,) = launch(
            edge_kernel,
            [adjoint_state, coefficients],
            [(2, *one_edge)],
            (),
            [in_vmem(FIELD)] * 3,
            copies=3,
        )
        west = moved(edges[0], plain, 0, 1)
        east = moved(edges[1], plain, 0, -1)
        to_north, to_south, to_polar = launch(
            line_kernel,
            [adjoint_state, innovation, coefficients, west, east],
            [LINES, LINES, LINES],
            (),
            [in_vmem(FIELD), in_vmem(FIELD), in_vmem(COEFF), in_vmem(one_edge), in_vmem(one_edge)],
            copies=5,
        )
        received, across, tiles = blanks(CHUNKS, LINE, TILES)
        return received, across, tiles, to_polar, to_north, to_south, jnp.stack([west, east])

    received, across, tiles, to_polar, to_north, to_south, edge = lax.cond(
        polar, polar_first, plain_first
    )
    beyond = next_to_pole(to_polar, False)

    def respond(received):
        return launch(
            respond_kernel,
            [received, wave_cutoff, tiles],
            [CHUNKS, TILES],
            (),
            [in_vmem(CHUNKS), small, in_vmem(TILES)],
            copies=3,
        )

    def polar_second():
        send, opened = respond(received)
        return exchanged(send), opened, to_north, to_south

    def plain_second():
        below = moved(to_north, range(1, TOP - 1), 1, 0)
        above = moved(to_south, range(2, TOP), -1, 0)
        return *blanks(CHUNKS, TILES), below, above

    waves, opened, below, above = lax.cond(polar, polar_second, plain_second)

    def polar_third():
        return tuple(launch(
            middle_kernel,
            [waves, table, polar_mask, adjoint_state, innovation, coefficients, opened, beyond, across],
            [CHUNKS, LINES, LINE, EDGES],
            [FIELD],
            [in_vmem(CHUNKS), table_scratch, small, in_vmem(FIELD), in_vmem(FIELD), in_vmem(COEFF)]
            + [in_vmem(TILES), in_vmem(LINES), in_vmem(LINE), in_vmem(FIELD), *wave_scratch],
            copies=9,
        ))

    def plain_third():
        return blanks(CHUNKS, LINES, LINE, EDGES, FIELD)

    send, to_next, next_line, edges, middle = lax.cond(polar, polar_third, plain_third)
    reached = next_to_pole(to_next, True)

    def polar_fourth():
        received = exchanged(send)
        again, opened = respond(received)
        return exchanged(again), opened, middle

    def plain_fourth():
        west, east = edge[0], edge[1]
        second, lines, middle = launch(
            plain_middle_kernel,
            [adjoint_state, innovation, coefficients, west, east, below, above, reached],
            [(2, *one_edge), (2, *LINE)],
            [FIELD],
            [in_vmem(FIELD), in_vmem(FIELD), in_vmem(COEFF), in_vmem(one_edge), in_vmem(one_edge)]
            + [in_vmem(LINES), in_vmem(LINES), in_vmem(LINES), in_vmem(FIELD)],
            copies=8,
        )
        west = moved(second[0], plain, 0, 1)
        east = moved(second[1], plain, 0, -1)
        (result,) = launch(
            plain_final_kernel,
            [middle, coefficients, west, east, lines],
            [FIELD],
            (),
            [in_vmem(FIELD), in_vmem(COEFF), in_vmem(one_edge), in_vmem(one_edge), in_vmem((2, *LINE))],
            copies=5,
        )
        return *blanks(CHUNKS, TILES), result

    waves, opened, result = lax.cond(polar, polar_fourth, plain_fourth)
    waves_beyond = next_to_pole(waves, True)

    def polar_fifth():
        (out,) = launch(
            final_kernel,
            [waves, table, polar_mask, result, coefficients, edges, opened, next_line, across],
            [FIELD],
            (),
            [in_vmem(CHUNKS), table_scratch, small, in_vmem(FIELD), in_vmem(COEFF), in_vmem(EDGES)]
            + [in_vmem(TILES), in_vmem(LINE), in_vmem(LINE), *wave_scratch],
            copies=9,
        )
        return out

    def plain_fifth():
        (out,) = launch(
            reach_kernel,
            [result, waves_beyond, table, reached],
            (),
            [FIELD],
            [in_vmem(HALF_FIELD), in_vmem(CHUNKS), table_scratch, in_vmem(LINES)],
            copies=4,
            aliases={0: 0},
        )
        return out

    return lax.cond(polar, polar_fifth, plain_fifth)


def forward_kernel_with_blanks(*refs):
    forward_kernel(*refs[:5], *refs[9:])


def solution(mesh):
    return jax.shard_map(
        local,
        mesh=mesh,
        in_specs=(
            P(None, None, "lat", "lon"),
            P(None, None, "lat", "lon"),
            P(None, None, None, "lat", "lon"),
            P("lat"),
            P("lat"),
        ),
        out_specs=P(None, None, "lat", "lon"),
        check_vma=False,
    )
```

```python
import math

import jax
import jax.numpy as jnp
import numpy as np
from jax import lax
from jax.experimental import pallas as pl
from jax.experimental.pallas import tpu as pltpu
from jax.sharding import PartitionSpec as P

NLON = 5760
KMAX = 64
WAVES = 2 * KMAX
FIELDS = 3
LEV = 12
BAND = 16
HALF = BAND // 2
LON_DEV = 16
LAT_DEV = 16
TOP = LAT_DEV - 1
WIDTH = NLON // LON_DEV
WIDE = 384
SLABS = FIELDS * LEV
ROWS = SLABS * BAND
SHARE = WAVES // LON_DEV
UNROLL = 4

FIELD = (FIELDS, LEV, BAND, WIDTH)
HALF_FIELD = (FIELDS, LEV, HALF, WIDTH)
COEFF = (FIELDS, 5, LEV, BAND, WIDTH)
CHUNKS = (LON_DEV, SHARE, ROWS + 64)
LINE = (SLABS, WIDTH)
LINES = (3, SLABS, WIDTH)
TILES = (2, HALF, 128)
EDGES = (2, BAND, 128)


def wave_tables():
    columns = np.concatenate([np.arange(WIDTH), [WIDTH, -1]])
    phases = (np.arange(LON_DEV)[:, None] * WIDTH + columns[None, :]) % NLON
    phases = phases[:, None, :] * np.arange(KMAX)[None, :, None] % NLON
    radians = phases * (2.0 * math.pi / NLON)
    both = np.concatenate([np.cos(radians), np.sin(radians)], axis=1)
    return np.pad(both, ((0, 0), (0, 0), (0, WIDE - WIDTH - 2))).astype(np.float32)


def split(value):
    high = value.astype(jnp.bfloat16)
    return high, (value - high.astype(jnp.float32)).astype(jnp.bfloat16)


def pair_dot(left, right, left_dim, right_dim):
    return lax.dot_general(
        left, right, (((left_dim,), (right_dim,)), ((), ())), preferred_element_type=jnp.float32
    )


def dot(left, right, left_dim, right_dim):
    (left_high, left_low), (right_high, right_low) = split(left), split(right)
    total = pair_dot(left_high, right_low, left_dim, right_dim)
    total = total + pair_dot(left_low, right_high, left_dim, right_dim)
    return total + pair_dot(left_high, right_high, left_dim, right_dim)


def iota(shape, dim):
    return lax.broadcasted_iota(jnp.int32, shape, dim)


def in_vmem(shape):
    return pltpu.VMEM(shape, jnp.float32)


def launch(kernel, operands, outs, far_outs=(), scratch=(), copies=0, aliases=None):
    shapes = [*outs, *far_outs]
    nbytes = sum(4 * math.prod(shape) for shape in shapes)
    nbytes += sum(4 * math.prod(operand.shape) for operand in operands)
    return pl.pallas_call(
        kernel,
        in_specs=[pl.BlockSpec(memory_space=pltpu.HBM)] * len(operands),
        out_specs=[pl.BlockSpec(memory_space=pltpu.VMEM)] * len(outs)
        + [pl.BlockSpec(memory_space=pltpu.HBM)] * len(far_outs),
        out_shape=[jax.ShapeDtypeStruct(shape, jnp.float32) for shape in shapes],
        scratch_shapes=[*scratch, pltpu.SemaphoreType.DMA((copies,))],
        input_output_aliases=aliases or {},
        compiler_params=pltpu.CompilerParams(vmem_limit_bytes=24 * 2**20),
        cost_estimate=pl.CostEstimate(flops=0, bytes_accessed=nbytes, transcendentals=0),
    )(*operands)


def begin(sems, *pairs):
    started = []
    for index, (source, target) in enumerate(pairs):
        copy = pltpu.make_async_copy(source, target, sems.at[index])
        copy.start()
        started.append(copy)
    return started


def by_field(*pairs):
    return [(source.at[field], target.at[field]) for field in range(FIELDS) for source, target in pairs]


def finish(*started):
    for copy in started:
        copy.wait()


def for_levels(field, one, carry=0):
    def some(step, carry):
        for level in range(UNROLL):
            carry = one(field, step * UNROLL + level, carry)
        return carry

    return lax.fori_loop(0, LEV // UNROLL, some, carry)


def for_slabs(one, carry=0):
    for field in range(FIELDS):
        carry = for_levels(field, one, carry)
    return carry


def lane_of(tile, slab):
    return jnp.sum(jnp.where(iota(tile.shape, 1) == slab, tile, 0.0), axis=1, keepdims=True)


def with_lane(tile, slab, column):
    return jnp.where(iota(tile.shape, 1) == slab, column, tile)


def place():
    return lax.axis_index("lon"), lax.axis_index("lat")


def open_row(lat):
    return pl.multiple_of(jnp.where(lat == TOP, 0, HALF), HALF)


def row_weight(mask, first, shape):
    row = iota(shape, 0)
    weight = jnp.zeros(shape, jnp.float32)
    for r in range(shape[0]):
        weight = jnp.where(row == r, mask[first + r].astype(jnp.float32), weight)
    return weight


def forward_kernel(
    field_in, coeff_in, table_in, mask_in, send, field, table, to_east, to_west, mask, sems
):
    lon, lat = place()
    first = open_row(lat)
    rows = pl.ds(first, HALF)
    field_copy, table_copy, *rest = begin(
        sems,
        (field_in, field),
        (table_in.at[lon], table),
        (coeff_in.at[:, 3, :, rows], to_east),
        (coeff_in.at[:, 4, :, rows], to_west),
        (mask_in, mask),
    )
    finish(field_copy, table_copy)
    waves = dot(table[:, :WIDTH], field[...].reshape(ROWS, WIDTH), 1, 1)
    send[:, :, :ROWS] = waves.reshape(LON_DEV, SHARE, ROWS)
    finish(*rest)
    filtered = row_weight(mask, first, (HALF, 1)) > 0.5
    east = west = jnp.zeros((HALF, 128), jnp.float32)
    for slab in range(SLABS):
        at = slab // LEV, slab % LEV
        value = field[*at, rows]
        coeff = to_east[at][:, WIDTH - 1 :]
        east = with_lane(east, slab, jnp.where(filtered, coeff, coeff * value[:, WIDTH - 1 :]))
        coeff = to_west[at][:, 0:1]
        west = with_lane(west, slab, jnp.where(filtered, coeff, coeff * value[:, 0:1]))
    for target in range(LON_DEV):
        send[target, :, ROWS:] = jnp.where(target == (lon + 1) % LON_DEV, east, west)[:, :64]


def across_kernel(coeff_in, across, tiles, pole, to_east, to_west, sems):
    lon, lat = place()
    top = lat == TOP
    closed = pl.ds(pl.multiple_of(HALF - open_row(lat), HALF), HALF)
    term = jnp.where(top, 1, 2)
    finish(
        *begin(
            sems,
            (coeff_in.at[:, term, :, closed], pole),
            (coeff_in.at[:, 3, :, closed], to_east),
            (coeff_in.at[:, 4, :, closed], to_west),
        )
    )
    east = west = jnp.zeros((HALF, 128), jnp.float32)
    for slab in range(SLABS):
        at = slab // LEV, slab % LEV
        sign = 1.0 if at[0] == FIELDS - 1 else -1.0
        lines = pole[at]
        across[slab : slab + 1] = sign * jnp.where(top, lines[HALF - 1 :], lines[0:1])
        east = with_lane(east, slab, to_east[at][:, WIDTH - 1 :])
        west = with_lane(west, slab, to_west[at][:, 0:1])
    tiles[0] = east
    tiles[1] = west


def respond_kernel(received_in, cutoff_in, tiles_in, send, edges, received, cutoff, tiles, sems):
    lon, _ = place()
    main, *rest = begin(
        sems, (received_in, received), (cutoff_in, cutoff), (tiles_in, tiles)
    )
    finish(*rest)
    shape = (SHARE, ROWS)
    wave = (lon * SHARE + iota(shape, 0)) % KMAX
    row = iota(shape, 1) % BAND
    limit = jnp.zeros(shape, jnp.int32)
    for r in range(BAND):
        limit = jnp.where(row == r, cutoff[r], limit)
    ratio = limit.astype(jnp.float32) / jnp.maximum(wave, 1).astype(jnp.float32)
    response = jnp.where(wave <= limit, 1.0, ratio * ratio)
    response = response * jnp.where(wave == 0, 1.0 / NLON, 2.0 / NLON)
    finish(main)
    total = received[0, :, :ROWS]
    for source in range(1, LON_DEV):
        total = total + received[source, :, :ROWS]
    total = total * response
    for target in range(LON_DEV):
        send[target, :, :ROWS] = total
        tile = jnp.where(target == (lon + 1) % LON_DEV, tiles[0], tiles[1])
        send[target, :, ROWS:] = tile[:, :64]
    blank = jnp.zeros((HALF, 64), jnp.float32)
    west = received[(lon + LON_DEV - 1) % LON_DEV, :, ROWS:]
    east = received[(lon + 1) % LON_DEV, :, ROWS:]
    edges[0] = jnp.concatenate([west, blank], axis=1)
    edges[1] = jnp.concatenate([east, blank], axis=1)


def gather_terms(value, coeff, south_line, north_line, west_edge, east_edge):
    to_north, to_south = coeff[1] * value, coeff[2] * value
    total = coeff[0] * value
    total = total + jnp.concatenate([south_line, to_north[:-1]], axis=0)
    total = total + jnp.concatenate([to_south[1:], north_line], axis=0)
    total = total + jnp.concatenate([west_edge, (coeff[3] * value)[:, :-1]], axis=1)
    total = total + jnp.concatenate([(coeff[4] * value)[:, 1:], east_edge], axis=1)
    return total, to_north, to_south


def load_coeff(coeff, field, level):
    return [coeff[field, term, level] for term in range(5)]


def one_row(waves, table, row, opposite):
    picked = iota((ROWS, 128), 0) == iota((ROWS, 128), 1) * BAND + row
    picked = picked.astype(jnp.float32).astype(jnp.bfloat16)
    high, low = split(waves)
    chosen = pair_dot(high, picked, 1, 0) + pair_dot(low, picked, 1, 0)
    if opposite:
        chosen = jnp.where(iota((WAVES, 128), 0) % 2 == 1, -chosen, chosen)
    return dot(chosen, table, 0, 0)


def whole_band(closed, opened, top):
    return jnp.where(
        top, jnp.concatenate([opened, closed], axis=0), jnp.concatenate([closed, opened], axis=0)
    )


def middle_kernel(
    waves_in, table_in, mask_in, state_in, extra_in, coeff_in, opened_in, beyond_in, across_in,
    send, to_next, next_line, edges, middle_out,
    waves, table, mask, state, extra, coeff_ref, opened, beyond, across, middle,
    filtered, opposite, sems,
):
    lon, lat = place()
    top = lat == TOP
    waves_copy, table_copy, *rest = begin(
        sems,
        (waves_in, waves),
        (table_in.at[lon], table),
        (mask_in, mask),
        (opened_in, opened),
        (beyond_in, beyond),
        (across_in, across),
        *by_field((state_in, state), (extra_in, extra), (coeff_in, coeff_ref)),
    )
    rest, fields = rest[:4], rest[4:]
    finish(waves_copy, table_copy)
    flat = waves[:, :, :ROWS].reshape(WAVES, ROWS)
    filtered[...] = dot(flat, table[...], 0, 0)
    polar_row = jnp.where(top, BAND - 1, 0)
    opposite[...] = one_row(flat, table[...], polar_row, True)
    finish(*rest)
    blank = jnp.zeros((HALF, 64), jnp.float32)
    sides = (lon + LON_DEV - 1) % LON_DEV, (lon + 1) % LON_DEV
    for side in range(2):
        closed = jnp.concatenate([waves[sides[side], :, ROWS:], blank], axis=1)
        edges[side] = whole_band(closed, opened[side], top)
    weight = row_weight(mask, 0, (BAND, WIDTH))
    is_filtered = weight[:, 0:1] > 0.5
    next_weight = jnp.where(top, weight[0:1], weight[BAND - 1 :])
    row = iota((BAND, WIDTH), 0)

    def one(field, level, carry):
        east_tile, west_tile = carry
        slab = field * LEV + level
        here = pl.ds(slab, 1)
        value = state[field, level]
        smooth = filtered[pl.ds(slab * BAND, BAND)]
        value = value + weight * (smooth[:, :WIDTH] - value)
        coeff = load_coeff(coeff_ref, field, level)
        west = lane_of(edges[0], slab)
        west = jnp.where(is_filtered, west * smooth[:, WIDTH + 1 : WIDTH + 2], west)
        east = lane_of(edges[1], slab)
        east = jnp.where(is_filtered, east * smooth[:, WIDTH : WIDTH + 1], east)
        halo = beyond[2, here]
        total, north, south = gather_terms(
            value, coeff, jnp.where(top, halo, 0.0), jnp.where(top, 0.0, halo), west, east
        )
        pole = across[here] * opposite[here][:, :WIDTH]
        total = total + jnp.where(row == polar_row, pole, 0.0) + extra[field, level]
        middle[field, level] = total
        product = jnp.where(top, south[0:1], north[BAND - 1 :])
        near = jnp.where(top, total[0:1], total[BAND - 1 :])
        near_coeff = jnp.where(top, coeff[2][0:1], coeff[1][BAND - 1 :])
        to_next[0, here] = product
        to_next[1, here] = (1.0 - next_weight) * near_coeff * near
        to_next[2, here] = next_weight * near_coeff
        next_line[here] = beyond[1, here] * (beyond[0, here] + product)
        column = (coeff[3] * total)[:, WIDTH - 1 :]
        east_tile = with_lane(east_tile, slab, jnp.where(top, column[:HALF], column[HALF:]))
        column = (coeff[4] * total)[:, 0:1]
        west_tile = with_lane(west_tile, slab, jnp.where(top, column[:HALF], column[HALF:]))
        return east_tile, west_tile

    none = jnp.zeros((HALF, 128), jnp.float32)
    carry, stored = (none, none), []
    for field in range(FIELDS):
        finish(*fields[3 * field : 3 * field + 3])
        carry = for_levels(field, one, carry)
        stored += begin(sems.at[field : field + 1], (middle.at[field], middle_out.at[field]))
    east_tile, west_tile = carry
    sums = dot(table[:, :WIDTH], middle[...].reshape(ROWS, WIDTH), 1, 1)
    send[:, :, :ROWS] = sums.reshape(LON_DEV, SHARE, ROWS)
    for target in range(LON_DEV):
        tile = jnp.where(target == (lon + 1) % LON_DEV, east_tile, west_tile)
        send[target, :, ROWS:] = tile[:, :64]
    finish(*stored)


def final_kernel(
    waves_in, table_in, mask_in, middle_in, coeff_in, edges_in, opened_in, line_in, across_in,
    out,
    waves, table, mask, middle, coeff_ref, edges, opened, next_line, across, result,
    filtered, opposite, sems,
):
    lon, lat = place()
    top = lat == TOP
    waves_copy, table_copy, *rest = begin(
        sems,
        (waves_in, waves),
        (table_in.at[lon], table),
        (mask_in, mask),
        (edges_in, edges),
        (opened_in, opened),
        (line_in, next_line),
        (across_in, across),
        *by_field((middle_in, middle), (coeff_in, coeff_ref)),
    )
    rest, fields = rest[:5], rest[5:]
    finish(waves_copy, table_copy)
    flat = waves[:, :, :ROWS].reshape(WAVES, ROWS)
    filtered[...] = dot(flat, table[...], 0, 0)
    polar_row = jnp.where(top, BAND - 1, 0)
    opposite[...] = one_row(flat, table[...], polar_row, True)
    finish(*rest)
    weight = row_weight(mask, 0, (BAND, WIDTH))
    is_filtered = weight[:, 0:1] > 0.5
    row = iota((BAND, WIDTH), 0)
    none = jnp.zeros((HALF, 128), jnp.float32)
    west_band = whole_band(none, opened[0], top)
    east_band = whole_band(none, opened[1], top)

    def one(field, level, carry):
        slab = field * LEV + level
        here = pl.ds(slab, 1)
        value = middle[field, level]
        smooth = filtered[pl.ds(slab * BAND, BAND)]
        value = value + weight * (smooth[:, :WIDTH] - value)
        coeff = load_coeff(coeff_ref, field, level)
        west = lane_of(edges[0], slab) * smooth[:, WIDTH + 1 : WIDTH + 2]
        west = jnp.where(is_filtered, west, lane_of(west_band, slab))
        east = lane_of(edges[1], slab) * smooth[:, WIDTH : WIDTH + 1]
        east = jnp.where(is_filtered, east, lane_of(east_band, slab))
        halo = next_line[here]
        total, _, _ = gather_terms(
            value, coeff, jnp.where(top, halo, 0.0), jnp.where(top, 0.0, halo), west, east
        )
        pole = across[here] * opposite[here][:, :WIDTH]
        result[field, level] = total + jnp.where(row == polar_row, pole, 0.0)
        return carry

    stored = []
    for field in range(FIELDS):
        finish(*fields[2 * field : 2 * field + 2])
        for_levels(field, one)
        stored += begin(sems.at[field : field + 1], (result.at[field], out.at[field]))
    finish(*stored)


def edge_kernel(field_in, coeff_in, edges, field, to_east, to_west, sems):
    finish(
        *begin(
            sems,
            (field_in, field),
            (coeff_in.at[:, 3], to_east),
            (coeff_in.at[:, 4], to_west),
        )
    )
    east = west = jnp.zeros((BAND, 128), jnp.float32)
    for slab in range(SLABS):
        at = slab // LEV, slab % LEV
        value = field[at]
        east = with_lane(east, slab, (to_east[at] * value)[:, WIDTH - 1 :])
        west = with_lane(west, slab, (to_west[at] * value)[:, 0:1])
    edges[0] = east
    edges[1] = west


def line_kernel(
    field_in, extra_in, coeff_in, west_in, east_in,
    to_north, to_south, to_polar,
    field_ref, extra, coeff_ref, west_edge, east_edge, sems,
):
    _, lat = place()
    finish(
        *begin(
            sems,
            (field_in, field_ref),
            (extra_in, extra),
            (coeff_in, coeff_ref),
            (west_in, west_edge),
            (east_in, east_edge),
        )
    )
    none = jnp.zeros((1, WIDTH), jnp.float32)

    def one(field, level, carry):
        slab = field * LEV + level
        here = pl.ds(slab, 1)
        coeff = load_coeff(coeff_ref, field, level)
        west, east = lane_of(west_edge[...], slab), lane_of(east_edge[...], slab)
        total, north, south = gather_terms(field_ref[field, level], coeff, none, none, west, east)
        total = total + extra[field, level]
        norths = total[BAND - 1 :], coeff[1][BAND - 1 :], north[BAND - 1 :]
        souths = total[0:1], coeff[2][0:1], south[0:1]
        for part in range(3):
            to_north[part, here] = norths[part]
            to_south[part, here] = souths[part]
            to_polar[part, here] = jnp.where(lat == 1, souths[part], norths[part])
        return carry

    for_slabs(one)


def plain_middle_kernel(
    state_in, extra_in, coeff_in, west_in, east_in, below_in, above_in, polar_in,
    edges, lines, middle_out,
    state, extra, coeff_ref, west_edge, east_edge, below, above, polar, middle, sems,
):
    _, lat = place()
    finish(
        *begin(
            sems,
            (state_in, state),
            (extra_in, extra),
            (coeff_in, coeff_ref),
            (west_in, west_edge),
            (east_in, east_edge),
            (below_in, below),
            (above_in, above),
            (polar_in, polar),
        )
    )

    def one(field, level, carry):
        east_tile, west_tile = carry
        slab = field * LEV + level
        here = pl.ds(slab, 1)
        coeff = load_coeff(coeff_ref, field, level)
        west, east = lane_of(west_edge[...], slab), lane_of(east_edge[...], slab)
        reached = polar[0, here]
        total, north, south = gather_terms(
            state[field, level],
            coeff,
            jnp.where(lat == 1, reached, below[2, here]),
            jnp.where(lat == TOP - 1, reached, above[2, here]),
            west,
            east,
        )
        total = total + extra[field, level]
        middle[field, level] = total
        low = below[1, here] * (below[0, here] + south[0:1])
        high = above[1, here] * (above[0, here] + north[BAND - 1 :])
        lines[0, here] = jnp.where(lat == 1, 0.0, low)
        lines[1, here] = jnp.where(lat == TOP - 1, 0.0, high)
        east_tile = with_lane(east_tile, slab, (coeff[3] * total)[:, WIDTH - 1 :])
        west_tile = with_lane(west_tile, slab, (coeff[4] * total)[:, 0:1])
        return east_tile, west_tile

    none = jnp.zeros((BAND, 128), jnp.float32)
    edges[0], edges[1] = for_slabs(one, (none, none))
    finish(*begin(sems, (middle, middle_out)))


def plain_final_kernel(
    middle_in, coeff_in, west_in, east_in, lines_in,
    out,
    middle, coeff_ref, west_edge, east_edge, lines, sems,
):
    finish(
        *begin(
            sems,
            (middle_in, middle),
            (coeff_in, coeff_ref),
            (west_in, west_edge),
            (east_in, east_edge),
            (lines_in, lines),
        )
    )

    def one(field, level, carry):
        slab = field * LEV + level
        here = pl.ds(slab, 1)
        coeff = load_coeff(coeff_ref, field, level)
        west, east = lane_of(west_edge[...], slab), lane_of(east_edge[...], slab)
        value = middle[field, level]
        out[field, level] = gather_terms(value, coeff, lines[0, here], lines[1, here], west, east)[0]
        return carry

    for_slabs(one)


def reach_kernel(result_in, waves_in, table_in, polar_in, result_out, part, waves, table, polar, sems):
    lon, lat = place()
    next_to = (lat == 1) | (lat == TOP - 1)
    bottom = lat == 1
    rows = pl.ds(pl.multiple_of(jnp.where(bottom, 0, HALF), HALF), HALF)

    @pl.when(next_to)
    def _():
        finish(
            *begin(
                sems,
                (result_in.at[:, :, rows], part),
                (waves_in, waves),
                (table_in.at[lon], table),
                (polar_in, polar),
            )
        )
        flat = waves[:, :, :ROWS].reshape(WAVES, ROWS)
        smooth = one_row(flat, table[...], jnp.where(bottom, BAND - 1, 0), False)
        line = polar[1] + polar[2] * smooth[:SLABS, :WIDTH]
        row = iota((HALF, WIDTH), 0)
        mine = row == jnp.where(bottom, 0, HALF - 1)
        for slab in range(SLABS):
            at = slab // LEV, slab % LEV
            part[at] = part[at] + jnp.where(mine, line[slab : slab + 1], 0.0)
        finish(*begin(sems, (part, result_out.at[:, :, rows])))


def exchanged(chunks):
    return lax.all_to_all(chunks, "lon", split_axis=0, concat_axis=0, tiled=True)


def moved(value, lats, north, east):
    pairs = []
    for lat, lon in [(lat, lon) for lat in lats for lon in range(LON_DEV)]:
        pairs.append((lat * LON_DEV + lon, (lat + north) * LON_DEV + (lon + east) % LON_DEV))
    return lax.ppermute(value, ("lat", "lon"), pairs)


def next_to_pole(value, outward):
    pairs = []
    for lon in range(LON_DEV):
        for polar, other in ((0, 1), (TOP, TOP - 1)):
            pair = polar * LON_DEV + lon, other * LON_DEV + lon
            pairs.append(pair if outward else pair[::-1])
    return lax.ppermute(value, ("lat", "lon"), pairs)


def local(adjoint_state, innovation, coefficients, polar_mask, wave_cutoff):
    lat = lax.axis_index("lat")
    polar = (lat == 0) | (lat == TOP)
    table = jnp.asarray(wave_tables())
    small = pltpu.SMEM((BAND,), jnp.int32)
    plain = range(1, TOP)
    table_scratch = in_vmem((WAVES, WIDE))
    wave_scratch = [in_vmem((ROWS, WIDE)), in_vmem((128, WIDE))]
    one_edge = (BAND, 128)

    def blanks(*shapes):
        return tuple(jnp.zeros(shape, jnp.float32) for shape in shapes)

    def respond(received, tiles):
        return launch(
            respond_kernel,
            [received, wave_cutoff, tiles],
            [CHUNKS, TILES],
            (),
            [in_vmem(CHUNKS), small, in_vmem(TILES)],
            copies=3,
        )

    def polar_first():
        half = in_vmem(HALF_FIELD)
        send, to_polar, to_north, to_south, edge = launch(
            forward_kernel_with_blanks,
            [adjoint_state, coefficients, table, polar_mask],
            [CHUNKS],
            [LINES, LINES, LINES, (2, *one_edge)],
            [in_vmem(FIELD), table_scratch, half, half, small],
            copies=5,
        )
        received = exchanged(send)
        cross, tiles = launch(
            across_kernel, [coefficients], [LINE, TILES], (), [half, half, half], copies=3
        )
        send, opened = respond(received, tiles)
        return send, opened, cross, tiles, to_polar, to_north, to_south, edge

    def plain_first():
        (edges,) = launch(
            edge_kernel,
            [adjoint_state, coefficients],
            [(2, *one_edge)],
            (),
            [in_vmem(FIELD)] * 3,
            copies=3,
        )
        west = moved(edges[0], plain, 0, 1)
        east = moved(edges[1], plain, 0, -1)
        to_north, to_south, to_polar = launch(
            line_kernel,
            [adjoint_state, innovation, coefficients, west, east],
            [LINES, LINES, LINES],
            (),
            [in_vmem(FIELD), in_vmem(FIELD), in_vmem(COEFF), in_vmem(one_edge), in_vmem(one_edge)],
            copies=5,
        )
        send, opened, cross, tiles = blanks(CHUNKS, TILES, LINE, TILES)
        edge = jnp.stack([west, east])
        return send, opened, cross, tiles, to_polar, to_north, to_south, edge

    send, opened, cross, tiles, to_polar, to_north, to_south, edge = lax.cond(
        polar, polar_first, plain_first
    )
    beyond = next_to_pole(to_polar, False)

    def polar_second():
        waves = exchanged(send)
        across = moved(cross, (0, TOP), 0, LON_DEV // 2)
        return waves, across, to_north, to_south

    def plain_second():
        below = moved(to_north, range(1, TOP - 1), 1, 0)
        above = moved(to_south, range(2, TOP), -1, 0)
        return *blanks(CHUNKS, LINE), below, above

    waves, across, below, above = lax.cond(polar, polar_second, plain_second)

    def polar_third():
        return tuple(launch(
            middle_kernel,
            [waves, table, polar_mask, adjoint_state, innovation, coefficients, opened, beyond, across],
            [CHUNKS, LINES, LINE, EDGES],
            [FIELD],
            [in_vmem(CHUNKS), table_scratch, small, in_vmem(FIELD), in_vmem(FIELD), in_vmem(COEFF)]
            + [in_vmem(TILES), in_vmem(LINES), in_vmem(LINE), in_vmem(FIELD), *wave_scratch],
            copies=15,
        ))

    def plain_third():
        return blanks(CHUNKS, LINES, LINE, EDGES, FIELD)

    send, to_next, next_line, edges, middle = lax.cond(polar, polar_third, plain_third)
    reached = next_to_pole(to_next, True)

    def polar_fourth():
        received = exchanged(send)
        again, opened = respond(received, tiles)
        return exchanged(again), opened, middle

    def plain_fourth():
        west, east = edge[0], edge[1]
        second, lines, middle = launch(
            plain_middle_kernel,
            [adjoint_state, innovation, coefficients, west, east, below, above, reached],
            [(2, *one_edge), (2, *LINE)],
            [FIELD],
            [in_vmem(FIELD), in_vmem(FIELD), in_vmem(COEFF), in_vmem(one_edge), in_vmem(one_edge)]
            + [in_vmem(LINES), in_vmem(LINES), in_vmem(LINES), in_vmem(FIELD)],
            copies=8,
        )
        west = moved(second[0], plain, 0, 1)
        east = moved(second[1], plain, 0, -1)
        (result,) = launch(
            plain_final_kernel,
            [middle, coefficients, west, east, lines],
            [FIELD],
            (),
            [in_vmem(FIELD), in_vmem(COEFF), in_vmem(one_edge), in_vmem(one_edge), in_vmem((2, *LINE))],
            copies=5,
        )
        return *blanks(CHUNKS, TILES), result

    waves, opened, result = lax.cond(polar, polar_fourth, plain_fourth)
    waves_beyond = next_to_pole(waves, True)

    def polar_fifth():
        (out,) = launch(
            final_kernel,
            [waves, table, polar_mask, result, coefficients, edges, opened, next_line, across],
            (),
            [FIELD],
            [in_vmem(CHUNKS), table_scratch, small, in_vmem(FIELD), in_vmem(COEFF), in_vmem(EDGES)]
            + [in_vmem(TILES), in_vmem(LINE), in_vmem(LINE), in_vmem(FIELD), *wave_scratch],
            copies=13,
        )
        return out

    result = lax.cond(polar, polar_fifth, lambda kept=result: kept)
    (out,) = launch(
        reach_kernel,
        [result, waves_beyond, table, reached],
        (),
        [FIELD],
        [in_vmem(HALF_FIELD), in_vmem(CHUNKS), table_scratch, in_vmem(LINES)],
        copies=4,
        aliases={0: 0},
    )
    return out


def forward_kernel_with_blanks(*refs):
    forward_kernel(*refs[:5], *refs[9:])


def solution(mesh):
    return jax.shard_map(
        local,
        mesh=mesh,
        in_specs=(
            P(None, None, "lat", "lon"),
            P(None, None, "lat", "lon"),
            P(None, None, None, "lat", "lon"),
            P("lat"),
            P("lat"),
        ),
        out_specs=P(None, None, "lat", "lon"),
        check_vma=False,
    )
```

```python
import math

import jax
import jax.numpy as jnp
import numpy as np
from jax import lax
from jax.experimental import pallas as pl
from jax.experimental.pallas import tpu as pltpu
from jax.sharding import PartitionSpec as P

NLON = 5760
KMAX = 64
WAVES = 2 * KMAX
FIELDS = 3
LEV = 12
BAND = 16
HALF = BAND // 2
LON_DEV = 16
LAT_DEV = 16
TOP = LAT_DEV - 1
WIDTH = NLON // LON_DEV
WIDE = 384
SLABS = FIELDS * LEV
ROWS = SLABS * BAND
SHARE = WAVES // LON_DEV
UNROLL = 4

FIELD = (FIELDS, LEV, BAND, WIDTH)
HALF_FIELD = (FIELDS, LEV, HALF, WIDTH)
COEFF = (FIELDS, 5, LEV, BAND, WIDTH)
MORE = ROWS + 64
CHUNKS = (LON_DEV, SHARE, MORE)
FIRST_CHUNKS = (LON_DEV, SHARE, MORE + 128)
LAST_TILE = (LON_DEV, SHARE, 128)
LINE = (SLABS, WIDTH)
ACROSS = (40, WIDE)
LINES = (3, SLABS, WIDTH)
TILES = (2, HALF, 128)
EDGES = (2, BAND, 128)


def wave_tables():
    columns = np.concatenate([np.arange(WIDTH), [WIDTH, -1]])
    phases = (np.arange(LON_DEV)[:, None] * WIDTH + columns[None, :]) % NLON
    phases = phases[:, None, :] * np.arange(KMAX)[None, :, None] % NLON
    radians = phases * (2.0 * math.pi / NLON)
    both = np.concatenate([np.cos(radians), np.sin(radians)], axis=1)
    return np.pad(both, ((0, 0), (0, 0), (0, WIDE - WIDTH - 2))).astype(np.float32)


def split(value):
    high = value.astype(jnp.bfloat16)
    return high, (value - high.astype(jnp.float32)).astype(jnp.bfloat16)


def pair_dot(left, right, left_dim, right_dim):
    return lax.dot_general(
        left, right, (((left_dim,), (right_dim,)), ((), ())), preferred_element_type=jnp.float32
    )


def dot(left, right, left_dim, right_dim):
    (left_high, left_low), (right_high, right_low) = split(left), split(right)
    total = pair_dot(left_high, right_low, left_dim, right_dim)
    total = total + pair_dot(left_low, right_high, left_dim, right_dim)
    return total + pair_dot(left_high, right_high, left_dim, right_dim)


def iota(shape, dim):
    return lax.broadcasted_iota(jnp.int32, shape, dim)


def in_vmem(shape):
    return pltpu.VMEM(shape, jnp.float32)


def launch(kernel, operands, outs, far_outs=(), scratch=(), copies=0, aliases=None, near=0, pinned=False):
    shapes = [*outs, *far_outs]
    nbytes = sum(4 * math.prod(shape) for shape in shapes)
    nbytes += sum(4 * math.prod(operand.shape) for operand in operands)
    return pl.pallas_call(
        kernel,
        in_specs=[pl.BlockSpec(memory_space=pltpu.VMEM)] * near
        + [pl.BlockSpec(memory_space=pltpu.HBM)] * (len(operands) - near),
        out_specs=[pl.BlockSpec(memory_space=pltpu.VMEM)] * len(outs)
        + [pl.BlockSpec(memory_space=pltpu.HBM)] * len(far_outs),
        out_shape=[
            (pltpu.HBM if pinned else jax.ShapeDtypeStruct)(shape, jnp.float32) for shape in shapes
        ],
        scratch_shapes=[*scratch, pltpu.SemaphoreType.DMA((copies,))],
        input_output_aliases=aliases or {},
        compiler_params=pltpu.CompilerParams(vmem_limit_bytes=24 * 2**20),
        cost_estimate=pl.CostEstimate(flops=0, bytes_accessed=nbytes, transcendentals=0),
    )(*operands)


def begin(sems, *pairs):
    started = []
    for index, (source, target) in enumerate(pairs):
        copy = pltpu.make_async_copy(source, target, sems.at[index])
        copy.start()
        started.append(copy)
    return started


def by_field(*pairs):
    return [(source.at[field], target.at[field]) for field in range(FIELDS) for source, target in pairs]


def finish(*started):
    for copy in started:
        copy.wait()


def for_levels(field, one, carry=0):
    def some(step, carry):
        for level in range(UNROLL):
            carry = one(field, step * UNROLL + level, carry)
        return carry

    return lax.fori_loop(0, LEV // UNROLL, some, carry)


def for_slabs(one, carry=0):
    for field in range(FIELDS):
        carry = for_levels(field, one, carry)
    return carry


def lane_of(tile, slab):
    return jnp.sum(jnp.where(iota(tile.shape, 1) == slab, tile, 0.0), axis=1, keepdims=True)


def with_lane(tile, slab, column):
    return jnp.where(iota(tile.shape, 1) == slab, column, tile)


def place():
    return lax.axis_index("lon"), lax.axis_index("lat")


def open_row(lat):
    return pl.multiple_of(jnp.where(lat == TOP, 0, HALF), HALF)


def row_weight(mask, first, shape):
    row = iota(shape, 0)
    weight = jnp.zeros(shape, jnp.float32)
    for r in range(shape[0]):
        weight = jnp.where(row == r, mask[first + r].astype(jnp.float32), weight)
    return weight


TILED = ACROSS[0] // 8 * (WIDE // 128)


def tile_place(index):
    row, column = index // (WIDE // 128), index % (WIDE // 128)
    return slice(8 * row, 8 * row + 8), slice(128 * column, 128 * column + 128)


def forward_kernel(
    field_in, coeff_in, table_in, mask_in,
    send,
    field, table, to_east, to_west, pole, across, mask, sems,
):
    lon, lat = place()
    top = lat == TOP
    first = open_row(lat)
    rows = pl.ds(first, HALF)
    closed = pl.ds(pl.multiple_of(HALF - first, HALF), HALF)
    field_copy, table_copy, *rest = begin(
        sems,
        (field_in, field),
        (table_in.at[lon], table),
        (coeff_in.at[:, 3, :, rows], to_east),
        (coeff_in.at[:, 4, :, rows], to_west),
        (mask_in, mask),
        (coeff_in.at[:, jnp.where(top, 1, 2), :, closed], pole),
    )
    across[...] = jnp.zeros(ACROSS, jnp.float32)
    finish(field_copy, table_copy)
    waves = dot(table[:, :WIDTH], field[...].reshape(ROWS, WIDTH), 1, 1)
    send[:, :, :ROWS] = waves.reshape(LON_DEV, SHARE, ROWS)
    finish(*rest)
    filtered = row_weight(mask, first, (HALF, 1)) > 0.5
    east = west = jnp.zeros((HALF, 128), jnp.float32)
    for slab in range(SLABS):
        at = slab // LEV, slab % LEV
        value = field[*at, rows]
        coeff = to_east[at][:, WIDTH - 1 :]
        east = with_lane(east, slab, jnp.where(filtered, coeff, coeff * value[:, WIDTH - 1 :]))
        coeff = to_west[at][:, 0:1]
        west = with_lane(west, slab, jnp.where(filtered, coeff, coeff * value[:, 0:1]))
        sign = 1.0 if at[0] == FIELDS - 1 else -1.0
        lines = pole[at]
        line = jnp.where(top, lines[HALF - 1 :], lines[0:1])
        across[slab : slab + 1, :WIDTH] = sign * line
    for target in range(LON_DEV):
        tile = jnp.where(target == (lon + 1) % LON_DEV, east, west)
        send[target, :, ROWS:MORE] = tile[:, :64]
        send[target, :, MORE:] = across[tile_place(target)] if target < TILED else tile


def closed_kernel(coeff_in, tiles, to_east, to_west, sems):
    _, lat = place()
    closed = pl.ds(pl.multiple_of(HALF - open_row(lat), HALF), HALF)
    finish(
        *begin(
            sems,
            (coeff_in.at[:, 3, :, closed], to_east),
            (coeff_in.at[:, 4, :, closed], to_west),
        )
    )
    east = west = jnp.zeros((HALF, 128), jnp.float32)
    for slab in range(SLABS):
        at = slab // LEV, slab % LEV
        east = with_lane(east, slab, to_east[at][:, WIDTH - 1 :])
        west = with_lane(west, slab, to_west[at][:, 0:1])
    tiles[0] = east
    tiles[1] = west


def responded(received, cutoff, edges):
    lon, _ = place()
    shape = (SHARE, ROWS)
    wave = (lon * SHARE + iota(shape, 0)) % KMAX
    row = iota(shape, 1) % BAND
    limit = jnp.zeros(shape, jnp.int32)
    for r in range(BAND):
        limit = jnp.where(row == r, cutoff[r], limit)
    ratio = limit.astype(jnp.float32) / jnp.maximum(wave, 1).astype(jnp.float32)
    response = jnp.where(wave <= limit, 1.0, ratio * ratio)
    response = response * jnp.where(wave == 0, 1.0 / NLON, 2.0 / NLON)
    total = received[0, :, :ROWS]
    for source in range(1, LON_DEV):
        total = total + received[source, :, :ROWS]
    blank = jnp.zeros((HALF, 64), jnp.float32)
    west = received[(lon + LON_DEV - 1) % LON_DEV, :, ROWS:MORE]
    east = received[(lon + 1) % LON_DEV, :, ROWS:MORE]
    edges[0] = jnp.concatenate([west, blank], axis=1)
    edges[1] = jnp.concatenate([east, blank], axis=1)
    return total * response


def first_respond_kernel(received, cutoff_in, tiles_in, send, edges, cutoff, tiles, sems):
    lon, _ = place()
    finish(*begin(sems, (cutoff_in, cutoff), (tiles_in, tiles)))
    total = responded(received, cutoff, edges)
    for target in range(LON_DEV):
        send[target, :, :ROWS] = total
        tile = jnp.where(target == (lon + 1) % LON_DEV, tiles[0], tiles[1])
        send[target, :, ROWS:MORE] = tile[:, :64]
        send[target, :, MORE:] = received[(target + LON_DEV // 2) % LON_DEV, :, MORE:]


def second_respond_kernel(received, cutoff_in, send, edges, cutoff, sems):
    _, lat = place()
    finish(*begin(sems, (cutoff_in, cutoff)))
    total = responded(received, cutoff, edges)
    near = row_waves(total, jnp.where(lat == TOP, 0, BAND - 1))
    for target in range(LON_DEV):
        send[target, :, :ROWS] = total
        send[target, :, ROWS:] = near[:, :64]


def gather_terms(value, coeff, south_line, north_line, west_edge, east_edge):
    to_north, to_south = coeff[1] * value, coeff[2] * value
    total = coeff[0] * value
    total = total + jnp.concatenate([south_line, to_north[:-1]], axis=0)
    total = total + jnp.concatenate([to_south[1:], north_line], axis=0)
    total = total + jnp.concatenate([west_edge, (coeff[3] * value)[:, :-1]], axis=1)
    total = total + jnp.concatenate([(coeff[4] * value)[:, 1:], east_edge], axis=1)
    return total, to_north, to_south


def load_coeff(coeff, field, level):
    return [coeff[field, term, level] for term in range(5)]


def row_waves(waves, row):
    picked = iota((ROWS, 128), 0) == iota((ROWS, 128), 1) * BAND + row
    picked = picked.astype(jnp.float32).astype(jnp.bfloat16)
    high, low = split(waves)
    return pair_dot(high, picked, 1, 0) + pair_dot(low, picked, 1, 0)


def across_pole(waves, table, row):
    chosen = row_waves(waves, row)
    chosen = jnp.where(iota((WAVES, 128), 0) % 2 == 1, -chosen, chosen)
    return dot(chosen, table, 0, 0)


def whole_band(closed, opened, top):
    return jnp.where(
        top, jnp.concatenate([opened, closed], axis=0), jnp.concatenate([closed, opened], axis=0)
    )


def middle_kernel(
    waves, table_in, mask_in, state_in, extra_in, coeff_in, opened_in, beyond_in,
    send, to_next, next_line, edges, across, middle_out,
    table, mask, state, extra, coeff_ref, opened, beyond, middle,
    filtered, opposite, sems,
):
    lon, lat = place()
    top = lat == TOP
    table_copy, *rest = begin(
        sems,
        (table_in.at[lon], table),
        (mask_in, mask),
        (opened_in, opened),
        (beyond_in, beyond),
        *by_field((state_in, state), (extra_in, extra), (coeff_in, coeff_ref)),
    )
    rest, fields = rest[:3], rest[3:]
    for tile in range(TILED):
        across[tile_place(tile)] = waves[tile, :, MORE:]
    finish(table_copy)
    flat = waves[:, :, :ROWS].reshape(WAVES, ROWS)
    filtered[...] = dot(flat, table[...], 0, 0)
    polar_row = jnp.where(top, BAND - 1, 0)
    opposite[...] = across_pole(flat, table[...], polar_row)
    finish(*rest)
    blank = jnp.zeros((HALF, 64), jnp.float32)
    sides = (lon + LON_DEV - 1) % LON_DEV, (lon + 1) % LON_DEV
    for side in range(2):
        closed = jnp.concatenate([waves[sides[side], :, ROWS:MORE], blank], axis=1)
        edges[side] = whole_band(closed, opened[side], top)
    weight = row_weight(mask, 0, (BAND, WIDTH))
    is_filtered = weight[:, 0:1] > 0.5
    next_weight = jnp.where(top, weight[0:1], weight[BAND - 1 :])
    row = iota((BAND, WIDTH), 0)

    def one(field, level, carry):
        east_tile, west_tile = carry
        slab = field * LEV + level
        here = pl.ds(slab, 1)
        value = state[field, level]
        smooth = filtered[pl.ds(slab * BAND, BAND)]
        value = value + weight * (smooth[:, :WIDTH] - value)
        coeff = load_coeff(coeff_ref, field, level)
        west = lane_of(edges[0], slab)
        west = jnp.where(is_filtered, west * smooth[:, WIDTH + 1 : WIDTH + 2], west)
        east = lane_of(edges[1], slab)
        east = jnp.where(is_filtered, east * smooth[:, WIDTH : WIDTH + 1], east)
        halo = beyond[2, here]
        total, north, south = gather_terms(
            value, coeff, jnp.where(top, halo, 0.0), jnp.where(top, 0.0, halo), west, east
        )
        pole = (across[here] * opposite[here])[:, :WIDTH]
        total = total + jnp.where(row == polar_row, pole, 0.0) + extra[field, level]
        middle[field, level] = total
        product = jnp.where(top, south[0:1], north[BAND - 1 :])
        near = jnp.where(top, total[0:1], total[BAND - 1 :])
        near_coeff = jnp.where(top, coeff[2][0:1], coeff[1][BAND - 1 :])
        to_next[0, here] = product
        to_next[1, here] = (1.0 - next_weight) * near_coeff * near
        to_next[2, here] = next_weight * near_coeff
        next_line[here] = beyond[1, here] * (beyond[0, here] + product)
        column = (coeff[3] * total)[:, WIDTH - 1 :]
        east_tile = with_lane(east_tile, slab, jnp.where(top, column[:HALF], column[HALF:]))
        column = (coeff[4] * total)[:, 0:1]
        west_tile = with_lane(west_tile, slab, jnp.where(top, column[:HALF], column[HALF:]))
        return east_tile, west_tile

    none = jnp.zeros((HALF, 128), jnp.float32)
    carry, stored = (none, none), []
    for field in range(FIELDS):
        finish(*fields[3 * field : 3 * field + 3])
        carry = for_levels(field, one, carry)
        stored += begin(sems.at[field : field + 1], (middle.at[field], middle_out.at[field]))
    east_tile, west_tile = carry
    sums = dot(table[:, :WIDTH], middle[...].reshape(ROWS, WIDTH), 1, 1)
    send[:, :, :ROWS] = sums.reshape(LON_DEV, SHARE, ROWS)
    for target in range(LON_DEV):
        tile = jnp.where(target == (lon + 1) % LON_DEV, east_tile, west_tile)
        send[target, :, ROWS:] = tile[:, :64]
    finish(*stored)


def final_kernel(
    waves, table_in, mask_in, middle_in, coeff_in, edges_in, opened_in, line_in, across_in,
    out,
    table, mask, middle, coeff_ref, edges, opened, next_line, across, result,
    filtered, opposite, sems,
):
    lon, lat = place()
    top = lat == TOP
    table_copy, *rest = begin(
        sems,
        (table_in.at[lon], table),
        (mask_in, mask),
        (edges_in, edges),
        (opened_in, opened),
        (line_in, next_line),
        (across_in, across),
        *by_field((middle_in, middle), (coeff_in, coeff_ref)),
    )
    rest, fields = rest[:5], rest[5:]
    finish(table_copy)
    flat = waves[:, :, :ROWS].reshape(WAVES, ROWS)
    filtered[...] = dot(flat, table[...], 0, 0)
    polar_row = jnp.where(top, BAND - 1, 0)
    opposite[...] = across_pole(flat, table[...], polar_row)
    finish(*rest)
    weight = row_weight(mask, 0, (BAND, WIDTH))
    is_filtered = weight[:, 0:1] > 0.5
    row = iota((BAND, WIDTH), 0)
    none = jnp.zeros((HALF, 128), jnp.float32)
    west_band = whole_band(none, opened[0], top)
    east_band = whole_band(none, opened[1], top)

    def one(field, level, carry):
        slab = field * LEV + level
        here = pl.ds(slab, 1)
        value = middle[field, level]
        smooth = filtered[pl.ds(slab * BAND, BAND)]
        value = value + weight * (smooth[:, :WIDTH] - value)
        coeff = load_coeff(coeff_ref, field, level)
        west = lane_of(edges[0], slab) * smooth[:, WIDTH + 1 : WIDTH + 2]
        west = jnp.where(is_filtered, west, lane_of(west_band, slab))
        east = lane_of(edges[1], slab) * smooth[:, WIDTH : WIDTH + 1]
        east = jnp.where(is_filtered, east, lane_of(east_band, slab))
        halo = next_line[here]
        total, _, _ = gather_terms(
            value, coeff, jnp.where(top, halo, 0.0), jnp.where(top, 0.0, halo), west, east
        )
        pole = (across[here] * opposite[here])[:, :WIDTH]
        result[field, level] = total + jnp.where(row == polar_row, pole, 0.0)
        return carry

    stored = []
    for field in range(FIELDS):
        finish(*fields[2 * field : 2 * field + 2])
        for_levels(field, one)
        stored += begin(sems.at[field : field + 1], (result.at[field], out.at[field]))
    finish(*stored)


def edge_kernel(field_in, coeff_in, edges, field, to_east, to_west, sems):
    finish(
        *begin(
            sems,
            (field_in, field),
            (coeff_in.at[:, 3], to_east),
            (coeff_in.at[:, 4], to_west),
        )
    )
    east = west = jnp.zeros((BAND, 128), jnp.float32)
    for slab in range(SLABS):
        at = slab // LEV, slab % LEV
        value = field[at]
        east = with_lane(east, slab, (to_east[at] * value)[:, WIDTH - 1 :])
        west = with_lane(west, slab, (to_west[at] * value)[:, 0:1])
    edges[0] = east
    edges[1] = west


def line_kernel(
    field_in, extra_in, coeff_in, west_in, east_in,
    to_north, to_south, to_polar,
    field_ref, extra, coeff_ref, west_edge, east_edge, sems,
):
    _, lat = place()
    finish(
        *begin(
            sems,
            (field_in, field_ref),
            (extra_in, extra),
            (coeff_in, coeff_ref),
            (west_in, west_edge),
            (east_in, east_edge),
        )
    )
    none = jnp.zeros((1, WIDTH), jnp.float32)

    def one(field, level, carry):
        slab = field * LEV + level
        here = pl.ds(slab, 1)
        coeff = load_coeff(coeff_ref, field, level)
        west, east = lane_of(west_edge[...], slab), lane_of(east_edge[...], slab)
        total, north, south = gather_terms(field_ref[field, level], coeff, none, none, west, east)
        total = total + extra[field, level]
        norths = total[BAND - 1 :], coeff[1][BAND - 1 :], north[BAND - 1 :]
        souths = total[0:1], coeff[2][0:1], south[0:1]
        for part in range(3):
            to_north[part, here] = norths[part]
            to_south[part, here] = souths[part]
            to_polar[part, here] = jnp.where(lat == 1, souths[part], norths[part])
        return carry

    for_slabs(one)


def plain_middle_kernel(
    state_in, extra_in, coeff_in, west_in, east_in, below_in, above_in, polar_in,
    edges, lines, middle_out,
    state, extra, coeff_ref, west_edge, east_edge, below, above, polar, middle, sems,
):
    _, lat = place()
    finish(
        *begin(
            sems,
            (state_in, state),
            (extra_in, extra),
            (coeff_in, coeff_ref),
            (west_in, west_edge),
            (east_in, east_edge),
            (below_in, below),
            (above_in, above),
            (polar_in, polar),
        )
    )

    def one(field, level, carry):
        east_tile, west_tile = carry
        slab = field * LEV + level
        here = pl.ds(slab, 1)
        coeff = load_coeff(coeff_ref, field, level)
        west, east = lane_of(west_edge[...], slab), lane_of(east_edge[...], slab)
        reached = polar[0, here]
        total, north, south = gather_terms(
            state[field, level],
            coeff,
            jnp.where(lat == 1, reached, below[2, here]),
            jnp.where(lat == TOP - 1, reached, above[2, here]),
            west,
            east,
        )
        total = total + extra[field, level]
        middle[field, level] = total
        low = below[1, here] * (below[0, here] + south[0:1])
        high = above[1, here] * (above[0, here] + north[BAND - 1 :])
        lines[0, here] = jnp.where(lat == 1, 0.0, low)
        lines[1, here] = jnp.where(lat == TOP - 1, 0.0, high)
        east_tile = with_lane(east_tile, slab, (coeff[3] * total)[:, WIDTH - 1 :])
        west_tile = with_lane(west_tile, slab, (coeff[4] * total)[:, 0:1])
        return east_tile, west_tile

    none = jnp.zeros((BAND, 128), jnp.float32)
    edges[0], edges[1] = for_slabs(one, (none, none))
    finish(*begin(sems, (middle, middle_out)))


def plain_final_kernel(
    middle_in, coeff_in, west_in, east_in, lines_in,
    out,
    middle, coeff_ref, west_edge, east_edge, lines, sems,
):
    finish(
        *begin(
            sems,
            (middle_in, middle),
            (coeff_in, coeff_ref),
            (west_in, west_edge),
            (east_in, east_edge),
            (lines_in, lines),
        )
    )

    def one(field, level, carry):
        slab = field * LEV + level
        here = pl.ds(slab, 1)
        coeff = load_coeff(coeff_ref, field, level)
        west, east = lane_of(west_edge[...], slab), lane_of(east_edge[...], slab)
        value = middle[field, level]
        out[field, level] = gather_terms(value, coeff, lines[0, here], lines[1, here], west, east)[0]
        return carry

    for_slabs(one)


def reach_kernel(result_in, waves_in, table_in, polar_in, result_out, part, waves, table, polar, sems):
    lon, lat = place()
    next_to = (lat == 1) | (lat == TOP - 1)
    bottom = lat == 1
    rows = pl.ds(pl.multiple_of(jnp.where(bottom, 0, HALF), HALF), HALF)

    @pl.when(next_to)
    def _():
        finish(
            *begin(
                sems,
                (result_in.at[:, :, rows], part),
                (waves_in, waves),
                (table_in.at[lon], table),
                (polar_in, polar),
            )
        )
        smooth = dot(waves[...].reshape(WAVES, 128), table[...], 0, 0)
        line = polar[1] + polar[2] * smooth[64 : 64 + SLABS, :WIDTH]
        row = iota((HALF, WIDTH), 0)
        mine = row == jnp.where(bottom, 0, HALF - 1)
        for slab in range(SLABS):
            at = slab // LEV, slab % LEV
            part[at] = part[at] + jnp.where(mine, line[slab : slab + 1], 0.0)
        finish(*begin(sems, (part, result_out.at[:, :, rows])))


def exchanged(chunks):
    return lax.all_to_all(chunks, "lon", split_axis=0, concat_axis=0, tiled=True)


def moved(value, lats, north, east):
    pairs = []
    for lat, lon in [(lat, lon) for lat in lats for lon in range(LON_DEV)]:
        pairs.append((lat * LON_DEV + lon, (lat + north) * LON_DEV + (lon + east) % LON_DEV))
    return lax.ppermute(value, ("lat", "lon"), pairs)


def next_to_pole(value, outward):
    pairs = []
    for lon in range(LON_DEV):
        for polar, other in ((0, 1), (TOP, TOP - 1)):
            pair = polar * LON_DEV + lon, other * LON_DEV + lon
            pairs.append(pair if outward else pair[::-1])
    return lax.ppermute(value, ("lat", "lon"), pairs)


def local(adjoint_state, innovation, coefficients, polar_mask, wave_cutoff):
    lat = lax.axis_index("lat")
    polar = (lat == 0) | (lat == TOP)
    table = jnp.asarray(wave_tables())
    small = pltpu.SMEM((BAND,), jnp.int32)
    plain = range(1, TOP)
    table_scratch = in_vmem((WAVES, WIDE))
    wave_scratch = [in_vmem((ROWS, WIDE)), in_vmem((128, WIDE))]
    one_edge = (BAND, 128)

    def blanks(*shapes):
        return tuple(jnp.zeros(shape, jnp.float32) for shape in shapes)

    def polar_first():
        half = in_vmem(HALF_FIELD)
        send, to_polar, to_north, to_south, edge = launch(
            forward_kernel_with_blanks,
            [adjoint_state, coefficients, table, polar_mask],
            [FIRST_CHUNKS],
            [LINES, LINES, LINES, (2, *one_edge)],
            [in_vmem(FIELD), table_scratch, half, half, half, in_vmem(ACROSS), small],
            copies=6,
        )
        received = exchanged(send)
        (tiles,) = launch(closed_kernel, [coefficients], [TILES], (), [half, half], copies=2)
        send, opened = launch(
            first_respond_kernel,
            [received, wave_cutoff, tiles],
            [FIRST_CHUNKS, TILES],
            (),
            [small, in_vmem(TILES)],
            copies=2,
            near=1,
        )
        return send, opened, to_polar, to_north, to_south, edge

    def plain_first():
        (edges,) = launch(
            edge_kernel,
            [adjoint_state, coefficients],
            [(2, *one_edge)],
            (),
            [in_vmem(FIELD)] * 3,
            copies=3,
        )
        west = moved(edges[0], plain, 0, 1)
        east = moved(edges[1], plain, 0, -1)
        to_north, to_south, to_polar = launch(
            line_kernel,
            [adjoint_state, innovation, coefficients, west, east],
            [LINES, LINES, LINES],
            (),
            [in_vmem(FIELD), in_vmem(FIELD), in_vmem(COEFF), in_vmem(one_edge), in_vmem(one_edge)],
            copies=5,
        )
        send, opened = blanks(FIRST_CHUNKS, TILES)
        return send, opened, to_polar, to_north, to_south, jnp.stack([west, east])

    send, opened, to_polar, to_north, to_south, edge = lax.cond(polar, polar_first, plain_first)
    beyond = next_to_pole(to_polar, False)

    def polar_second():
        return exchanged(send), to_north, to_south

    def plain_second():
        below = moved(to_north, range(1, TOP - 1), 1, 0)
        above = moved(to_south, range(2, TOP), -1, 0)
        return *blanks(FIRST_CHUNKS), below, above

    waves, below, above = lax.cond(polar, polar_second, plain_second)

    def polar_third():
        return tuple(launch(
            middle_kernel,
            [waves, table, polar_mask, adjoint_state, innovation, coefficients, opened, beyond],
            [CHUNKS, LINES, LINE, EDGES, ACROSS],
            [FIELD],
            [table_scratch, small, in_vmem(FIELD), in_vmem(FIELD), in_vmem(COEFF)]
            + [in_vmem(TILES), in_vmem(LINES), in_vmem(FIELD), *wave_scratch],
            copies=13,
            near=1,
        ))

    def plain_third():
        return blanks(CHUNKS, LINES, LINE, EDGES, ACROSS, FIELD)

    send, to_next, next_line, edges, across, middle = lax.cond(polar, polar_third, plain_third)
    reached = next_to_pole(to_next, True)

    def polar_fourth():
        received = exchanged(send)
        again, opened = launch(
            second_respond_kernel,
            [received, wave_cutoff],
            [CHUNKS, TILES],
            (),
            [small],
            copies=1,
            near=1,
        )
        waves = exchanged(again)
        return waves, lax.slice_in_dim(waves, MORE - 128, MORE, axis=2), opened, middle

    def plain_fourth():
        west, east = edge[0], edge[1]
        second, lines, middle = launch(
            plain_middle_kernel,
            [adjoint_state, innovation, coefficients, west, east, below, above, reached],
            [(2, *one_edge), (2, *LINE)],
            [FIELD],
            [in_vmem(FIELD), in_vmem(FIELD), in_vmem(COEFF), in_vmem(one_edge), in_vmem(one_edge)]
            + [in_vmem(LINES), in_vmem(LINES), in_vmem(LINES), in_vmem(FIELD)],
            copies=8,
        )
        west = moved(second[0], plain, 0, 1)
        east = moved(second[1], plain, 0, -1)
        (result,) = launch(
            plain_final_kernel,
            [middle, coefficients, west, east, lines],
            [FIELD],
            (),
            [in_vmem(FIELD), in_vmem(COEFF), in_vmem(one_edge), in_vmem(one_edge), in_vmem((2, *LINE))],
            copies=5,
        )
        return *blanks(CHUNKS, LAST_TILE, TILES), result

    waves, near_waves, opened, result = lax.cond(polar, polar_fourth, plain_fourth)
    waves_beyond = next_to_pole(near_waves, True)

    def polar_fifth():
        (out,) = launch(
            final_kernel,
            [waves, table, polar_mask, result, coefficients, edges, opened, next_line, across],
            (),
            [FIELD],
            [table_scratch, small, in_vmem(FIELD), in_vmem(COEFF), in_vmem(EDGES)]
            + [in_vmem(TILES), in_vmem(LINE), in_vmem(ACROSS), in_vmem(FIELD), *wave_scratch],
            copies=12,
            near=1,
            pinned=True,
        )
        return out

    result = lax.cond(polar, polar_fifth, lambda kept=result: kept)
    (out,) = launch(
        reach_kernel,
        [result, waves_beyond, table, reached],
        (),
        [FIELD],
        [in_vmem(HALF_FIELD), in_vmem(LAST_TILE), table_scratch, in_vmem(LINES)],
        copies=4,
        aliases={0: 0},
        pinned=True,
    )
    return out


def forward_kernel_with_blanks(*refs):
    forward_kernel(*refs[:5], *refs[9:])


def solution(mesh):
    return jax.shard_map(
        local,
        mesh=mesh,
        in_specs=(
            P(None, None, "lat", "lon"),
            P(None, None, "lat", "lon"),
            P(None, None, None, "lat", "lon"),
            P("lat"),
            P("lat"),
        ),
        out_specs=P(None, None, "lat", "lon"),
        check_vma=False,
    )
```

```python
import math

import jax
import jax.numpy as jnp
import numpy as np
from jax import lax
from jax.experimental import pallas as pl
from jax.experimental.pallas import tpu as pltpu
from jax.sharding import PartitionSpec as P

NLON = 5760
KMAX = 64
WAVES = 2 * KMAX
FIELDS = 3
LEV = 12
BAND = 16
HALF = BAND // 2
LON_DEV = 16
LAT_DEV = 16
TOP = LAT_DEV - 1
WIDTH = NLON // LON_DEV
WIDE = 384
LAST = (WIDTH - 1) // 128 * 128
SLABS = FIELDS * LEV
ROWS = SLABS * BAND
SHARE = WAVES // LON_DEV
UNROLL = 6

FIELD = (FIELDS, LEV, BAND, WIDTH)
HALF_FIELD = (FIELDS, LEV, HALF, WIDTH)
COEFF = (FIELDS, 5, LEV, BAND, WIDTH)
MORE = ROWS + 64
CHUNKS = (LON_DEV, SHARE, MORE)
FIRST_CHUNKS = (LON_DEV, SHARE, MORE + 128)
LAST_TILE = (LON_DEV, SHARE, 128)
LINE = (SLABS, WIDTH)
ACROSS = (40, WIDE)
LINES = (3, SLABS, WIDTH)
TILES = (2, HALF, 128)
EDGES = (2, BAND, 128)


def wave_tables():
    columns = np.concatenate([np.arange(WIDTH), [WIDTH, -1]])
    phases = (np.arange(LON_DEV)[:, None] * WIDTH + columns[None, :]) % NLON
    phases = phases[:, None, :] * np.arange(KMAX)[None, :, None] % NLON
    radians = phases * (2.0 * math.pi / NLON)
    both = np.concatenate([np.cos(radians), np.sin(radians)], axis=1)
    return np.pad(both, ((0, 0), (0, 0), (0, WIDE - WIDTH - 2))).astype(np.float32)


def split(value):
    high = value.astype(jnp.bfloat16)
    return high, (value - high.astype(jnp.float32)).astype(jnp.bfloat16)


def pair_dot(left, right, left_dim, right_dim):
    return lax.dot_general(
        left, right, (((left_dim,), (right_dim,)), ((), ())), preferred_element_type=jnp.float32
    )


def dot(left, right, left_dim, right_dim):
    (left_high, left_low), (right_high, right_low) = split(left), split(right)
    total = pair_dot(left_high, right_low, left_dim, right_dim)
    total = total + pair_dot(left_low, right_high, left_dim, right_dim)
    return total + pair_dot(left_high, right_high, left_dim, right_dim)


def iota(shape, dim):
    return lax.broadcasted_iota(jnp.int32, shape, dim)


def in_vmem(shape):
    return pltpu.VMEM(shape, jnp.float32)


def launch(kernel, operands, outs, far_outs=(), scratch=(), copies=0, aliases=None, near=0, pinned=False):
    shapes = [*outs, *far_outs]
    nbytes = sum(4 * math.prod(shape) for shape in shapes)
    nbytes += sum(4 * math.prod(operand.shape) for operand in operands)
    return pl.pallas_call(
        kernel,
        in_specs=[pl.BlockSpec(memory_space=pltpu.VMEM)] * near
        + [pl.BlockSpec(memory_space=pltpu.HBM)] * (len(operands) - near),
        out_specs=[pl.BlockSpec(memory_space=pltpu.VMEM)] * len(outs)
        + [pl.BlockSpec(memory_space=pltpu.HBM)] * len(far_outs),
        out_shape=[
            (pltpu.HBM if pinned else jax.ShapeDtypeStruct)(shape, jnp.float32) for shape in shapes
        ],
        scratch_shapes=[*scratch, pltpu.SemaphoreType.DMA((copies,))],
        input_output_aliases=aliases or {},
        compiler_params=pltpu.CompilerParams(vmem_limit_bytes=24 * 2**20),
        cost_estimate=pl.CostEstimate(flops=0, bytes_accessed=nbytes, transcendentals=0),
    )(*operands)


def begin(sems, *pairs):
    started = []
    for index, (source, target) in enumerate(pairs):
        copy = pltpu.make_async_copy(source, target, sems.at[index])
        copy.start()
        started.append(copy)
    return started


def by_field(*pairs):
    return [(source.at[field], target.at[field]) for field in range(FIELDS) for source, target in pairs]


def finish(*started):
    for copy in started:
        copy.wait()


def for_levels(field, one, carry=0):
    def some(step, carry):
        for level in range(UNROLL):
            carry = one(field, step * UNROLL + level, carry)
        return carry

    return lax.fori_loop(0, LEV // UNROLL, some, carry)


def for_slabs(one, carry=0):
    for field in range(FIELDS):
        carry = for_levels(field, one, carry)
    return carry


def lane_of(tile, slab):
    return jnp.sum(jnp.where(iota(tile.shape, 1) == slab, tile, 0.0), axis=1, keepdims=True)


def with_lane(tile, slab, column):
    return jnp.where(iota(tile.shape, 1) == slab, column, tile)


def exact_dot(value, chosen, left_dim=1, right_dim=0):
    high, low = split(value)
    chosen = chosen.astype(jnp.float32).astype(jnp.bfloat16)
    return pair_dot(high, chosen, left_dim, right_dim) + pair_dot(low, chosen, left_dim, right_dim)


def every_lane(values, lane):
    return exact_dot(values, iota((values.shape[1], 128), 0) == lane)


def own_lane(rows):
    shape = (SLABS * rows, 128)
    return iota(shape, 0) // rows == iota(shape, 1)


def tile_of(values, lane, rows, first):
    spread = jnp.where(own_lane(rows), every_lane(values, lane), 0.0)
    shape = (HALF, SLABS * rows)
    picked = iota(shape, 1) % rows == iota(shape, 0) + first
    picked = picked.astype(jnp.float32).astype(jnp.bfloat16)
    high, low = split(spread)
    return pair_dot(picked, high, 1, 0) + pair_dot(picked, low, 1, 0)


def halo_of(tile, wave_lanes, lane, weight):
    tall = jnp.concatenate([tile] * SLABS, axis=0)
    spread = exact_dot(jnp.where(own_lane(BAND), tall, 0.0), iota((128, 128), 0) >= 0)
    filtered = jnp.concatenate([weight] * SLABS, axis=0) > 0.5
    return spread * jnp.where(filtered, every_lane(wave_lanes, lane), 1.0)


def place():
    return lax.axis_index("lon"), lax.axis_index("lat")


def open_row(lat):
    return pl.multiple_of(jnp.where(lat == TOP, 0, HALF), HALF)


def row_weight(mask, first, shape):
    row = iota(shape, 0)
    weight = jnp.zeros(shape, jnp.float32)
    for r in range(shape[0]):
        weight = jnp.where(row == r, mask[first + r].astype(jnp.float32), weight)
    return weight


TILED = ACROSS[0] // 8 * (WIDE // 128)


def tile_place(index):
    row, column = index // (WIDE // 128), index % (WIDE // 128)
    return slice(8 * row, 8 * row + 8), slice(128 * column, 128 * column + 128)


def forward_kernel(
    field_in, coeff_in, table_in, mask_in,
    send,
    field, table, to_east, to_west, pole, across, mask, sems,
):
    lon, lat = place()
    top = lat == TOP
    first = open_row(lat)
    rows = pl.ds(first, HALF)
    closed = pl.ds(pl.multiple_of(HALF - first, HALF), HALF)
    field_copy, table_copy, *rest = begin(
        sems,
        (field_in, field),
        (table_in.at[lon], table),
        (coeff_in.at[:, 3, :, rows], to_east),
        (coeff_in.at[:, 4, :, rows], to_west),
        (mask_in, mask),
        (coeff_in.at[:, jnp.where(top, 1, 2), :, closed], pole),
    )
    across[...] = jnp.zeros(ACROSS, jnp.float32)
    finish(field_copy, table_copy)
    waves = dot(table[:, :WIDTH], field[...].reshape(ROWS, WIDTH), 1, 1)
    send[:, :, :ROWS] = waves.reshape(LON_DEV, SHARE, ROWS)
    finish(*rest)
    filtered = row_weight(mask, first, (HALF, 128)) > 0.5
    filtered = jnp.concatenate([filtered.astype(jnp.float32)] * SLABS, axis=0) > 0.5
    flat = SLABS * HALF, 128
    coeff, value = to_west[:, :, :, :128].reshape(flat), field[:, :, rows, :128].reshape(flat)
    west = tile_of(jnp.where(filtered, coeff, coeff * value), 0, HALF, 0)
    flat, filtered = (flat[0], WIDTH - LAST), filtered[:, : WIDTH - LAST]
    coeff, value = to_east[:, :, :, LAST:].reshape(flat), field[:, :, rows, LAST:].reshape(flat)
    east = tile_of(jnp.where(filtered, coeff, coeff * value), WIDTH - LAST - 1, HALF, 0)
    for slab in range(SLABS):
        at = slab // LEV, slab % LEV
        sign = 1.0 if at[0] == FIELDS - 1 else -1.0
        lines = pole[at]
        line = jnp.where(top, lines[HALF - 1 :], lines[0:1])
        across[slab : slab + 1, :WIDTH] = sign * line
    for target in range(LON_DEV):
        tile = jnp.where(target == (lon + 1) % LON_DEV, east, west)
        send[target, :, ROWS:MORE] = tile[:, :64]
        send[target, :, MORE:] = across[tile_place(target)] if target < TILED else tile


def closed_kernel(coeff_in, tiles, to_east, to_west, sems):
    _, lat = place()
    closed = pl.ds(pl.multiple_of(HALF - open_row(lat), HALF), HALF)
    finish(
        *begin(
            sems,
            (coeff_in.at[:, 3, :, closed], to_east),
            (coeff_in.at[:, 4, :, closed], to_west),
        )
    )
    east = west = jnp.zeros((HALF, 128), jnp.float32)
    for slab in range(SLABS):
        at = slab // LEV, slab % LEV
        east = with_lane(east, slab, to_east[at][:, WIDTH - 1 :])
        west = with_lane(west, slab, to_west[at][:, 0:1])
    tiles[0] = east
    tiles[1] = west


def responded(received, cutoff, edges):
    lon, _ = place()
    shape = (SHARE, ROWS)
    wave = (lon * SHARE + iota(shape, 0)) % KMAX
    row = iota(shape, 1) % BAND
    limit = jnp.zeros(shape, jnp.int32)
    for r in range(BAND):
        limit = jnp.where(row == r, cutoff[r], limit)
    ratio = limit.astype(jnp.float32) / jnp.maximum(wave, 1).astype(jnp.float32)
    response = jnp.where(wave <= limit, 1.0, ratio * ratio)
    response = response * jnp.where(wave == 0, 1.0 / NLON, 2.0 / NLON)
    total = received[0, :, :ROWS]
    for source in range(1, LON_DEV):
        total = total + received[source, :, :ROWS]
    blank = jnp.zeros((HALF, 64), jnp.float32)
    west = received[(lon + LON_DEV - 1) % LON_DEV, :, ROWS:MORE]
    east = received[(lon + 1) % LON_DEV, :, ROWS:MORE]
    edges[0] = jnp.concatenate([west, blank], axis=1)
    edges[1] = jnp.concatenate([east, blank], axis=1)
    return total * response


def first_respond_kernel(received, cutoff_in, tiles_in, send, edges, cutoff, tiles, sems):
    lon, _ = place()
    finish(*begin(sems, (cutoff_in, cutoff), (tiles_in, tiles)))
    total = responded(received, cutoff, edges)
    for target in range(LON_DEV):
        send[target, :, :ROWS] = total
        tile = jnp.where(target == (lon + 1) % LON_DEV, tiles[0], tiles[1])
        send[target, :, ROWS:MORE] = tile[:, :64]
        send[target, :, MORE:] = received[(target + LON_DEV // 2) % LON_DEV, :, MORE:]


def second_respond_kernel(received, cutoff_in, send, edges, cutoff, sems):
    _, lat = place()
    finish(*begin(sems, (cutoff_in, cutoff)))
    total = responded(received, cutoff, edges)
    near = row_waves(total, jnp.where(lat == TOP, 0, BAND - 1))
    for target in range(LON_DEV):
        send[target, :, :ROWS] = total
        send[target, :, ROWS:] = near[:, :64]


def gather_terms(value, coeff, south_line, north_line, west_edge, east_edge):
    to_north, to_south = coeff[1] * value, coeff[2] * value
    total = coeff[0] * value
    total = total + jnp.concatenate([south_line, to_north[:-1]], axis=0)
    total = total + jnp.concatenate([to_south[1:], north_line], axis=0)
    total = total + jnp.concatenate([west_edge, (coeff[3] * value)[:, :-1]], axis=1)
    total = total + jnp.concatenate([(coeff[4] * value)[:, 1:], east_edge], axis=1)
    return total, to_north, to_south


def load_coeff(coeff, field, level):
    return [coeff[field, term, level] for term in range(5)]


def row_waves(waves, row):
    picked = iota((ROWS, 128), 0) == iota((ROWS, 128), 1) * BAND + row
    picked = picked.astype(jnp.float32).astype(jnp.bfloat16)
    high, low = split(waves)
    return pair_dot(high, picked, 1, 0) + pair_dot(low, picked, 1, 0)


def across_pole(waves, table, row):
    chosen = row_waves(waves, row)
    chosen = jnp.where(iota((WAVES, 128), 0) % 2 == 1, -chosen, chosen)
    return dot(chosen, table, 0, 0)


def whole_band(closed, opened, top):
    return jnp.where(
        top, jnp.concatenate([opened, closed], axis=0), jnp.concatenate([closed, opened], axis=0)
    )


def middle_kernel(
    waves_in, table_in, mask_in, state_in, extra_in, coeff_in, opened_in, beyond_in,
    send, to_next, next_line, edges, across, middle_out,
    waves, table, mask, state, extra, coeff_ref, opened, beyond, middle,
    filtered, opposite, halos, ends, sems,
):
    lon, lat = place()
    top = lat == TOP
    waves_copy, table_copy, *rest = begin(
        sems,
        (waves_in, waves),
        (table_in.at[lon], table),
        (mask_in, mask),
        (opened_in, opened),
        (beyond_in, beyond),
        *by_field((state_in, state), (extra_in, extra), (coeff_in, coeff_ref)),
    )
    rest, fields = rest[:3], rest[3:]
    finish(waves_copy, table_copy)
    for tile in range(TILED):
        across[tile_place(tile)] = waves[tile, :, MORE:]
    flat = waves[:, :, :ROWS].reshape(WAVES, ROWS)
    filtered[...] = dot(flat, table[...], 0, 0)
    polar_row = jnp.where(top, BAND - 1, 0)
    opposite[...] = across_pole(flat, table[...], polar_row)
    finish(*rest)
    blank = jnp.zeros((HALF, 64), jnp.float32)
    sides = (lon + LON_DEV - 1) % LON_DEV, (lon + 1) % LON_DEV
    for side in range(2):
        closed = jnp.concatenate([waves[sides[side], :, ROWS:MORE], blank], axis=1)
        edges[side] = whole_band(closed, opened[side], top)
    weight = row_weight(mask, 0, (BAND, WIDTH))
    narrow = row_weight(mask, 0, (BAND, 128))
    for side, lane in enumerate((WIDTH + 1 - LAST, WIDTH - LAST)):
        halos[side] = halo_of(edges[side], filtered[:, LAST:], lane, narrow)
    next_weight = jnp.where(top, weight[0:1], weight[BAND - 1 :])
    row = iota((BAND, WIDTH), 0)

    def one(field, level, carry):
        slab = field * LEV + level
        here = pl.ds(slab, 1)
        value = state[field, level]
        smooth = filtered[pl.ds(slab * BAND, BAND)]
        value = value + weight * (smooth[:, :WIDTH] - value)
        coeff = load_coeff(coeff_ref, field, level)
        band = pl.ds(slab * BAND, BAND)
        west, east = halos[0, band, 0:1], halos[1, band, 0:1]
        halo = beyond[2, here]
        total, north, south = gather_terms(
            value, coeff, jnp.where(top, halo, 0.0), jnp.where(top, 0.0, halo), west, east
        )
        pole = (across[here] * opposite[here])[:, :WIDTH]
        total = total + jnp.where(row == polar_row, pole, 0.0) + extra[field, level]
        middle[field, level] = total
        product = jnp.where(top, south[0:1], north[BAND - 1 :])
        near = jnp.where(top, total[0:1], total[BAND - 1 :])
        near_coeff = jnp.where(top, coeff[2][0:1], coeff[1][BAND - 1 :])
        to_next[0, here] = product
        to_next[1, here] = (1.0 - next_weight) * near_coeff * near
        to_next[2, here] = next_weight * near_coeff
        next_line[here] = beyond[1, here] * (beyond[0, here] + product)
        ends[0, band, : WIDTH - LAST] = (coeff[3] * total)[:, LAST:]
        ends[1, band] = (coeff[4] * total)[:, :128]
        return carry

    stored = []
    for field in range(FIELDS):
        finish(*fields[3 * field : 3 * field + 3])
        for_levels(field, one)
        stored += begin(sems.at[field : field + 1], (middle.at[field], middle_out.at[field]))
    sums = dot(table[:, :WIDTH], middle[...].reshape(ROWS, WIDTH), 1, 1)
    send[:, :, :ROWS] = sums.reshape(LON_DEV, SHARE, ROWS)
    east_tile = tile_of(ends[0, :, : WIDTH - LAST], WIDTH - LAST - 1, BAND, open_row(lat))
    west_tile = tile_of(ends[1], 0, BAND, open_row(lat))
    for target in range(LON_DEV):
        tile = jnp.where(target == (lon + 1) % LON_DEV, east_tile, west_tile)
        send[target, :, ROWS:] = tile[:, :64]
    finish(*stored)


def final_kernel(
    waves_in, table_in, mask_in, middle_in, coeff_in, edges_in, opened_in, line_in, across_in,
    out,
    waves, table, mask, middle, coeff_ref, edges, opened, next_line, across, result,
    filtered, opposite, halos, sems,
):
    lon, lat = place()
    top = lat == TOP
    waves_copy, table_copy, *rest = begin(
        sems,
        (waves_in, waves),
        (table_in.at[lon], table),
        (mask_in, mask),
        (edges_in, edges),
        (opened_in, opened),
        (line_in, next_line),
        (across_in, across),
        *by_field((middle_in, middle), (coeff_in, coeff_ref)),
    )
    rest, fields = rest[:5], rest[5:]
    finish(waves_copy, table_copy)
    flat = waves[:, :, :ROWS].reshape(WAVES, ROWS)
    filtered[...] = dot(flat, table[...], 0, 0)
    polar_row = jnp.where(top, BAND - 1, 0)
    opposite[...] = across_pole(flat, table[...], polar_row)
    finish(*rest)
    weight = row_weight(mask, 0, (BAND, WIDTH))
    row = iota((BAND, WIDTH), 0)
    none = jnp.zeros((HALF, 128), jnp.float32)
    narrow = row_weight(mask, 0, (BAND, 128))
    for side, lane in enumerate((WIDTH + 1 - LAST, WIDTH - LAST)):
        tile = jnp.where(narrow > 0.5, edges[side], whole_band(none, opened[side], top))
        halos[side] = halo_of(tile, filtered[:, LAST:], lane, narrow)

    def one(field, level, carry):
        slab = field * LEV + level
        here = pl.ds(slab, 1)
        value = middle[field, level]
        smooth = filtered[pl.ds(slab * BAND, BAND)]
        value = value + weight * (smooth[:, :WIDTH] - value)
        coeff = load_coeff(coeff_ref, field, level)
        band = pl.ds(slab * BAND, BAND)
        west, east = halos[0, band, 0:1], halos[1, band, 0:1]
        halo = next_line[here]
        total, _, _ = gather_terms(
            value, coeff, jnp.where(top, halo, 0.0), jnp.where(top, 0.0, halo), west, east
        )
        pole = (across[here] * opposite[here])[:, :WIDTH]
        result[field, level] = total + jnp.where(row == polar_row, pole, 0.0)
        return carry

    stored = []
    for field in range(FIELDS):
        finish(*fields[2 * field : 2 * field + 2])
        for_levels(field, one)
        stored += begin(sems.at[field : field + 1], (result.at[field], out.at[field]))
    finish(*stored)


def edge_kernel(field_in, coeff_in, edges, field, to_east, to_west, sems):
    finish(
        *begin(
            sems,
            (field_in, field),
            (coeff_in.at[:, 3], to_east),
            (coeff_in.at[:, 4], to_west),
        )
    )
    east = west = jnp.zeros((BAND, 128), jnp.float32)
    for slab in range(SLABS):
        at = slab // LEV, slab % LEV
        value = field[at]
        east = with_lane(east, slab, (to_east[at] * value)[:, WIDTH - 1 :])
        west = with_lane(west, slab, (to_west[at] * value)[:, 0:1])
    edges[0] = east
    edges[1] = west


def line_kernel(
    field_in, extra_in, coeff_in, west_in, east_in,
    to_north, to_south, to_polar,
    field_ref, extra, coeff_ref, west_edge, east_edge, sems,
):
    _, lat = place()
    finish(
        *begin(
            sems,
            (field_in, field_ref),
            (extra_in, extra),
            (coeff_in, coeff_ref),
            (west_in, west_edge),
            (east_in, east_edge),
        )
    )
    none = jnp.zeros((1, WIDTH), jnp.float32)

    def one(field, level, carry):
        slab = field * LEV + level
        here = pl.ds(slab, 1)
        coeff = load_coeff(coeff_ref, field, level)
        west, east = lane_of(west_edge[...], slab), lane_of(east_edge[...], slab)
        total, north, south = gather_terms(field_ref[field, level], coeff, none, none, west, east)
        total = total + extra[field, level]
        norths = total[BAND - 1 :], coeff[1][BAND - 1 :], north[BAND - 1 :]
        souths = total[0:1], coeff[2][0:1], south[0:1]
        for part in range(3):
            to_north[part, here] = norths[part]
            to_south[part, here] = souths[part]
            to_polar[part, here] = jnp.where(lat == 1, souths[part], norths[part])
        return carry

    for_slabs(one)


def plain_middle_kernel(
    state_in, extra_in, coeff_in, west_in, east_in, below_in, above_in, polar_in,
    edges, lines, middle_out,
    state, extra, coeff_ref, west_edge, east_edge, below, above, polar, middle, sems,
):
    _, lat = place()
    finish(
        *begin(
            sems,
            (state_in, state),
            (extra_in, extra),
            (coeff_in, coeff_ref),
            (west_in, west_edge),
            (east_in, east_edge),
            (below_in, below),
            (above_in, above),
            (polar_in, polar),
        )
    )

    def one(field, level, carry):
        east_tile, west_tile = carry
        slab = field * LEV + level
        here = pl.ds(slab, 1)
        coeff = load_coeff(coeff_ref, field, level)
        west, east = lane_of(west_edge[...], slab), lane_of(east_edge[...], slab)
        reached = polar[0, here]
        total, north, south = gather_terms(
            state[field, level],
            coeff,
            jnp.where(lat == 1, reached, below[2, here]),
            jnp.where(lat == TOP - 1, reached, above[2, here]),
            west,
            east,
        )
        total = total + extra[field, level]
        middle[field, level] = total
        low = below[1, here] * (below[0, here] + south[0:1])
        high = above[1, here] * (above[0, here] + north[BAND - 1 :])
        lines[0, here] = jnp.where(lat == 1, 0.0, low)
        lines[1, here] = jnp.where(lat == TOP - 1, 0.0, high)
        east_tile = with_lane(east_tile, slab, (coeff[3] * total)[:, WIDTH - 1 :])
        west_tile = with_lane(west_tile, slab, (coeff[4] * total)[:, 0:1])
        return east_tile, west_tile

    none = jnp.zeros((BAND, 128), jnp.float32)
    edges[0], edges[1] = for_slabs(one, (none, none))
    finish(*begin(sems, (middle, middle_out)))


def plain_final_kernel(
    middle_in, coeff_in, west_in, east_in, lines_in,
    out,
    middle, coeff_ref, west_edge, east_edge, lines, sems,
):
    finish(
        *begin(
            sems,
            (middle_in, middle),
            (coeff_in, coeff_ref),
            (west_in, west_edge),
            (east_in, east_edge),
            (lines_in, lines),
        )
    )

    def one(field, level, carry):
        slab = field * LEV + level
        here = pl.ds(slab, 1)
        coeff = load_coeff(coeff_ref, field, level)
        west, east = lane_of(west_edge[...], slab), lane_of(east_edge[...], slab)
        value = middle[field, level]
        out[field, level] = gather_terms(value, coeff, lines[0, here], lines[1, here], west, east)[0]
        return carry

    for_slabs(one)


def reach_kernel(result_in, waves_in, table_in, polar_in, result_out, part, waves, table, polar, sems):
    lon, lat = place()
    next_to = (lat == 1) | (lat == TOP - 1)
    bottom = lat == 1
    rows = pl.ds(pl.multiple_of(jnp.where(bottom, 0, HALF), HALF), HALF)

    @pl.when(next_to)
    def _():
        finish(
            *begin(
                sems,
                (result_in.at[:, :, rows], part),
                (waves_in, waves),
                (table_in.at[lon], table),
                (polar_in, polar),
            )
        )
        smooth = dot(waves[...].reshape(WAVES, 128), table[...], 0, 0)
        line = polar[1] + polar[2] * smooth[64 : 64 + SLABS, :WIDTH]
        row = iota((HALF, WIDTH), 0)
        mine = row == jnp.where(bottom, 0, HALF - 1)
        for slab in range(SLABS):
            at = slab // LEV, slab % LEV
            part[at] = part[at] + jnp.where(mine, line[slab : slab + 1], 0.0)
        finish(*begin(sems, (part, result_out.at[:, :, rows])))


def exchanged(chunks):
    return lax.all_to_all(chunks, "lon", split_axis=0, concat_axis=0, tiled=True)


def moved(value, lats, north, east):
    pairs = []
    for lat, lon in [(lat, lon) for lat in lats for lon in range(LON_DEV)]:
        pairs.append((lat * LON_DEV + lon, (lat + north) * LON_DEV + (lon + east) % LON_DEV))
    return lax.ppermute(value, ("lat", "lon"), pairs)


def next_to_pole(value, outward):
    pairs = []
    for lon in range(LON_DEV):
        for polar, other in ((0, 1), (TOP, TOP - 1)):
            pair = polar * LON_DEV + lon, other * LON_DEV + lon
            pairs.append(pair if outward else pair[::-1])
    return lax.ppermute(value, ("lat", "lon"), pairs)


def local(adjoint_state, innovation, coefficients, polar_mask, wave_cutoff):
    lat = lax.axis_index("lat")
    polar = (lat == 0) | (lat == TOP)
    table = jnp.asarray(wave_tables())
    small = pltpu.SMEM((BAND,), jnp.int32)
    plain = range(1, TOP)
    table_scratch = in_vmem((WAVES, WIDE))
    halo_scratch = in_vmem((2, ROWS, 128))
    wave_scratch = [in_vmem((ROWS, WIDE)), in_vmem((128, WIDE)), halo_scratch]
    one_edge = (BAND, 128)

    def blanks(*shapes):
        return tuple(jnp.zeros(shape, jnp.float32) for shape in shapes)

    def polar_first():
        half = in_vmem(HALF_FIELD)
        send, to_polar, to_north, to_south, edge = launch(
            forward_kernel_with_blanks,
            [adjoint_state, coefficients, table, polar_mask],
            [FIRST_CHUNKS],
            [LINES, LINES, LINES, (2, *one_edge)],
            [in_vmem(FIELD), table_scratch, half, half, half, in_vmem(ACROSS), small],
            copies=6,
        )
        received = exchanged(send)
        (tiles,) = launch(closed_kernel, [coefficients], [TILES], (), [half, half], copies=2)
        send, opened = launch(
            first_respond_kernel,
            [received, wave_cutoff, tiles],
            [FIRST_CHUNKS, TILES],
            (),
            [small, in_vmem(TILES)],
            copies=2,
            near=1,
        )
        return send, opened, to_polar, to_north, to_south, edge

    def plain_first():
        (edges,) = launch(
            edge_kernel,
            [adjoint_state, coefficients],
            [(2, *one_edge)],
            (),
            [in_vmem(FIELD)] * 3,
            copies=3,
        )
        west = moved(edges[0], plain, 0, 1)
        east = moved(edges[1], plain, 0, -1)
        to_north, to_south, to_polar = launch(
            line_kernel,
            [adjoint_state, innovation, coefficients, west, east],
            [LINES, LINES, LINES],
            (),
            [in_vmem(FIELD), in_vmem(FIELD), in_vmem(COEFF), in_vmem(one_edge), in_vmem(one_edge)],
            copies=5,
        )
        send, opened = blanks(FIRST_CHUNKS, TILES)
        return send, opened, to_polar, to_north, to_south, jnp.stack([west, east])

    send, opened, to_polar, to_north, to_south, edge = lax.cond(polar, polar_first, plain_first)
    beyond = next_to_pole(to_polar, False)

    def polar_second():
        return exchanged(send), to_north, to_south

    def plain_second():
        below = moved(to_north, range(1, TOP - 1), 1, 0)
        above = moved(to_south, range(2, TOP), -1, 0)
        return *blanks(FIRST_CHUNKS), below, above

    waves, below, above = lax.cond(polar, polar_second, plain_second)

    def polar_third():
        return tuple(launch(
            middle_kernel,
            [waves, table, polar_mask, adjoint_state, innovation, coefficients, opened, beyond],
            [CHUNKS, LINES, LINE, EDGES, ACROSS],
            [FIELD],
            [in_vmem(FIRST_CHUNKS), table_scratch, small, in_vmem(FIELD), in_vmem(FIELD), in_vmem(COEFF)]
            + [in_vmem(TILES), in_vmem(LINES), in_vmem(FIELD), *wave_scratch, halo_scratch],
            copies=14,
        ))

    def plain_third():
        return blanks(CHUNKS, LINES, LINE, EDGES, ACROSS, FIELD)

    send, to_next, next_line, edges, across, middle = lax.cond(polar, polar_third, plain_third)
    reached = next_to_pole(to_next, True)

    def polar_fourth():
        received = exchanged(send)
        again, opened, result = launch(
            second_respond_kernel_with_blank,
            [received, wave_cutoff],
            [CHUNKS, TILES],
            [FIELD],
            [small],
            copies=1,
            near=1,
        )
        waves = exchanged(again)
        return waves, lax.slice_in_dim(waves, MORE - 128, MORE, axis=2), opened, result

    def plain_fourth():
        west, east = edge[0], edge[1]
        second, lines, middle = launch(
            plain_middle_kernel,
            [adjoint_state, innovation, coefficients, west, east, below, above, reached],
            [(2, *one_edge), (2, *LINE)],
            [FIELD],
            [in_vmem(FIELD), in_vmem(FIELD), in_vmem(COEFF), in_vmem(one_edge), in_vmem(one_edge)]
            + [in_vmem(LINES), in_vmem(LINES), in_vmem(LINES), in_vmem(FIELD)],
            copies=8,
        )
        west = moved(second[0], plain, 0, 1)
        east = moved(second[1], plain, 0, -1)
        (result,) = launch(
            plain_final_kernel,
            [middle, coefficients, west, east, lines],
            [FIELD],
            (),
            [in_vmem(FIELD), in_vmem(COEFF), in_vmem(one_edge), in_vmem(one_edge), in_vmem((2, *LINE))],
            copies=5,
        )
        return *blanks(CHUNKS, LAST_TILE, TILES), result

    waves, near_waves, opened, result = lax.cond(polar, polar_fourth, plain_fourth)
    waves_beyond = next_to_pole(near_waves, True)

    def polar_fifth():
        (out,) = launch(
            final_kernel,
            [waves, table, polar_mask, middle, coefficients, edges, opened, next_line, across],
            (),
            [FIELD],
            [in_vmem(CHUNKS), table_scratch, small, in_vmem(FIELD), in_vmem(COEFF), in_vmem(EDGES)]
            + [in_vmem(TILES), in_vmem(LINE), in_vmem(ACROSS), in_vmem(FIELD), *wave_scratch],
            copies=13,
            pinned=True,
        )
        return out

    result = lax.cond(polar, polar_fifth, lambda kept=result: kept)
    (out,) = launch(
        reach_kernel,
        [result, waves_beyond, table, reached],
        (),
        [FIELD],
        [in_vmem(HALF_FIELD), in_vmem(LAST_TILE), table_scratch, in_vmem(LINES)],
        copies=4,
        aliases={0: 0},
        pinned=True,
    )
    return out


def forward_kernel_with_blanks(*refs):
    forward_kernel(*refs[:5], *refs[9:])


def second_respond_kernel_with_blank(*refs):
    second_respond_kernel(*refs[:4], *refs[5:])


def solution(mesh):
    return jax.shard_map(
        local,
        mesh=mesh,
        in_specs=(
            P(None, None, "lat", "lon"),
            P(None, None, "lat", "lon"),
            P(None, None, None, "lat", "lon"),
            P("lat"),
            P("lat"),
        ),
        out_specs=P(None, None, "lat", "lon"),
        check_vma=False,
    )
```

```python
import math

import jax
import jax.numpy as jnp
import numpy as np
from jax import lax
from jax.experimental import pallas as pl
from jax.experimental.pallas import tpu as pltpu
from jax.sharding import PartitionSpec as P

NLON = 5760
KMAX = 64
WAVES = 2 * KMAX
FIELDS = 3
LEV = 12
BAND = 16
HALF = BAND // 2
LON_DEV = 16
LAT_DEV = 16
TOP = LAT_DEV - 1
WIDTH = NLON // LON_DEV
WIDE = 384
LAST = (WIDTH - 1) // 128 * 128
SLABS = FIELDS * LEV
ROWS = SLABS * BAND
SHARE = WAVES // LON_DEV
UNROLL = 6

FIELD = (FIELDS, LEV, BAND, WIDTH)
HALF_FIELD = (FIELDS, LEV, HALF, WIDTH)
COEFF = (FIELDS, 5, LEV, BAND, WIDTH)
MORE = ROWS + 64
CHUNKS = (LON_DEV, SHARE, MORE)
FIRST_CHUNKS = (LON_DEV, SHARE, MORE + 128)
LAST_TILE = (LON_DEV, SHARE, 128)
LINE = (SLABS, WIDTH)
ACROSS = (40, WIDE)
LINES = (3, SLABS, WIDTH)
TILES = (2, HALF, 128)
EDGES = (2, BAND, 128)


def wave_tables():
    columns = np.concatenate([np.arange(WIDTH), [WIDTH, -1]])
    phases = (np.arange(LON_DEV)[:, None] * WIDTH + columns[None, :]) % NLON
    phases = phases[:, None, :] * np.arange(KMAX)[None, :, None] % NLON
    radians = phases * (2.0 * math.pi / NLON)
    both = np.concatenate([np.cos(radians), np.sin(radians)], axis=1)
    return np.pad(both, ((0, 0), (0, 0), (0, WIDE - WIDTH - 2))).astype(np.float32)


def split(value):
    high = value.astype(jnp.bfloat16)
    return high, (value - high.astype(jnp.float32)).astype(jnp.bfloat16)


def pair_dot(left, right, left_dim, right_dim):
    return lax.dot_general(
        left, right, (((left_dim,), (right_dim,)), ((), ())), preferred_element_type=jnp.float32
    )


def dot(left, right, left_dim, right_dim):
    (left_high, left_low), (right_high, right_low) = split(left), split(right)
    total = pair_dot(left_high, right_low, left_dim, right_dim)
    total = total + pair_dot(left_low, right_high, left_dim, right_dim)
    return total + pair_dot(left_high, right_high, left_dim, right_dim)


def iota(shape, dim):
    return lax.broadcasted_iota(jnp.int32, shape, dim)


def in_vmem(shape):
    return pltpu.VMEM(shape, jnp.float32)


def launch(kernel, operands, outs, far_outs=(), scratch=(), copies=0, aliases=None, near=0, pinned=False):
    shapes = [*outs, *far_outs]
    nbytes = sum(4 * math.prod(shape) for shape in shapes)
    nbytes += sum(4 * math.prod(operand.shape) for operand in operands)
    return pl.pallas_call(
        kernel,
        in_specs=[pl.BlockSpec(memory_space=pltpu.VMEM)] * near
        + [pl.BlockSpec(memory_space=pltpu.HBM)] * (len(operands) - near),
        out_specs=[pl.BlockSpec(memory_space=pltpu.VMEM)] * len(outs)
        + [pl.BlockSpec(memory_space=pltpu.HBM)] * len(far_outs),
        out_shape=[
            (pltpu.HBM if pinned else jax.ShapeDtypeStruct)(shape, jnp.float32) for shape in shapes
        ],
        scratch_shapes=[*scratch, pltpu.SemaphoreType.DMA((copies,))],
        input_output_aliases=aliases or {},
        compiler_params=pltpu.CompilerParams(vmem_limit_bytes=24 * 2**20),
        cost_estimate=pl.CostEstimate(flops=0, bytes_accessed=nbytes, transcendentals=0),
    )(*operands)


def begin(sems, *pairs):
    started = []
    for index, (source, target) in enumerate(pairs):
        copy = pltpu.make_async_copy(source, target, sems.at[index])
        copy.start()
        started.append(copy)
    return started


def by_field(*pairs):
    return [(source.at[field], target.at[field]) for field in range(FIELDS) for source, target in pairs]


def finish(*started):
    for copy in started:
        copy.wait()


def for_levels(field, one, carry=0):
    def some(step, carry):
        for level in range(UNROLL):
            carry = one(field, step * UNROLL + level, carry)
        return carry

    return lax.fori_loop(0, LEV // UNROLL, some, carry)


def for_slabs(one, carry=0):
    for field in range(FIELDS):
        carry = for_levels(field, one, carry)
    return carry


def lane_of(tile, slab):
    return jnp.sum(jnp.where(iota(tile.shape, 1) == slab, tile, 0.0), axis=1, keepdims=True)


def with_lane(tile, slab, column):
    return jnp.where(iota(tile.shape, 1) == slab, column, tile)


def exact_dot(value, chosen, left_dim=1, right_dim=0):
    high, low = split(value)
    chosen = chosen.astype(jnp.float32).astype(jnp.bfloat16)
    return pair_dot(high, chosen, left_dim, right_dim) + pair_dot(low, chosen, left_dim, right_dim)


def every_lane(values, lane):
    return exact_dot(values, iota((values.shape[1], 128), 0) == lane)


def own_lane(rows):
    shape = (SLABS * rows, 128)
    return iota(shape, 0) // rows == iota(shape, 1)


def tile_of(values, lane, rows, first):
    spread = jnp.where(own_lane(rows), every_lane(values, lane), 0.0)
    shape = (HALF, SLABS * rows)
    picked = iota(shape, 1) % rows == iota(shape, 0) + first
    picked = picked.astype(jnp.float32).astype(jnp.bfloat16)
    high, low = split(spread)
    return pair_dot(picked, high, 1, 0) + pair_dot(picked, low, 1, 0)


def halo_of(tile, wave_lanes, lane, weight):
    tall = jnp.concatenate([tile] * SLABS, axis=0)
    spread = exact_dot(jnp.where(own_lane(BAND), tall, 0.0), iota((128, 128), 0) >= 0)
    filtered = jnp.concatenate([weight] * SLABS, axis=0) > 0.5
    return spread * jnp.where(filtered, every_lane(wave_lanes, lane), 1.0)


def place():
    return lax.axis_index("lon"), lax.axis_index("lat")


def open_row(lat):
    return pl.multiple_of(jnp.where(lat == TOP, 0, HALF), HALF)


def row_weight(mask, first, shape):
    row = iota(shape, 0)
    weight = jnp.zeros(shape, jnp.float32)
    for r in range(shape[0]):
        weight = jnp.where(row == r, mask[first + r].astype(jnp.float32), weight)
    return weight


TILED = ACROSS[0] // 8 * (WIDE // 128)


def tile_place(index):
    row, column = index // (WIDE // 128), index % (WIDE // 128)
    return slice(8 * row, 8 * row + 8), slice(128 * column, 128 * column + 128)


def forward_kernel(
    field_in, coeff_in, table_in, mask_in,
    send,
    field, table, to_east, to_west, pole, across, mask, sems,
):
    lon, lat = place()
    top = lat == TOP
    first = open_row(lat)
    rows = pl.ds(first, HALF)
    closed = pl.ds(pl.multiple_of(HALF - first, HALF), HALF)
    field_copy, table_copy, *rest = begin(
        sems,
        (field_in, field),
        (table_in.at[lon], table),
        (coeff_in.at[:, 3, :, rows], to_east),
        (coeff_in.at[:, 4, :, rows], to_west),
        (mask_in, mask),
        (coeff_in.at[:, jnp.where(top, 1, 2), :, closed], pole),
    )
    across[...] = jnp.zeros(ACROSS, jnp.float32)
    finish(field_copy, table_copy)
    waves = dot(table[:, :WIDTH], field[...].reshape(ROWS, WIDTH), 1, 1)
    send[:, :, :ROWS] = waves.reshape(LON_DEV, SHARE, ROWS)
    finish(*rest)
    filtered = row_weight(mask, first, (HALF, 1)) > 0.5
    east = west = jnp.zeros((HALF, 128), jnp.float32)
    for slab in range(SLABS):
        at = slab // LEV, slab % LEV
        value = field[*at, rows]
        coeff = to_east[at][:, WIDTH - 1 :]
        east = with_lane(east, slab, jnp.where(filtered, coeff, coeff * value[:, WIDTH - 1 :]))
        coeff = to_west[at][:, 0:1]
        west = with_lane(west, slab, jnp.where(filtered, coeff, coeff * value[:, 0:1]))
        sign = 1.0 if at[0] == FIELDS - 1 else -1.0
        lines = pole[at]
        line = jnp.where(top, lines[HALF - 1 :], lines[0:1])
        across[slab : slab + 1, :WIDTH] = sign * line
    for target in range(LON_DEV):
        tile = jnp.where(target == (lon + 1) % LON_DEV, east, west)
        send[target, :, ROWS:MORE] = tile[:, :64]
        send[target, :, MORE:] = across[tile_place(target)] if target < TILED else tile


def closed_kernel(coeff_in, tiles, to_east, to_west, sems):
    _, lat = place()
    closed = pl.ds(pl.multiple_of(HALF - open_row(lat), HALF), HALF)
    finish(
        *begin(
            sems,
            (coeff_in.at[:, 3, :, closed], to_east),
            (coeff_in.at[:, 4, :, closed], to_west),
        )
    )
    east = west = jnp.zeros((HALF, 128), jnp.float32)
    for slab in range(SLABS):
        at = slab // LEV, slab % LEV
        east = with_lane(east, slab, to_east[at][:, WIDTH - 1 :])
        west = with_lane(west, slab, to_west[at][:, 0:1])
    tiles[0] = east
    tiles[1] = west


def responded(received, cutoff, edges):
    lon, _ = place()
    shape = (SHARE, ROWS)
    wave = (lon * SHARE + iota(shape, 0)) % KMAX
    row = iota(shape, 1) % BAND
    limit = jnp.zeros(shape, jnp.int32)
    for r in range(BAND):
        limit = jnp.where(row == r, cutoff[r], limit)
    ratio = limit.astype(jnp.float32) / jnp.maximum(wave, 1).astype(jnp.float32)
    response = jnp.where(wave <= limit, 1.0, ratio * ratio)
    response = response * jnp.where(wave == 0, 1.0 / NLON, 2.0 / NLON)
    total = received[0, :, :ROWS]
    for source in range(1, LON_DEV):
        total = total + received[source, :, :ROWS]
    blank = jnp.zeros((HALF, 64), jnp.float32)
    west = received[(lon + LON_DEV - 1) % LON_DEV, :, ROWS:MORE]
    east = received[(lon + 1) % LON_DEV, :, ROWS:MORE]
    edges[0] = jnp.concatenate([west, blank], axis=1)
    edges[1] = jnp.concatenate([east, blank], axis=1)
    return total * response


def first_respond_kernel(received, tiles, cutoff_in, send, edges, cutoff, sems):
    lon, _ = place()
    finish(*begin(sems, (cutoff_in, cutoff)))
    total = responded(received, cutoff, edges)
    for target in range(LON_DEV):
        send[target, :, :ROWS] = total
        tile = jnp.where(target == (lon + 1) % LON_DEV, tiles[0], tiles[1])
        send[target, :, ROWS:MORE] = tile[:, :64]
        send[target, :, MORE:] = received[(target + LON_DEV // 2) % LON_DEV, :, MORE:]


def second_respond_kernel(received, cutoff_in, mask_in, send, edges, cutoff, mask, sems):
    _, lat = place()
    finish(*begin(sems, (cutoff_in, cutoff), (mask_in, mask)))
    total = responded(received, cutoff, edges)
    near_row = jnp.where(lat == TOP, 0, BAND - 1)
    near = row_waves(total, near_row)
    near = with_lane(near, SLABS, mask[near_row].astype(jnp.float32))
    for target in range(LON_DEV):
        send[target, :, :ROWS] = total
        send[target, :, ROWS:] = near[:, :64]


def gather_terms(value, coeff, south_line, north_line, west_edge, east_edge):
    to_north, to_south = coeff[1] * value, coeff[2] * value
    total = coeff[0] * value
    total = total + jnp.concatenate([south_line, to_north[:-1]], axis=0)
    total = total + jnp.concatenate([to_south[1:], north_line], axis=0)
    total = total + jnp.concatenate([west_edge, (coeff[3] * value)[:, :-1]], axis=1)
    total = total + jnp.concatenate([(coeff[4] * value)[:, 1:], east_edge], axis=1)
    return total, to_north, to_south


def load_coeff(coeff, field, level):
    return [coeff[field, term, level] for term in range(5)]


def row_waves(waves, row):
    picked = iota((ROWS, 128), 0) == iota((ROWS, 128), 1) * BAND + row
    picked = picked.astype(jnp.float32).astype(jnp.bfloat16)
    high, low = split(waves)
    return pair_dot(high, picked, 1, 0) + pair_dot(low, picked, 1, 0)


def across_pole(waves, table, row):
    chosen = row_waves(waves, row)
    chosen = jnp.where(iota((WAVES, 128), 0) % 2 == 1, -chosen, chosen)
    return dot(chosen, table, 0, 0)


def whole_band(closed, opened, top):
    return jnp.where(
        top, jnp.concatenate([opened, closed], axis=0), jnp.concatenate([closed, opened], axis=0)
    )


def middle_kernel(
    waves_in, table_in, mask_in, state_in, extra_in, coeff_in, opened_in, beyond_in,
    send, to_next, next_line, edges, across, middle_out,
    waves, table, mask, state, extra, coeff_ref, opened, beyond, middle,
    filtered, opposite, halos, ends, sems,
):
    lon, lat = place()
    top = lat == TOP
    waves_copy, table_copy, *rest = begin(
        sems,
        (waves_in, waves),
        (table_in.at[lon], table),
        (mask_in, mask),
        (opened_in, opened),
        (beyond_in, beyond),
        *by_field((state_in, state), (extra_in, extra), (coeff_in, coeff_ref)),
    )
    rest, fields = rest[:3], rest[3:]
    finish(waves_copy, table_copy)
    for tile in range(TILED):
        across[tile_place(tile)] = waves[tile, :, MORE:]
    flat = waves[:, :, :ROWS].reshape(WAVES, ROWS)
    filtered[...] = dot(flat, table[...], 0, 0)
    polar_row = jnp.where(top, BAND - 1, 0)
    opposite[...] = across_pole(flat, table[...], polar_row)
    finish(*rest)
    blank = jnp.zeros((HALF, 64), jnp.float32)
    sides = (lon + LON_DEV - 1) % LON_DEV, (lon + 1) % LON_DEV
    for side in range(2):
        closed = jnp.concatenate([waves[sides[side], :, ROWS:MORE], blank], axis=1)
        edges[side] = whole_band(closed, opened[side], top)
    weight = row_weight(mask, 0, (BAND, WIDTH))
    narrow = row_weight(mask, 0, (BAND, 128))
    for side, lane in enumerate((WIDTH + 1 - LAST, WIDTH - LAST)):
        halos[side] = halo_of(edges[side], filtered[:, LAST:], lane, narrow)
    next_weight = jnp.where(top, weight[0:1], weight[BAND - 1 :])
    row = iota((BAND, WIDTH), 0)

    def one(field, level, carry):
        slab = field * LEV + level
        here = pl.ds(slab, 1)
        value = state[field, level]
        smooth = filtered[pl.ds(slab * BAND, BAND)]
        value = value + weight * (smooth[:, :WIDTH] - value)
        coeff = load_coeff(coeff_ref, field, level)
        band = pl.ds(slab * BAND, BAND)
        west, east = halos[0, band, 0:1], halos[1, band, 0:1]
        halo = beyond[2, here]
        total, north, south = gather_terms(
            value, coeff, jnp.where(top, halo, 0.0), jnp.where(top, 0.0, halo), west, east
        )
        pole = (across[here] * opposite[here])[:, :WIDTH]
        total = total + jnp.where(row == polar_row, pole, 0.0) + extra[field, level]
        middle[field, level] = total
        product = jnp.where(top, south[0:1], north[BAND - 1 :])
        near = jnp.where(top, total[0:1], total[BAND - 1 :])
        near_coeff = jnp.where(top, coeff[2][0:1], coeff[1][BAND - 1 :])
        to_next[0, here] = product
        to_next[1, here] = jnp.where(next_weight > 0.5, near_coeff, near_coeff * near)
        next_line[here] = beyond[1, here] * (beyond[0, here] + product)
        ends[0, band, : WIDTH - LAST] = (coeff[3] * total)[:, LAST:]
        ends[1, band] = (coeff[4] * total)[:, :128]
        return carry

    stored = []
    for field in range(FIELDS):
        finish(*fields[3 * field : 3 * field + 3])
        for_levels(field, one)
        stored += begin(sems.at[field : field + 1], (middle.at[field], middle_out.at[field]))
    sums = dot(table[:, :WIDTH], middle[...].reshape(ROWS, WIDTH), 1, 1)
    send[:, :, :ROWS] = sums.reshape(LON_DEV, SHARE, ROWS)
    east_tile = tile_of(ends[0, :, : WIDTH - LAST], WIDTH - LAST - 1, BAND, open_row(lat))
    west_tile = tile_of(ends[1], 0, BAND, open_row(lat))
    for target in range(LON_DEV):
        tile = jnp.where(target == (lon + 1) % LON_DEV, east_tile, west_tile)
        send[target, :, ROWS:] = tile[:, :64]
    finish(*stored)


def final_kernel(
    waves_in, table_in, mask_in, middle_in, coeff_in, edges_in, opened_in, line_in, across_in,
    out,
    waves, table, mask, middle, coeff_ref, edges, opened, next_line, across, result,
    filtered, opposite, halos, sems,
):
    lon, lat = place()
    top = lat == TOP
    waves_copy, table_copy, *rest = begin(
        sems,
        (waves_in, waves),
        (table_in.at[lon], table),
        (mask_in, mask),
        (edges_in, edges),
        (opened_in, opened),
        (line_in, next_line),
        (across_in, across),
        *by_field((middle_in, middle), (coeff_in, coeff_ref)),
    )
    rest, fields = rest[:5], rest[5:]
    finish(waves_copy, table_copy)
    flat = waves[:, :, :ROWS].reshape(WAVES, ROWS)
    filtered[...] = dot(flat, table[...], 0, 0)
    polar_row = jnp.where(top, BAND - 1, 0)
    opposite[...] = across_pole(flat, table[...], polar_row)
    finish(*rest)
    weight = row_weight(mask, 0, (BAND, WIDTH))
    row = iota((BAND, WIDTH), 0)
    none = jnp.zeros((HALF, 128), jnp.float32)
    narrow = row_weight(mask, 0, (BAND, 128))
    for side, lane in enumerate((WIDTH + 1 - LAST, WIDTH - LAST)):
        tile = jnp.where(narrow > 0.5, edges[side], whole_band(none, opened[side], top))
        halos[side] = halo_of(tile, filtered[:, LAST:], lane, narrow)

    def one(field, level, carry):
        slab = field * LEV + level
        here = pl.ds(slab, 1)
        value = middle[field, level]
        smooth = filtered[pl.ds(slab * BAND, BAND)]
        value = value + weight * (smooth[:, :WIDTH] - value)
        coeff = load_coeff(coeff_ref, field, level)
        band = pl.ds(slab * BAND, BAND)
        west, east = halos[0, band, 0:1], halos[1, band, 0:1]
        halo = next_line[here]
        total, _, _ = gather_terms(
            value, coeff, jnp.where(top, halo, 0.0), jnp.where(top, 0.0, halo), west, east
        )
        pole = (across[here] * opposite[here])[:, :WIDTH]
        result[field, level] = total + jnp.where(row == polar_row, pole, 0.0)
        return carry

    stored = []
    for field in range(FIELDS):
        finish(*fields[2 * field : 2 * field + 2])
        for_levels(field, one)
        stored += begin(sems.at[field : field + 1], (result.at[field], out.at[field]))
    finish(*stored)


def edge_kernel(field_in, coeff_in, edges, field, to_east, to_west, sems):
    finish(
        *begin(
            sems,
            (field_in, field),
            (coeff_in.at[:, 3], to_east),
            (coeff_in.at[:, 4], to_west),
        )
    )
    east = west = jnp.zeros((BAND, 128), jnp.float32)
    for slab in range(SLABS):
        at = slab // LEV, slab % LEV
        value = field[at]
        east = with_lane(east, slab, (to_east[at] * value)[:, WIDTH - 1 :])
        west = with_lane(west, slab, (to_west[at] * value)[:, 0:1])
    edges[0] = east
    edges[1] = west


def line_kernel(
    field_in, extra_in, coeff_in, west_in, east_in,
    to_north, to_south, to_polar,
    field_ref, extra, coeff_ref, west_edge, east_edge, sems,
):
    _, lat = place()
    finish(
        *begin(
            sems,
            (field_in, field_ref),
            (extra_in, extra),
            (coeff_in, coeff_ref),
            (west_in, west_edge),
            (east_in, east_edge),
        )
    )
    none = jnp.zeros((1, WIDTH), jnp.float32)

    def one(field, level, carry):
        slab = field * LEV + level
        here = pl.ds(slab, 1)
        coeff = load_coeff(coeff_ref, field, level)
        west, east = lane_of(west_edge[...], slab), lane_of(east_edge[...], slab)
        total, north, south = gather_terms(field_ref[field, level], coeff, none, none, west, east)
        total = total + extra[field, level]
        norths = total[BAND - 1 :], coeff[1][BAND - 1 :], north[BAND - 1 :]
        souths = total[0:1], coeff[2][0:1], south[0:1]
        for part in range(3):
            to_north[part, here] = norths[part]
            to_south[part, here] = souths[part]
            to_polar[part, here] = jnp.where(lat == 1, souths[part], norths[part])
        return carry

    for_slabs(one)


def plain_middle_kernel(
    state_in, extra_in, coeff_in, west_in, east_in, below_in, above_in, polar_in,
    edges, lines, middle_out,
    state, extra, coeff_ref, west_edge, east_edge, below, above, polar, middle, sems,
):
    _, lat = place()
    finish(
        *begin(
            sems,
            (state_in, state),
            (extra_in, extra),
            (coeff_in, coeff_ref),
            (west_in, west_edge),
            (east_in, east_edge),
            (below_in, below),
            (above_in, above),
            (polar_in, polar),
        )
    )

    def one(field, level, carry):
        east_tile, west_tile = carry
        slab = field * LEV + level
        here = pl.ds(slab, 1)
        coeff = load_coeff(coeff_ref, field, level)
        west, east = lane_of(west_edge[...], slab), lane_of(east_edge[...], slab)
        reached = polar[0, here]
        total, north, south = gather_terms(
            state[field, level],
            coeff,
            jnp.where(lat == 1, reached, below[2, here]),
            jnp.where(lat == TOP - 1, reached, above[2, here]),
            west,
            east,
        )
        total = total + extra[field, level]
        middle[field, level] = total
        low = below[1, here] * (below[0, here] + south[0:1])
        high = above[1, here] * (above[0, here] + north[BAND - 1 :])
        lines[0, here] = jnp.where(lat == 1, 0.0, low)
        lines[1, here] = jnp.where(lat == TOP - 1, 0.0, high)
        east_tile = with_lane(east_tile, slab, (coeff[3] * total)[:, WIDTH - 1 :])
        west_tile = with_lane(west_tile, slab, (coeff[4] * total)[:, 0:1])
        return east_tile, west_tile

    none = jnp.zeros((BAND, 128), jnp.float32)
    edges[0], edges[1] = for_slabs(one, (none, none))
    finish(*begin(sems, (middle, middle_out)))


def plain_final_kernel(
    middle_in, coeff_in, west_in, east_in, lines_in, table_in,
    out, part, table,
    middle, coeff_ref, west_edge, east_edge, lines, sems,
):
    lon, lat = place()
    finish(
        *begin(
            sems,
            (middle_in, middle),
            (coeff_in, coeff_ref),
            (west_in, west_edge),
            (east_in, east_edge),
            (lines_in, lines),
            (table_in.at[lon], table),
        )
    )

    def one(field, level, carry):
        slab = field * LEV + level
        here = pl.ds(slab, 1)
        coeff = load_coeff(coeff_ref, field, level)
        west, east = lane_of(west_edge[...], slab), lane_of(east_edge[...], slab)
        value = middle[field, level]
        total = gather_terms(value, coeff, lines[0, here], lines[1, here], west, east)[0]
        out[field, level] = total
        part[field, level] = jnp.where(lat == 1, total[:HALF], total[HALF:])
        return carry

    for_slabs(one)


def reach_kernel(part, waves, table, polar, result_in, result_out, changed, sems):
    _, lat = place()
    bottom = lat == 1
    rows = pl.ds(pl.multiple_of(jnp.where(bottom, 0, HALF), HALF), HALF)

    @pl.when(bottom | (lat == TOP - 1))
    def _():
        flat = waves[...].reshape(WAVES, 128)
        smooth = dot(flat, table[...], 0, 0)[64 : 64 + SLABS, :WIDTH]
        masked = flat[0:1, 64 + SLABS : 65 + SLABS] > 0.5
        line = polar[1] * jnp.where(masked, smooth, 1.0)
        row = iota((HALF, WIDTH), 0)
        mine = row == jnp.where(bottom, 0, HALF - 1)
        for slab in range(SLABS):
            at = slab // LEV, slab % LEV
            changed[at] = part[at] + jnp.where(mine, line[slab : slab + 1], 0.0)
        finish(*begin(sems, (changed, result_out.at[:, :, rows])))


def exchanged(chunks):
    return lax.all_to_all(chunks, "lon", split_axis=0, concat_axis=0, tiled=True)


def moved(value, lats, north, east):
    pairs = []
    for lat, lon in [(lat, lon) for lat in lats for lon in range(LON_DEV)]:
        pairs.append((lat * LON_DEV + lon, (lat + north) * LON_DEV + (lon + east) % LON_DEV))
    return lax.ppermute(value, ("lat", "lon"), pairs)


def next_to_pole(value, outward):
    pairs = []
    for lon in range(LON_DEV):
        for polar, other in ((0, 1), (TOP, TOP - 1)):
            pair = polar * LON_DEV + lon, other * LON_DEV + lon
            pairs.append(pair if outward else pair[::-1])
    return lax.ppermute(value, ("lat", "lon"), pairs)


def local(adjoint_state, innovation, coefficients, polar_mask, wave_cutoff):
    lat = lax.axis_index("lat")
    polar = (lat == 0) | (lat == TOP)
    table = jnp.asarray(wave_tables())
    small = pltpu.SMEM((BAND,), jnp.int32)
    plain = range(1, TOP)
    table_scratch = in_vmem((WAVES, WIDE))
    halo_scratch = in_vmem((2, ROWS, 128))
    wave_scratch = [in_vmem((ROWS, WIDE)), in_vmem((128, WIDE)), halo_scratch]
    one_edge = (BAND, 128)

    def blanks(*shapes):
        return tuple(jnp.zeros(shape, jnp.float32) for shape in shapes)

    def polar_first():
        half = in_vmem(HALF_FIELD)
        send, to_polar, to_north, to_south, edge = launch(
            forward_kernel_with_blanks,
            [adjoint_state, coefficients, table, polar_mask],
            [FIRST_CHUNKS],
            [LINES, LINES, LINES, (2, *one_edge)],
            [in_vmem(FIELD), table_scratch, half, half, half, in_vmem(ACROSS), small],
            copies=6,
        )
        received = exchanged(send)
        (tiles,) = launch(closed_kernel, [coefficients], [TILES], (), [half, half], copies=2)
        send, opened = launch(
            first_respond_kernel,
            [received, tiles, wave_cutoff],
            [FIRST_CHUNKS, TILES],
            (),
            [small],
            copies=1,
            near=2,
        )
        return send, opened, to_polar, to_north, to_south, edge

    def plain_first():
        (edges,) = launch(
            edge_kernel,
            [adjoint_state, coefficients],
            [(2, *one_edge)],
            (),
            [in_vmem(FIELD)] * 3,
            copies=3,
        )
        west = moved(edges[0], plain, 0, 1)
        east = moved(edges[1], plain, 0, -1)
        to_north, to_south, to_polar = launch(
            line_kernel,
            [adjoint_state, innovation, coefficients, west, east],
            [LINES, LINES, LINES],
            (),
            [in_vmem(FIELD), in_vmem(FIELD), in_vmem(COEFF), in_vmem(one_edge), in_vmem(one_edge)],
            copies=5,
        )
        send, opened = blanks(FIRST_CHUNKS, TILES)
        return send, opened, to_polar, to_north, to_south, jnp.stack([west, east])

    send, opened, to_polar, to_north, to_south, edge = lax.cond(polar, polar_first, plain_first)
    beyond = next_to_pole(to_polar, False)

    def polar_second():
        return exchanged(send), to_north, to_south

    def plain_second():
        below = moved(to_north, range(1, TOP - 1), 1, 0)
        above = moved(to_south, range(2, TOP), -1, 0)
        return *blanks(FIRST_CHUNKS), below, above

    waves, below, above = lax.cond(polar, polar_second, plain_second)

    def polar_third():
        return tuple(launch(
            middle_kernel,
            [waves, table, polar_mask, adjoint_state, innovation, coefficients, opened, beyond],
            [CHUNKS, (2, *LINE), LINE, EDGES, ACROSS],
            [FIELD],
            [in_vmem(FIRST_CHUNKS), table_scratch, small, in_vmem(FIELD), in_vmem(FIELD), in_vmem(COEFF)]
            + [in_vmem(TILES), in_vmem(LINES), in_vmem(FIELD), *wave_scratch, halo_scratch],
            copies=14,
        ))

    def plain_third():
        return blanks(CHUNKS, (2, *LINE), LINE, EDGES, ACROSS, FIELD)

    send, to_next, next_line, edges, across, middle = lax.cond(polar, polar_third, plain_third)
    reached = next_to_pole(to_next, True)

    def polar_fourth():
        received = exchanged(send)
        again, opened, result, part, own_table = launch(
            second_respond_kernel_with_blank,
            [received, wave_cutoff, polar_mask],
            [CHUNKS, TILES],
            [FIELD, HALF_FIELD, (WAVES, WIDE)],
            [small, small],
            copies=2,
            near=1,
        )
        waves = exchanged(again)
        return waves, lax.slice_in_dim(waves, MORE - 128, MORE, axis=2), opened, result, part, own_table

    def plain_fourth():
        west, east = edge[0], edge[1]
        second, lines, middle = launch(
            plain_middle_kernel,
            [adjoint_state, innovation, coefficients, west, east, below, above, reached],
            [(2, *one_edge), (2, *LINE)],
            [FIELD],
            [in_vmem(FIELD), in_vmem(FIELD), in_vmem(COEFF), in_vmem(one_edge), in_vmem(one_edge)]
            + [in_vmem(LINES), in_vmem(LINES), in_vmem((2, *LINE)), in_vmem(FIELD)],
            copies=8,
        )
        west = moved(second[0], plain, 0, 1)
        east = moved(second[1], plain, 0, -1)
        result, part, own_table = launch(
            plain_final_kernel,
            [middle, coefficients, west, east, lines, table],
            [FIELD, HALF_FIELD, (WAVES, WIDE)],
            (),
            [in_vmem(FIELD), in_vmem(COEFF), in_vmem(one_edge), in_vmem(one_edge), in_vmem((2, *LINE))],
            copies=6,
        )
        return *blanks(CHUNKS, LAST_TILE, TILES), result, part, own_table

    waves, near_waves, opened, result, part, own_table = lax.cond(polar, polar_fourth, plain_fourth)
    waves_beyond = next_to_pole(near_waves, True)

    def polar_fifth():
        (out,) = launch(
            final_kernel,
            [waves, table, polar_mask, middle, coefficients, edges, opened, next_line, across],
            (),
            [FIELD],
            [in_vmem(CHUNKS), table_scratch, small, in_vmem(FIELD), in_vmem(COEFF), in_vmem(EDGES)]
            + [in_vmem(TILES), in_vmem(LINE), in_vmem(ACROSS), in_vmem(FIELD), *wave_scratch],
            copies=13,
            pinned=True,
        )
        return out

    result = lax.cond(polar, polar_fifth, lambda kept=result: kept)
    (out,) = launch(
        reach_kernel,
        [part, waves_beyond, own_table, reached, result],
        (),
        [FIELD],
        [in_vmem(HALF_FIELD)],
        copies=1,
        aliases={4: 0},
        near=4,
        pinned=True,
    )
    return out


def forward_kernel_with_blanks(*refs):
    forward_kernel(*refs[:5], *refs[9:])


def second_respond_kernel_with_blank(*refs):
    second_respond_kernel(*refs[:5], *refs[8:])


def solution(mesh):
    return jax.shard_map(
        local,
        mesh=mesh,
        in_specs=(
            P(None, None, "lat", "lon"),
            P(None, None, "lat", "lon"),
            P(None, None, None, "lat", "lon"),
            P("lat"),
            P("lat"),
        ),
        out_specs=P(None, None, "lat", "lon"),
        check_vma=False,
    )
```

```python
import math

import jax
import jax.numpy as jnp
import numpy as np
from jax import lax
from jax.experimental import pallas as pl
from jax.experimental.pallas import tpu as pltpu
from jax.sharding import PartitionSpec as P

NLON = 5760
KMAX = 64
WAVES = 2 * KMAX
FIELDS = 3
LEV = 12
BAND = 16
HALF = BAND // 2
LON_DEV = 16
LAT_DEV = 16
TOP = LAT_DEV - 1
WIDTH = NLON // LON_DEV
WIDE = 384
LAST = (WIDTH - 1) // 128 * 128
SLABS = FIELDS * LEV
ROWS = SLABS * BAND
SHARE = WAVES // LON_DEV
UNROLL = 6

FIELD = (FIELDS, LEV, BAND, WIDTH)
HALF_FIELD = (FIELDS, LEV, HALF, WIDTH)
COEFF = (FIELDS, 5, LEV, BAND, WIDTH)
MORE = ROWS + 64
CHUNKS = (LON_DEV, SHARE, MORE)
FIRST_CHUNKS = (LON_DEV, SHARE, MORE + 128)
LINE = (SLABS, WIDTH)
ACROSS = (40, WIDE)
LINES = (3, SLABS, WIDTH)
TILES = (2, HALF, 128)
EDGES = (3, BAND, 128)


def wave_tables():
    columns = np.concatenate([np.arange(WIDTH), [WIDTH, -1]])
    phases = (np.arange(LON_DEV)[:, None] * WIDTH + columns[None, :]) % NLON
    phases = phases[:, None, :] * np.arange(KMAX)[None, :, None] % NLON
    radians = phases * (2.0 * math.pi / NLON)
    both = np.concatenate([np.cos(radians), np.sin(radians)], axis=1)
    return np.pad(both, ((0, 0), (0, 0), (0, WIDE - WIDTH - 2))).astype(np.float32)


def split(value):
    high = value.astype(jnp.bfloat16)
    return high, (value - high.astype(jnp.float32)).astype(jnp.bfloat16)


def pair_dot(left, right, left_dim, right_dim):
    return lax.dot_general(
        left, right, (((left_dim,), (right_dim,)), ((), ())), preferred_element_type=jnp.float32
    )


def dot(left, right, left_dim, right_dim):
    (left_high, left_low), (right_high, right_low) = split(left), split(right)
    total = pair_dot(left_high, right_low, left_dim, right_dim)
    total = total + pair_dot(left_low, right_high, left_dim, right_dim)
    return total + pair_dot(left_high, right_high, left_dim, right_dim)


def iota(shape, dim):
    return lax.broadcasted_iota(jnp.int32, shape, dim)


def in_vmem(shape):
    return pltpu.VMEM(shape, jnp.float32)


def launch(kernel, operands, outs, far_outs=(), scratch=(), copies=0, aliases=None, near=0, pinned=False):
    shapes = [*outs, *far_outs]
    nbytes = sum(4 * math.prod(shape) for shape in shapes)
    nbytes += sum(4 * math.prod(operand.shape) for operand in operands)
    return pl.pallas_call(
        kernel,
        in_specs=[pl.BlockSpec(memory_space=pltpu.VMEM)] * near
        + [pl.BlockSpec(memory_space=pltpu.HBM)] * (len(operands) - near),
        out_specs=[pl.BlockSpec(memory_space=pltpu.VMEM)] * len(outs)
        + [pl.BlockSpec(memory_space=pltpu.HBM)] * len(far_outs),
        out_shape=[
            (pltpu.HBM if pinned else jax.ShapeDtypeStruct)(shape, jnp.float32) for shape in shapes
        ],
        scratch_shapes=[*scratch, pltpu.SemaphoreType.DMA((copies,))],
        input_output_aliases=aliases or {},
        compiler_params=pltpu.CompilerParams(vmem_limit_bytes=24 * 2**20),
        cost_estimate=pl.CostEstimate(flops=0, bytes_accessed=nbytes, transcendentals=0),
    )(*operands)


def begin(sems, *pairs):
    started = []
    for index, (source, target) in enumerate(pairs):
        copy = pltpu.make_async_copy(source, target, sems.at[index])
        copy.start()
        started.append(copy)
    return started


def by_field(*pairs):
    return [(source.at[field], target.at[field]) for field in range(FIELDS) for source, target in pairs]


def finish(*started):
    for copy in started:
        copy.wait()


def for_levels(field, one, carry=0):
    def some(step, carry):
        for level in range(UNROLL):
            carry = one(field, step * UNROLL + level, carry)
        return carry

    return lax.fori_loop(0, LEV // UNROLL, some, carry)


def for_slabs(one, carry=0):
    for field in range(FIELDS):
        carry = for_levels(field, one, carry)
    return carry


def lane_of(tile, slab):
    return jnp.sum(jnp.where(iota(tile.shape, 1) == slab, tile, 0.0), axis=1, keepdims=True)


def with_lane(tile, slab, column):
    return jnp.where(iota(tile.shape, 1) == slab, column, tile)


def exact_dot(value, chosen, left_dim=1, right_dim=0):
    high, low = split(value)
    chosen = chosen.astype(jnp.float32).astype(jnp.bfloat16)
    return pair_dot(high, chosen, left_dim, right_dim) + pair_dot(low, chosen, left_dim, right_dim)


def every_lane(values, lane):
    return exact_dot(values, iota((values.shape[1], 128), 0) == lane)


def own_lane(rows):
    shape = (SLABS * rows, 128)
    return iota(shape, 0) // rows == iota(shape, 1)


def tile_of(values, lane, rows, first):
    spread = jnp.where(own_lane(rows), every_lane(values, lane), 0.0)
    shape = (HALF, SLABS * rows)
    picked = iota(shape, 1) % rows == iota(shape, 0) + first
    picked = picked.astype(jnp.float32).astype(jnp.bfloat16)
    high, low = split(spread)
    return pair_dot(picked, high, 1, 0) + pair_dot(picked, low, 1, 0)


def halo_of(tile, wave_lanes, lane, weight):
    tall = jnp.concatenate([tile] * SLABS, axis=0)
    spread = exact_dot(jnp.where(own_lane(BAND), tall, 0.0), iota((128, 128), 0) >= 0)
    filtered = jnp.concatenate([weight] * SLABS, axis=0) > 0.5
    return spread * jnp.where(filtered, every_lane(wave_lanes, lane), 1.0)


def place():
    return lax.axis_index("lon"), lax.axis_index("lat")


def open_row(lat):
    return pl.multiple_of(jnp.where(lat == TOP, 0, HALF), HALF)


def row_weight(mask, first, shape):
    row = iota(shape, 0)
    weight = jnp.zeros(shape, jnp.float32)
    for r in range(shape[0]):
        weight = jnp.where(row == r, mask[first + r].astype(jnp.float32), weight)
    return weight


TILED = ACROSS[0] // 8 * (WIDE // 128)


def tile_place(index):
    row, column = index // (WIDE // 128), index % (WIDE // 128)
    return slice(8 * row, 8 * row + 8), slice(128 * column, 128 * column + 128)


def forward_kernel(
    field_in, coeff_in, table_in, mask_in,
    send,
    field, table, to_east, to_west, pole, across, mask, sems,
):
    lon, lat = place()
    top = lat == TOP
    first = open_row(lat)
    rows = pl.ds(first, HALF)
    closed = pl.ds(pl.multiple_of(HALF - first, HALF), HALF)
    field_copy, table_copy, *rest = begin(
        sems,
        (field_in, field),
        (table_in.at[lon], table),
        (coeff_in.at[:, 3, :, rows], to_east),
        (coeff_in.at[:, 4, :, rows], to_west),
        (mask_in, mask),
        (coeff_in.at[:, jnp.where(top, 1, 2), :, closed], pole),
    )
    across[...] = jnp.zeros(ACROSS, jnp.float32)
    finish(field_copy, table_copy)
    waves = dot(table[:, :WIDTH], field[...].reshape(ROWS, WIDTH), 1, 1)
    send[:, :, :ROWS] = waves.reshape(LON_DEV, SHARE, ROWS)
    finish(*rest)
    filtered = row_weight(mask, first, (HALF, 1)) > 0.5
    east = west = jnp.zeros((HALF, 128), jnp.float32)
    for slab in range(SLABS):
        at = slab // LEV, slab % LEV
        value = field[*at, rows]
        coeff = to_east[at][:, WIDTH - 1 :]
        east = with_lane(east, slab, jnp.where(filtered, coeff, coeff * value[:, WIDTH - 1 :]))
        coeff = to_west[at][:, 0:1]
        west = with_lane(west, slab, jnp.where(filtered, coeff, coeff * value[:, 0:1]))
        sign = 1.0 if at[0] == FIELDS - 1 else -1.0
        lines = pole[at]
        line = jnp.where(top, lines[HALF - 1 :], lines[0:1])
        across[slab : slab + 1, :WIDTH] = sign * line
    for target in range(LON_DEV):
        tile = jnp.where(target == (lon + 1) % LON_DEV, east, west)
        send[target, :, ROWS:MORE] = tile[:, :64]
        send[target, :, MORE:] = across[tile_place(target)] if target < TILED else tile


def closed_kernel(coeff_in, tiles, to_east, to_west, sems):
    _, lat = place()
    closed = pl.ds(pl.multiple_of(HALF - open_row(lat), HALF), HALF)
    finish(
        *begin(
            sems,
            (coeff_in.at[:, 3, :, closed], to_east),
            (coeff_in.at[:, 4, :, closed], to_west),
        )
    )
    east = west = jnp.zeros((HALF, 128), jnp.float32)
    for slab in range(SLABS):
        at = slab // LEV, slab % LEV
        east = with_lane(east, slab, to_east[at][:, WIDTH - 1 :])
        west = with_lane(west, slab, to_west[at][:, 0:1])
    tiles[0] = east
    tiles[1] = west


def responded(received, cutoff, edges):
    lon, _ = place()
    shape = (SHARE, ROWS)
    wave = (lon * SHARE + iota(shape, 0)) % KMAX
    row = iota(shape, 1) % BAND
    limit = jnp.zeros(shape, jnp.int32)
    for r in range(BAND):
        limit = jnp.where(row == r, cutoff[r], limit)
    ratio = limit.astype(jnp.float32) / jnp.maximum(wave, 1).astype(jnp.float32)
    response = jnp.where(wave <= limit, 1.0, ratio * ratio)
    response = response * jnp.where(wave == 0, 1.0 / NLON, 2.0 / NLON)
    total = received[0, :, :ROWS]
    for source in range(1, LON_DEV):
        total = total + received[source, :, :ROWS]
    blank = jnp.zeros((HALF, 64), jnp.float32)
    west = received[(lon + LON_DEV - 1) % LON_DEV, :, ROWS:MORE]
    east = received[(lon + 1) % LON_DEV, :, ROWS:MORE]
    edges[0] = jnp.concatenate([west, blank], axis=1)
    edges[1] = jnp.concatenate([east, blank], axis=1)
    return total * response


def first_respond_kernel(received, tiles, cutoff_in, send, edges, cutoff, sems):
    lon, _ = place()
    finish(*begin(sems, (cutoff_in, cutoff)))
    total = responded(received, cutoff, edges)
    for target in range(LON_DEV):
        send[target, :, :ROWS] = total
        tile = jnp.where(target == (lon + 1) % LON_DEV, tiles[0], tiles[1])
        send[target, :, ROWS:MORE] = tile[:, :64]
        send[target, :, MORE:] = received[(target + LON_DEV // 2) % LON_DEV, :, MORE:]


def second_respond_kernel(received, cutoff_in, mask_in, send, edges, cutoff, mask, sems):
    _, lat = place()
    finish(*begin(sems, (cutoff_in, cutoff), (mask_in, mask)))
    total = responded(received, cutoff, edges)
    near_row = jnp.where(lat == TOP, 0, BAND - 1)
    near = row_waves(total, near_row)
    near = with_lane(near, SLABS, mask[near_row].astype(jnp.float32))
    for target in range(LON_DEV):
        send[target, :, :ROWS] = total
        send[target, :, ROWS:] = near[:, :64]


def gather_terms(value, coeff, south_line, north_line, west_edge, east_edge):
    to_north, to_south = coeff[1] * value, coeff[2] * value
    total = coeff[0] * value
    total = total + jnp.concatenate([south_line, to_north[:-1]], axis=0)
    total = total + jnp.concatenate([to_south[1:], north_line], axis=0)
    total = total + jnp.concatenate([west_edge, (coeff[3] * value)[:, :-1]], axis=1)
    total = total + jnp.concatenate([(coeff[4] * value)[:, 1:], east_edge], axis=1)
    return total, to_north, to_south


def load_coeff(coeff, field, level):
    return [coeff[field, term, level] for term in range(5)]


def row_waves(waves, row):
    picked = iota((ROWS, 128), 0) == iota((ROWS, 128), 1) * BAND + row
    picked = picked.astype(jnp.float32).astype(jnp.bfloat16)
    high, low = split(waves)
    return pair_dot(high, picked, 1, 0) + pair_dot(low, picked, 1, 0)


def across_pole(waves, table, row):
    chosen = row_waves(waves, row)
    chosen = jnp.where(iota((WAVES, 128), 0) % 2 == 1, -chosen, chosen)
    return dot(chosen, table, 0, 0)


def whole_band(closed, opened, top):
    return jnp.where(
        top, jnp.concatenate([opened, closed], axis=0), jnp.concatenate([closed, opened], axis=0)
    )


def middle_kernel(
    waves_in, table_in, mask_in, state_in, extra_in, coeff_in, opened_in, beyond_in,
    send, to_next, next_line, edges, across, middle_out,
    waves, table, mask, state, extra, coeff_ref, opened, beyond, middle,
    filtered, opposite, halos, ends, sems,
):
    lon, lat = place()
    top = lat == TOP
    waves_copy, table_copy, *rest = begin(
        sems,
        (waves_in, waves),
        (table_in.at[lon], table),
        (mask_in, mask),
        (opened_in, opened),
        (beyond_in, beyond),
        *by_field((state_in, state), (extra_in, extra), (coeff_in, coeff_ref)),
    )
    rest, fields = rest[:3], rest[3:]
    finish(waves_copy, table_copy)
    for tile in range(TILED):
        across[tile_place(tile)] = waves[tile, :, MORE:]
    flat = waves[:, :, :ROWS].reshape(WAVES, ROWS)
    filtered[...] = dot(flat, table[...], 0, 0)
    polar_row = jnp.where(top, BAND - 1, 0)
    opposite[...] = across_pole(flat, table[...], polar_row)
    finish(*rest)
    blank = jnp.zeros((HALF, 64), jnp.float32)
    sides = (lon + LON_DEV - 1) % LON_DEV, (lon + 1) % LON_DEV
    for side in range(2):
        closed = jnp.concatenate([waves[sides[side], :, ROWS:MORE], blank], axis=1)
        edges[side] = whole_band(closed, opened[side], top)
    weight = row_weight(mask, 0, (BAND, WIDTH))
    narrow = row_weight(mask, 0, (BAND, 128))
    edges[2] = narrow
    for side, lane in enumerate((WIDTH + 1 - LAST, WIDTH - LAST)):
        halos[side] = halo_of(edges[side], filtered[:, LAST:], lane, narrow)
    next_weight = jnp.where(top, weight[0:1], weight[BAND - 1 :])
    row = iota((BAND, WIDTH), 0)

    def one(field, level, carry):
        slab = field * LEV + level
        here = pl.ds(slab, 1)
        value = state[field, level]
        smooth = filtered[pl.ds(slab * BAND, BAND)]
        value = value + weight * (smooth[:, :WIDTH] - value)
        coeff = load_coeff(coeff_ref, field, level)
        band = pl.ds(slab * BAND, BAND)
        west, east = halos[0, band, 0:1], halos[1, band, 0:1]
        halo = beyond[2, here]
        total, north, south = gather_terms(
            value, coeff, jnp.where(top, halo, 0.0), jnp.where(top, 0.0, halo), west, east
        )
        pole = (across[here] * opposite[here])[:, :WIDTH]
        total = total + jnp.where(row == polar_row, pole, 0.0) + extra[field, level]
        middle[field, level] = total
        product = jnp.where(top, south[0:1], north[BAND - 1 :])
        near = jnp.where(top, total[0:1], total[BAND - 1 :])
        near_coeff = jnp.where(top, coeff[2][0:1], coeff[1][BAND - 1 :])
        to_next[0, here] = product
        to_next[1, here] = jnp.where(next_weight > 0.5, near_coeff, near_coeff * near)
        next_line[here] = beyond[1, here] * (beyond[0, here] + product)
        ends[0, band, : WIDTH - LAST] = (coeff[3] * total)[:, LAST:]
        ends[1, band] = (coeff[4] * total)[:, :128]
        return carry

    stored = []
    for field in range(FIELDS):
        finish(*fields[3 * field : 3 * field + 3])
        for_levels(field, one)
        stored += begin(sems.at[field : field + 1], (middle.at[field], middle_out.at[field]))
    sums = dot(table[:, :WIDTH], middle[...].reshape(ROWS, WIDTH), 1, 1)
    send[:, :, :ROWS] = sums.reshape(LON_DEV, SHARE, ROWS)
    east_tile = tile_of(ends[0, :, : WIDTH - LAST], WIDTH - LAST - 1, BAND, open_row(lat))
    west_tile = tile_of(ends[1], 0, BAND, open_row(lat))
    for target in range(LON_DEV):
        tile = jnp.where(target == (lon + 1) % LON_DEV, east_tile, west_tile)
        send[target, :, ROWS:] = tile[:, :64]
    finish(*stored)


def final_kernel(
    waves_in, table_in, middle_in, coeff_in, edges_in, opened_in, line_in, across_in,
    out,
    waves, table, middle, coeff_ref, edges, opened, next_line, across, result,
    filtered, opposite, halos, sems,
):
    lon, lat = place()
    top = lat == TOP
    waves_copy, table_copy, *rest = begin(
        sems,
        (waves_in, waves),
        (table_in.at[lon], table),
        (edges_in, edges),
        (opened_in, opened),
        (line_in, next_line),
        (across_in, across),
        *by_field((middle_in, middle), (coeff_in, coeff_ref)),
    )
    rest, fields = rest[:4], rest[4:]
    finish(waves_copy, table_copy)
    flat = waves[:, :, :ROWS].reshape(WAVES, ROWS)
    filtered[...] = dot(flat, table[...], 0, 0)
    polar_row = jnp.where(top, BAND - 1, 0)
    opposite[...] = across_pole(flat, table[...], polar_row)
    finish(*rest)
    narrow = edges[2]
    weight = jnp.concatenate([narrow] * (WIDE // 128), axis=1)[:, :WIDTH]
    row = iota((BAND, WIDTH), 0)
    none = jnp.zeros((HALF, 128), jnp.float32)
    for side, lane in enumerate((WIDTH + 1 - LAST, WIDTH - LAST)):
        tile = jnp.where(narrow > 0.5, edges[side], whole_band(none, opened[side], top))
        halos[side] = halo_of(tile, filtered[:, LAST:], lane, narrow)

    def one(field, level, carry):
        slab = field * LEV + level
        here = pl.ds(slab, 1)
        value = middle[field, level]
        smooth = filtered[pl.ds(slab * BAND, BAND)]
        value = value + weight * (smooth[:, :WIDTH] - value)
        coeff = load_coeff(coeff_ref, field, level)
        band = pl.ds(slab * BAND, BAND)
        west, east = halos[0, band, 0:1], halos[1, band, 0:1]
        halo = next_line[here]
        total, _, _ = gather_terms(
            value, coeff, jnp.where(top, halo, 0.0), jnp.where(top, 0.0, halo), west, east
        )
        pole = (across[here] * opposite[here])[:, :WIDTH]
        result[field, level] = total + jnp.where(row == polar_row, pole, 0.0)
        return carry

    stored = []
    for field in range(FIELDS):
        finish(*fields[2 * field : 2 * field + 2])
        for_levels(field, one)
        stored += begin(sems.at[field : field + 1], (result.at[field], out.at[field]))
    finish(*stored)


def edge_kernel(field_in, coeff_in, edges, field, to_east, to_west, sems):
    finish(
        *begin(
            sems,
            (field_in, field),
            (coeff_in.at[:, 3], to_east),
            (coeff_in.at[:, 4], to_west),
        )
    )
    east = west = jnp.zeros((BAND, 128), jnp.float32)
    for slab in range(SLABS):
        at = slab // LEV, slab % LEV
        value = field[at]
        east = with_lane(east, slab, (to_east[at] * value)[:, WIDTH - 1 :])
        west = with_lane(west, slab, (to_west[at] * value)[:, 0:1])
    edges[0] = east
    edges[1] = west


def line_kernel(
    field_in, extra_in, coeff_in, west_in, east_in,
    to_north, to_south, to_polar,
    field_ref, extra, coeff_ref, west_edge, east_edge, sems,
):
    _, lat = place()
    finish(
        *begin(
            sems,
            (field_in, field_ref),
            (extra_in, extra),
            (coeff_in, coeff_ref),
            (west_in, west_edge),
            (east_in, east_edge),
        )
    )
    none = jnp.zeros((1, WIDTH), jnp.float32)

    def one(field, level, carry):
        slab = field * LEV + level
        here = pl.ds(slab, 1)
        coeff = load_coeff(coeff_ref, field, level)
        west, east = lane_of(west_edge[...], slab), lane_of(east_edge[...], slab)
        total, north, south = gather_terms(field_ref[field, level], coeff, none, none, west, east)
        total = total + extra[field, level]
        norths = total[BAND - 1 :], coeff[1][BAND - 1 :], north[BAND - 1 :]
        souths = total[0:1], coeff[2][0:1], south[0:1]
        for part in range(3):
            to_north[part, here] = norths[part]
            to_south[part, here] = souths[part]
            to_polar[part, here] = jnp.where(lat == 1, souths[part], norths[part])
        return carry

    for_slabs(one)


def plain_middle_kernel(
    state_in, extra_in, coeff_in, west_in, east_in, below_in, above_in, polar_in,
    edges, lines, middle_out,
    state, extra, coeff_ref, west_edge, east_edge, below, above, polar, middle, sems,
):
    _, lat = place()
    finish(
        *begin(
            sems,
            (state_in, state),
            (extra_in, extra),
            (coeff_in, coeff_ref),
            (west_in, west_edge),
            (east_in, east_edge),
            (below_in, below),
            (above_in, above),
            (polar_in, polar),
        )
    )

    def one(field, level, carry):
        east_tile, west_tile = carry
        slab = field * LEV + level
        here = pl.ds(slab, 1)
        coeff = load_coeff(coeff_ref, field, level)
        west, east = lane_of(west_edge[...], slab), lane_of(east_edge[...], slab)
        reached = polar[0, here]
        total, north, south = gather_terms(
            state[field, level],
            coeff,
            jnp.where(lat == 1, reached, below[2, here]),
            jnp.where(lat == TOP - 1, reached, above[2, here]),
            west,
            east,
        )
        total = total + extra[field, level]
        middle[field, level] = total
        low = below[1, here] * (below[0, here] + south[0:1])
        high = above[1, here] * (above[0, here] + north[BAND - 1 :])
        lines[0, here] = jnp.where(lat == 1, 0.0, low)
        lines[1, here] = jnp.where(lat == TOP - 1, 0.0, high)
        east_tile = with_lane(east_tile, slab, (coeff[3] * total)[:, WIDTH - 1 :])
        west_tile = with_lane(west_tile, slab, (coeff[4] * total)[:, 0:1])
        return east_tile, west_tile

    none = jnp.zeros((BAND, 128), jnp.float32)
    edges[0], edges[1] = for_slabs(one, (none, none))
    finish(*begin(sems, (middle, middle_out)))


def plain_final_kernel(
    middle_in, coeff_in, west_in, east_in, lines_in, table_in,
    out, part, table,
    middle, coeff_ref, west_edge, east_edge, lines, sems,
):
    lon, lat = place()
    finish(
        *begin(
            sems,
            (middle_in, middle),
            (coeff_in, coeff_ref),
            (west_in, west_edge),
            (east_in, east_edge),
            (lines_in, lines),
            (table_in.at[lon], table),
        )
    )

    def one(field, level, carry):
        slab = field * LEV + level
        here = pl.ds(slab, 1)
        coeff = load_coeff(coeff_ref, field, level)
        west, east = lane_of(west_edge[...], slab), lane_of(east_edge[...], slab)
        value = middle[field, level]
        total = gather_terms(value, coeff, lines[0, here], lines[1, here], west, east)[0]
        out[field, level] = total
        part[field, level] = jnp.where(lat == 1, total[:HALF], total[HALF:])
        return carry

    for_slabs(one)


def reach_kernel(part, waves, table, polar, result_in, result_out, changed, sems):
    _, lat = place()
    bottom = lat == 1
    rows = pl.ds(pl.multiple_of(jnp.where(bottom, 0, HALF), HALF), HALF)

    @pl.when(bottom | (lat == TOP - 1))
    def _():
        flat = waves[:, :, MORE - 128 :].reshape(WAVES, 128)
        smooth = dot(flat, table[...], 0, 0)[64 : 64 + SLABS, :WIDTH]
        masked = flat[0:1, 64 + SLABS : 65 + SLABS] > 0.5
        line = polar[1] * jnp.where(masked, smooth, 1.0)
        row = iota((HALF, WIDTH), 0)
        mine = row == jnp.where(bottom, 0, HALF - 1)
        for slab in range(SLABS):
            at = slab // LEV, slab % LEV
            changed[at] = part[at] + jnp.where(mine, line[slab : slab + 1], 0.0)
        finish(*begin(sems, (changed, result_out.at[:, :, rows])))


def exchanged(chunks):
    return lax.all_to_all(chunks, "lon", split_axis=0, concat_axis=0, tiled=True)


def moved(value, lats, north, east):
    pairs = []
    for lat, lon in [(lat, lon) for lat in lats for lon in range(LON_DEV)]:
        pairs.append((lat * LON_DEV + lon, (lat + north) * LON_DEV + (lon + east) % LON_DEV))
    return lax.ppermute(value, ("lat", "lon"), pairs)


def next_to_pole(value, outward):
    pairs = []
    for lon in range(LON_DEV):
        for polar, other in ((0, 1), (TOP, TOP - 1)):
            pair = polar * LON_DEV + lon, other * LON_DEV + lon
            pairs.append(pair if outward else pair[::-1])
    return lax.ppermute(value, ("lat", "lon"), pairs)


def local(adjoint_state, innovation, coefficients, polar_mask, wave_cutoff):
    lat = lax.axis_index("lat")
    polar = (lat == 0) | (lat == TOP)
    table = jnp.asarray(wave_tables())
    small = pltpu.SMEM((BAND,), jnp.int32)
    plain = range(1, TOP)
    table_scratch = in_vmem((WAVES, WIDE))
    halo_scratch = in_vmem((2, ROWS, 128))
    wave_scratch = [in_vmem((ROWS, WIDE)), in_vmem((128, WIDE)), halo_scratch]
    one_edge = (BAND, 128)

    def blanks(*shapes):
        return tuple(jnp.zeros(shape, jnp.float32) for shape in shapes)

    def polar_first():
        half = in_vmem(HALF_FIELD)
        send, to_polar, to_north, to_south, edge = launch(
            forward_kernel_with_blanks,
            [adjoint_state, coefficients, table, polar_mask],
            [FIRST_CHUNKS],
            [LINES, LINES, LINES, (2, *one_edge)],
            [in_vmem(FIELD), table_scratch, half, half, half, in_vmem(ACROSS), small],
            copies=6,
        )
        received = exchanged(send)
        (tiles,) = launch(closed_kernel, [coefficients], [TILES], (), [half, half], copies=2)
        send, opened = launch(
            first_respond_kernel,
            [received, tiles, wave_cutoff],
            [FIRST_CHUNKS, TILES],
            (),
            [small],
            copies=1,
            near=2,
        )
        return send, opened, to_polar, to_north, to_south, edge

    def plain_first():
        (edges,) = launch(
            edge_kernel,
            [adjoint_state, coefficients],
            [(2, *one_edge)],
            (),
            [in_vmem(FIELD)] * 3,
            copies=3,
        )
        west = moved(edges[0], plain, 0, 1)
        east = moved(edges[1], plain, 0, -1)
        to_north, to_south, to_polar = launch(
            line_kernel,
            [adjoint_state, innovation, coefficients, west, east],
            [LINES, LINES, LINES],
            (),
            [in_vmem(FIELD), in_vmem(FIELD), in_vmem(COEFF), in_vmem(one_edge), in_vmem(one_edge)],
            copies=5,
        )
        send, opened = blanks(FIRST_CHUNKS, TILES)
        return send, opened, to_polar, to_north, to_south, jnp.stack([west, east])

    send, opened, to_polar, to_north, to_south, edge = lax.cond(polar, polar_first, plain_first)
    beyond = next_to_pole(to_polar, False)

    def polar_second():
        return exchanged(send), to_north, to_south

    def plain_second():
        below = moved(to_north, range(1, TOP - 1), 1, 0)
        above = moved(to_south, range(2, TOP), -1, 0)
        return *blanks(FIRST_CHUNKS), below, above

    waves, below, above = lax.cond(polar, polar_second, plain_second)

    def polar_third():
        return tuple(launch(
            middle_kernel,
            [waves, table, polar_mask, adjoint_state, innovation, coefficients, opened, beyond],
            [CHUNKS, (2, *LINE), LINE, EDGES, ACROSS],
            [FIELD],
            [in_vmem(FIRST_CHUNKS), table_scratch, small, in_vmem(FIELD), in_vmem(FIELD), in_vmem(COEFF)]
            + [in_vmem(TILES), in_vmem(LINES), in_vmem(FIELD), *wave_scratch, halo_scratch],
            copies=14,
        ))

    def plain_third():
        return blanks(CHUNKS, (2, *LINE), LINE, EDGES, ACROSS, FIELD)

    send, to_next, next_line, edges, across, middle = lax.cond(polar, polar_third, plain_third)
    reached = next_to_pole(to_next, True)

    def polar_fourth():
        received = exchanged(send)
        again, opened = launch(
            second_respond_kernel,
            [received, wave_cutoff, polar_mask],
            [CHUNKS, TILES],
            (),
            [small, small],
            copies=2,
            near=1,
        )
        return exchanged(again), opened

    waves, opened = lax.cond(polar, polar_fourth, lambda: blanks(CHUNKS, TILES))
    reached, waves = lax.optimization_barrier((reached, waves))

    def polar_wait():
        return tuple(launch(lambda *_: None, [], (), [FIELD, HALF_FIELD, (WAVES, WIDE)], copies=1))

    def plain_fourth():
        west, east = edge[0], edge[1]
        second, lines, middle = launch(
            plain_middle_kernel,
            [adjoint_state, innovation, coefficients, west, east, below, above, reached],
            [(2, *one_edge), (2, *LINE)],
            [FIELD],
            [in_vmem(FIELD), in_vmem(FIELD), in_vmem(COEFF), in_vmem(one_edge), in_vmem(one_edge)]
            + [in_vmem(LINES), in_vmem(LINES), in_vmem((2, *LINE)), in_vmem(FIELD)],
            copies=8,
        )
        west = moved(second[0], plain, 0, 1)
        east = moved(second[1], plain, 0, -1)
        result, part, own_table = launch(
            plain_final_kernel,
            [middle, coefficients, west, east, lines, table],
            [FIELD, HALF_FIELD, (WAVES, WIDE)],
            (),
            [in_vmem(FIELD), in_vmem(COEFF), in_vmem(one_edge), in_vmem(one_edge), in_vmem((2, *LINE))],
            copies=6,
        )
        return result, part, own_table

    result, part, own_table = lax.cond(polar, polar_wait, plain_fourth)
    waves_beyond = next_to_pole(waves, True)

    def polar_fifth():
        (out,) = launch(
            final_kernel,
            [waves, table, middle, coefficients, edges, opened, next_line, across],
            (),
            [FIELD],
            [in_vmem(CHUNKS), table_scratch, in_vmem(FIELD), in_vmem(COEFF), in_vmem(EDGES)]
            + [in_vmem(TILES), in_vmem(LINE), in_vmem(ACROSS), in_vmem(FIELD), *wave_scratch],
            copies=12,
            pinned=True,
        )
        return out

    result = lax.cond(polar, polar_fifth, lambda kept=result: kept)
    (out,) = launch(
        reach_kernel,
        [part, waves_beyond, own_table, reached, result],
        (),
        [FIELD],
        [in_vmem(HALF_FIELD)],
        copies=1,
        aliases={4: 0},
        near=4,
        pinned=True,
    )
    return out


def forward_kernel_with_blanks(*refs):
    forward_kernel(*refs[:5], *refs[9:])


def solution(mesh):
    return jax.shard_map(
        local,
        mesh=mesh,
        in_specs=(
            P(None, None, "lat", "lon"),
            P(None, None, "lat", "lon"),
            P(None, None, None, "lat", "lon"),
            P("lat"),
            P("lat"),
        ),
        out_specs=P(None, None, "lat", "lon"),
        check_vma=False,
    )
```

```python
import math

import jax
import jax.numpy as jnp
import numpy as np
from jax import lax
from jax.experimental import pallas as pl
from jax.experimental.pallas import tpu as pltpu
from jax.sharding import PartitionSpec as P

NLON = 5760
KMAX = 64
WAVES = 2 * KMAX
FIELDS = 3
LEV = 12
BAND = 16
HALF = BAND // 2
LON_DEV = 16
LAT_DEV = 16
TOP = LAT_DEV - 1
WIDTH = NLON // LON_DEV
WIDE = 384
LAST = (WIDTH - 1) // 128 * 128
SLABS = FIELDS * LEV
ROWS = SLABS * BAND
SHARE = WAVES // LON_DEV
UNROLL = 12

FIELD = (FIELDS, LEV, BAND, WIDTH)
HALF_FIELD = (FIELDS, LEV, HALF, WIDTH)
COEFF = (FIELDS, 5, LEV, BAND, WIDTH)
MORE = ROWS + 64
CHUNKS = (LON_DEV, SHARE, MORE)
FIRST_CHUNKS = (LON_DEV, SHARE, MORE + 128)
LINE = (SLABS, WIDTH)
ACROSS = (40, WIDE)
LINES = (3, SLABS, WIDTH)
TILES = (2, HALF, 128)
EDGES = (3, BAND, 128)


def wave_tables():
    columns = np.concatenate([np.arange(WIDTH), [WIDTH, -1]])
    phases = (np.arange(LON_DEV)[:, None] * WIDTH + columns[None, :]) % NLON
    phases = phases[:, None, :] * np.arange(KMAX)[None, :, None] % NLON
    radians = phases * (2.0 * math.pi / NLON)
    both = np.concatenate([np.cos(radians), np.sin(radians)], axis=1)
    return np.pad(both, ((0, 0), (0, 0), (0, WIDE - WIDTH - 2))).astype(np.float32)


def split(value):
    high = value.astype(jnp.bfloat16)
    return high, (value - high.astype(jnp.float32)).astype(jnp.bfloat16)


def pair_dot(left, right, left_dim, right_dim):
    return lax.dot_general(
        left, right, (((left_dim,), (right_dim,)), ((), ())), preferred_element_type=jnp.float32
    )


def dot(left, right, left_dim, right_dim):
    (left_high, left_low), (right_high, right_low) = split(left), split(right)
    total = pair_dot(left_high, right_low, left_dim, right_dim)
    total = total + pair_dot(left_low, right_high, left_dim, right_dim)
    return total + pair_dot(left_high, right_high, left_dim, right_dim)


def iota(shape, dim):
    return lax.broadcasted_iota(jnp.int32, shape, dim)


def in_vmem(shape):
    return pltpu.VMEM(shape, jnp.float32)


def launch(kernel, operands, outs, far_outs=(), scratch=(), copies=0, aliases=None, near=0, pinned=False):
    shapes = [*outs, *far_outs]
    nbytes = sum(4 * math.prod(shape) for shape in shapes)
    nbytes += sum(4 * math.prod(operand.shape) for operand in operands)
    return pl.pallas_call(
        kernel,
        in_specs=[pl.BlockSpec(memory_space=pltpu.VMEM)] * near
        + [pl.BlockSpec(memory_space=pltpu.HBM)] * (len(operands) - near),
        out_specs=[pl.BlockSpec(memory_space=pltpu.VMEM)] * len(outs)
        + [pl.BlockSpec(memory_space=pltpu.HBM)] * len(far_outs),
        out_shape=[
            (pltpu.HBM if pinned else jax.ShapeDtypeStruct)(shape, jnp.float32) for shape in shapes
        ],
        scratch_shapes=[*scratch, pltpu.SemaphoreType.DMA((copies,))],
        input_output_aliases=aliases or {},
        compiler_params=pltpu.CompilerParams(vmem_limit_bytes=24 * 2**20),
        cost_estimate=pl.CostEstimate(flops=0, bytes_accessed=nbytes, transcendentals=0),
    )(*operands)


def begin(sems, *pairs):
    started = []
    for index, (source, target) in enumerate(pairs):
        copy = pltpu.make_async_copy(source, target, sems.at[index])
        copy.start()
        started.append(copy)
    return started


def by_field(*pairs):
    return [(source.at[field], target.at[field]) for field in range(FIELDS) for source, target in pairs]


def finish(*started):
    for copy in started:
        copy.wait()


def for_levels(field, one, carry=0):
    def some(step, carry):
        for level in range(UNROLL):
            carry = one(field, step * UNROLL + level, carry)
        return carry

    return lax.fori_loop(0, LEV // UNROLL, some, carry)


def for_slabs(one, carry=0):
    for field in range(FIELDS):
        carry = for_levels(field, one, carry)
    return carry


def lane_of(tile, slab):
    return jnp.sum(jnp.where(iota(tile.shape, 1) == slab, tile, 0.0), axis=1, keepdims=True)


def with_lane(tile, slab, column):
    return jnp.where(iota(tile.shape, 1) == slab, column, tile)


def exact_dot(value, chosen, left_dim=1, right_dim=0):
    high, low = split(value)
    chosen = chosen.astype(jnp.float32).astype(jnp.bfloat16)
    return pair_dot(high, chosen, left_dim, right_dim) + pair_dot(low, chosen, left_dim, right_dim)


def every_lane(values, lane):
    return exact_dot(values, iota((values.shape[1], 128), 0) == lane)


def own_lane(rows):
    shape = (SLABS * rows, 128)
    return iota(shape, 0) // rows == iota(shape, 1)


def tile_of(values, lane, rows, first):
    spread = jnp.where(own_lane(rows), every_lane(values, lane), 0.0)
    shape = (HALF, SLABS * rows)
    picked = iota(shape, 1) % rows == iota(shape, 0) + first
    picked = picked.astype(jnp.float32).astype(jnp.bfloat16)
    high, low = split(spread)
    return pair_dot(picked, high, 1, 0) + pair_dot(picked, low, 1, 0)


def halo_of(tile, wave_lanes, lane, weight):
    tall = jnp.concatenate([tile] * SLABS, axis=0)
    spread = exact_dot(jnp.where(own_lane(BAND), tall, 0.0), iota((128, 128), 0) >= 0)
    filtered = jnp.concatenate([weight] * SLABS, axis=0) > 0.5
    return spread * jnp.where(filtered, every_lane(wave_lanes, lane), 1.0)


def place():
    return lax.axis_index("lon"), lax.axis_index("lat")


def open_row(lat):
    return pl.multiple_of(jnp.where(lat == TOP, 0, HALF), HALF)


def row_weight(mask, first, shape):
    row = iota(shape, 0)
    weight = jnp.zeros(shape, jnp.float32)
    for r in range(shape[0]):
        weight = jnp.where(row == r, mask[first + r].astype(jnp.float32), weight)
    return weight


TILED = ACROSS[0] // 8 * (WIDE // 128)


def tile_place(index):
    row, column = index // (WIDE // 128), index % (WIDE // 128)
    return slice(8 * row, 8 * row + 8), slice(128 * column, 128 * column + 128)


def forward_kernel(
    field_in, coeff_in, table_in, mask_in,
    send,
    field, table, to_east, to_west, pole, across, mask, sems,
):
    lon, lat = place()
    top = lat == TOP
    first = open_row(lat)
    rows = pl.ds(first, HALF)
    closed = pl.ds(pl.multiple_of(HALF - first, HALF), HALF)
    field_copy, table_copy, *rest = begin(
        sems,
        (field_in, field),
        (table_in.at[lon], table),
        (coeff_in.at[:, 3, :, rows], to_east),
        (coeff_in.at[:, 4, :, rows], to_west),
        (mask_in, mask),
        (coeff_in.at[:, jnp.where(top, 1, 2), :, closed], pole),
    )
    across[...] = jnp.zeros(ACROSS, jnp.float32)
    finish(field_copy, table_copy)
    waves = dot(table[:, :WIDTH], field[...].reshape(ROWS, WIDTH), 1, 1)
    send[:, :, :ROWS] = waves.reshape(LON_DEV, SHARE, ROWS)
    finish(*rest)
    filtered = row_weight(mask, first, (HALF, 1)) > 0.5
    east = west = jnp.zeros((HALF, 128), jnp.float32)
    for slab in range(SLABS):
        at = slab // LEV, slab % LEV
        value = field[*at, rows]
        coeff = to_east[at][:, WIDTH - 1 :]
        east = with_lane(east, slab, jnp.where(filtered, coeff, coeff * value[:, WIDTH - 1 :]))
        coeff = to_west[at][:, 0:1]
        west = with_lane(west, slab, jnp.where(filtered, coeff, coeff * value[:, 0:1]))
        sign = 1.0 if at[0] == FIELDS - 1 else -1.0
        lines = pole[at]
        line = jnp.where(top, lines[HALF - 1 :], lines[0:1])
        across[slab : slab + 1, :WIDTH] = sign * line
    for target in range(LON_DEV):
        tile = jnp.where(target == (lon + 1) % LON_DEV, east, west)
        send[target, :, ROWS:MORE] = tile[:, :64]
        send[target, :, MORE:] = across[tile_place(target)] if target < TILED else tile


def closed_kernel(coeff_in, tiles, to_east, to_west, sems):
    _, lat = place()
    closed = pl.ds(pl.multiple_of(HALF - open_row(lat), HALF), HALF)
    finish(
        *begin(
            sems,
            (coeff_in.at[:, 3, :, closed], to_east),
            (coeff_in.at[:, 4, :, closed], to_west),
        )
    )
    east = west = jnp.zeros((HALF, 128), jnp.float32)
    for slab in range(SLABS):
        at = slab // LEV, slab % LEV
        east = with_lane(east, slab, to_east[at][:, WIDTH - 1 :])
        west = with_lane(west, slab, to_west[at][:, 0:1])
    tiles[0] = east
    tiles[1] = west


def responded(received, cutoff, edges):
    lon, _ = place()
    shape = (SHARE, ROWS)
    wave = (lon * SHARE + iota(shape, 0)) % KMAX
    row = iota(shape, 1) % BAND
    limit = jnp.zeros(shape, jnp.int32)
    for r in range(BAND):
        limit = jnp.where(row == r, cutoff[r], limit)
    ratio = limit.astype(jnp.float32) / jnp.maximum(wave, 1).astype(jnp.float32)
    response = jnp.where(wave <= limit, 1.0, ratio * ratio)
    response = response * jnp.where(wave == 0, 1.0 / NLON, 2.0 / NLON)
    total = received[0, :, :ROWS]
    for source in range(1, LON_DEV):
        total = total + received[source, :, :ROWS]
    blank = jnp.zeros((HALF, 64), jnp.float32)
    west = received[(lon + LON_DEV - 1) % LON_DEV, :, ROWS:MORE]
    east = received[(lon + 1) % LON_DEV, :, ROWS:MORE]
    edges[0] = jnp.concatenate([west, blank], axis=1)
    edges[1] = jnp.concatenate([east, blank], axis=1)
    return total * response


def first_respond_kernel(received, tiles, cutoff_in, send, edges, cutoff, sems):
    lon, _ = place()
    finish(*begin(sems, (cutoff_in, cutoff)))
    total = responded(received, cutoff, edges)
    for target in range(LON_DEV):
        send[target, :, :ROWS] = total
        tile = jnp.where(target == (lon + 1) % LON_DEV, tiles[0], tiles[1])
        send[target, :, ROWS:MORE] = tile[:, :64]
        send[target, :, MORE:] = received[(target + LON_DEV // 2) % LON_DEV, :, MORE:]


def second_respond_kernel(received, cutoff_in, mask_in, send, edges, cutoff, mask, sems):
    _, lat = place()
    finish(*begin(sems, (cutoff_in, cutoff), (mask_in, mask)))
    total = responded(received, cutoff, edges)
    near_row = jnp.where(lat == TOP, 0, BAND - 1)
    near = row_waves(total, near_row)
    near = with_lane(near, SLABS, mask[near_row].astype(jnp.float32))
    for target in range(LON_DEV):
        send[target, :, :ROWS] = total
        send[target, :, ROWS:] = near[:, :64]


def gather_terms(value, coeff, south_line, north_line, west_edge, east_edge):
    to_north, to_south = coeff[1] * value, coeff[2] * value
    total = coeff[0] * value
    total = total + jnp.concatenate([south_line, to_north[:-1]], axis=0)
    total = total + jnp.concatenate([to_south[1:], north_line], axis=0)
    total = total + jnp.concatenate([west_edge, (coeff[3] * value)[:, :-1]], axis=1)
    total = total + jnp.concatenate([(coeff[4] * value)[:, 1:], east_edge], axis=1)
    return total, to_north, to_south


def load_coeff(coeff, field, level):
    return [coeff[field, term, level] for term in range(5)]


def row_waves(waves, row):
    picked = iota((ROWS, 128), 0) == iota((ROWS, 128), 1) * BAND + row
    picked = picked.astype(jnp.float32).astype(jnp.bfloat16)
    high, low = split(waves)
    return pair_dot(high, picked, 1, 0) + pair_dot(low, picked, 1, 0)


def across_pole(waves, table, row):
    chosen = row_waves(waves, row)
    chosen = jnp.where(iota((WAVES, 128), 0) % 2 == 1, -chosen, chosen)
    return dot(chosen, table, 0, 0)


def whole_band(closed, opened, top):
    return jnp.where(
        top, jnp.concatenate([opened, closed], axis=0), jnp.concatenate([closed, opened], axis=0)
    )


def middle_kernel(
    waves_in, table_in, mask_in, state_in, extra_in, coeff_in, opened_in, beyond_in,
    send, to_next, next_line, edges, across, middle_out,
    waves, table, mask, state, extra, coeff_ref, opened, beyond, middle,
    filtered, opposite, halos, ends, sems,
):
    lon, lat = place()
    top = lat == TOP
    waves_copy, table_copy, *rest = begin(
        sems,
        (waves_in, waves),
        (table_in.at[lon], table),
        (mask_in, mask),
        (opened_in, opened),
        (beyond_in, beyond),
        *by_field((state_in, state), (extra_in, extra), (coeff_in, coeff_ref)),
    )
    rest, fields = rest[:3], rest[3:]
    finish(waves_copy, table_copy)
    for tile in range(TILED):
        across[tile_place(tile)] = waves[tile, :, MORE:]
    flat = waves[:, :, :ROWS].reshape(WAVES, ROWS)
    filtered[...] = dot(flat, table[...], 0, 0)
    polar_row = jnp.where(top, BAND - 1, 0)
    opposite[...] = across_pole(flat, table[...], polar_row)
    finish(*rest)
    blank = jnp.zeros((HALF, 64), jnp.float32)
    sides = (lon + LON_DEV - 1) % LON_DEV, (lon + 1) % LON_DEV
    for side in range(2):
        closed = jnp.concatenate([waves[sides[side], :, ROWS:MORE], blank], axis=1)
        edges[side] = whole_band(closed, opened[side], top)
    weight = row_weight(mask, 0, (BAND, WIDTH))
    narrow = row_weight(mask, 0, (BAND, 128))
    edges[2] = narrow
    for side, lane in enumerate((WIDTH + 1 - LAST, WIDTH - LAST)):
        halos[side] = halo_of(edges[side], filtered[:, LAST:], lane, narrow)
    next_weight = jnp.where(top, weight[0:1], weight[BAND - 1 :])
    row = iota((BAND, WIDTH), 0)

    def one(field, level, carry):
        slab = field * LEV + level
        here = pl.ds(slab, 1)
        value = state[field, level]
        smooth = filtered[pl.ds(slab * BAND, BAND)]
        value = value + weight * (smooth[:, :WIDTH] - value)
        coeff = load_coeff(coeff_ref, field, level)
        band = pl.ds(slab * BAND, BAND)
        west, east = halos[0, band, 0:1], halos[1, band, 0:1]
        halo = beyond[2, here]
        total, north, south = gather_terms(
            value, coeff, jnp.where(top, halo, 0.0), jnp.where(top, 0.0, halo), west, east
        )
        pole = (across[here] * opposite[here])[:, :WIDTH]
        total = total + jnp.where(row == polar_row, pole, 0.0) + extra[field, level]
        middle[field, level] = total
        product = jnp.where(top, south[0:1], north[BAND - 1 :])
        near = jnp.where(top, total[0:1], total[BAND - 1 :])
        near_coeff = jnp.where(top, coeff[2][0:1], coeff[1][BAND - 1 :])
        to_next[0, here] = product
        to_next[1, here] = jnp.where(next_weight > 0.5, near_coeff, near_coeff * near)
        next_line[here] = beyond[1, here] * (beyond[0, here] + product)
        ends[0, band, : WIDTH - LAST] = (coeff[3] * total)[:, LAST:]
        ends[1, band] = (coeff[4] * total)[:, :128]
        return carry

    stored = []
    for field in range(FIELDS):
        finish(*fields[3 * field : 3 * field + 3])
        for_levels(field, one)
        stored += begin(sems.at[field : field + 1], (middle.at[field], middle_out.at[field]))
    sums = dot(table[:, :WIDTH], middle[...].reshape(ROWS, WIDTH), 1, 1)
    send[:, :, :ROWS] = sums.reshape(LON_DEV, SHARE, ROWS)
    east_tile = tile_of(ends[0, :, : WIDTH - LAST], WIDTH - LAST - 1, BAND, open_row(lat))
    west_tile = tile_of(ends[1], 0, BAND, open_row(lat))
    for target in range(LON_DEV):
        tile = jnp.where(target == (lon + 1) % LON_DEV, east_tile, west_tile)
        send[target, :, ROWS:] = tile[:, :64]
    finish(*stored)


def final_kernel(
    waves_in, table_in, middle_in, coeff_in, edges_in, opened_in, line_in, across_in,
    out,
    waves, table, middle, coeff_ref, edges, opened, next_line, across, result,
    filtered, opposite, halos, sems,
):
    lon, lat = place()
    top = lat == TOP
    waves_copy, table_copy, *rest = begin(
        sems,
        (waves_in, waves),
        (table_in.at[lon], table),
        (edges_in, edges),
        (opened_in, opened),
        (line_in, next_line),
        (across_in, across),
        *by_field((middle_in, middle), (coeff_in, coeff_ref)),
    )
    rest, fields = rest[:4], rest[4:]
    finish(waves_copy, table_copy)
    flat = waves[:, :, :ROWS].reshape(WAVES, ROWS)
    filtered[...] = dot(flat, table[...], 0, 0)
    polar_row = jnp.where(top, BAND - 1, 0)
    opposite[...] = across_pole(flat, table[...], polar_row)
    finish(*rest)
    narrow = edges[2]
    weight = jnp.concatenate([narrow] * (WIDE // 128), axis=1)[:, :WIDTH]
    row = iota((BAND, WIDTH), 0)
    none = jnp.zeros((HALF, 128), jnp.float32)
    for side, lane in enumerate((WIDTH + 1 - LAST, WIDTH - LAST)):
        tile = jnp.where(narrow > 0.5, edges[side], whole_band(none, opened[side], top))
        halos[side] = halo_of(tile, filtered[:, LAST:], lane, narrow)

    def one(field, level, carry):
        slab = field * LEV + level
        here = pl.ds(slab, 1)
        value = middle[field, level]
        smooth = filtered[pl.ds(slab * BAND, BAND)]
        value = value + weight * (smooth[:, :WIDTH] - value)
        coeff = load_coeff(coeff_ref, field, level)
        band = pl.ds(slab * BAND, BAND)
        west, east = halos[0, band, 0:1], halos[1, band, 0:1]
        halo = next_line[here]
        total, _, _ = gather_terms(
            value, coeff, jnp.where(top, halo, 0.0), jnp.where(top, 0.0, halo), west, east
        )
        pole = (across[here] * opposite[here])[:, :WIDTH]
        result[field, level] = total + jnp.where(row == polar_row, pole, 0.0)
        return carry

    stored = []
    for field in range(FIELDS):
        finish(*fields[2 * field : 2 * field + 2])
        for_levels(field, one)
        stored += begin(sems.at[field : field + 1], (result.at[field], out.at[field]))
    finish(*stored)


def edge_kernel(field_in, coeff_in, edges, field, to_east, to_west, sems):
    finish(
        *begin(
            sems,
            (field_in, field),
            (coeff_in.at[:, 3], to_east),
            (coeff_in.at[:, 4], to_west),
        )
    )
    east = west = jnp.zeros((BAND, 128), jnp.float32)
    for slab in range(SLABS):
        at = slab // LEV, slab % LEV
        value = field[at]
        east = with_lane(east, slab, (to_east[at] * value)[:, WIDTH - 1 :])
        west = with_lane(west, slab, (to_west[at] * value)[:, 0:1])
    edges[0] = east
    edges[1] = west


def line_kernel(
    field_in, extra_in, coeff_in, west_in, east_in,
    to_north, to_south, to_polar,
    field_ref, extra, coeff_ref, west_edge, east_edge, sems,
):
    _, lat = place()
    finish(
        *begin(
            sems,
            (field_in, field_ref),
            (extra_in, extra),
            (coeff_in, coeff_ref),
            (west_in, west_edge),
            (east_in, east_edge),
        )
    )
    none = jnp.zeros((1, WIDTH), jnp.float32)

    def one(field, level, carry):
        slab = field * LEV + level
        here = pl.ds(slab, 1)
        coeff = load_coeff(coeff_ref, field, level)
        west, east = lane_of(west_edge[...], slab), lane_of(east_edge[...], slab)
        total, north, south = gather_terms(field_ref[field, level], coeff, none, none, west, east)
        total = total + extra[field, level]
        norths = total[BAND - 1 :], coeff[1][BAND - 1 :], north[BAND - 1 :]
        souths = total[0:1], coeff[2][0:1], south[0:1]
        for part in range(3):
            to_north[part, here] = norths[part]
            to_south[part, here] = souths[part]
            to_polar[part, here] = jnp.where(lat == 1, souths[part], norths[part])
        return carry

    for_slabs(one)


def plain_middle_kernel(
    state_in, extra_in, coeff_in, west_in, east_in, below_in, above_in, polar_in,
    edges, lines, middle_out,
    state, extra, coeff_ref, west_edge, east_edge, below, above, polar, middle, sems,
):
    _, lat = place()
    finish(
        *begin(
            sems,
            (state_in, state),
            (extra_in, extra),
            (coeff_in, coeff_ref),
            (west_in, west_edge),
            (east_in, east_edge),
            (below_in, below),
            (above_in, above),
            (polar_in, polar),
        )
    )

    def one(field, level, carry):
        east_tile, west_tile = carry
        slab = field * LEV + level
        here = pl.ds(slab, 1)
        coeff = load_coeff(coeff_ref, field, level)
        west, east = lane_of(west_edge[...], slab), lane_of(east_edge[...], slab)
        reached = polar[0, here]
        total, north, south = gather_terms(
            state[field, level],
            coeff,
            jnp.where(lat == 1, reached, below[2, here]),
            jnp.where(lat == TOP - 1, reached, above[2, here]),
            west,
            east,
        )
        total = total + extra[field, level]
        middle[field, level] = total
        low = below[1, here] * (below[0, here] + south[0:1])
        high = above[1, here] * (above[0, here] + north[BAND - 1 :])
        lines[0, here] = jnp.where(lat == 1, 0.0, low)
        lines[1, here] = jnp.where(lat == TOP - 1, 0.0, high)
        east_tile = with_lane(east_tile, slab, (coeff[3] * total)[:, WIDTH - 1 :])
        west_tile = with_lane(west_tile, slab, (coeff[4] * total)[:, 0:1])
        return east_tile, west_tile

    none = jnp.zeros((BAND, 128), jnp.float32)
    edges[0], edges[1] = for_slabs(one, (none, none))
    finish(*begin(sems, (middle, middle_out)))


def plain_final_kernel(
    middle_in, coeff_in, west_in, east_in, lines_in, table_in,
    out, part, table,
    middle, coeff_ref, west_edge, east_edge, lines, sems,
):
    lon, lat = place()
    finish(
        *begin(
            sems,
            (middle_in, middle),
            (coeff_in, coeff_ref),
            (west_in, west_edge),
            (east_in, east_edge),
            (lines_in, lines),
            (table_in.at[lon], table),
        )
    )

    def one(field, level, carry):
        slab = field * LEV + level
        here = pl.ds(slab, 1)
        coeff = load_coeff(coeff_ref, field, level)
        west, east = lane_of(west_edge[...], slab), lane_of(east_edge[...], slab)
        value = middle[field, level]
        total = gather_terms(value, coeff, lines[0, here], lines[1, here], west, east)[0]
        out[field, level] = total
        part[field, level] = jnp.where(lat == 1, total[:HALF], total[HALF:])
        return carry

    for_slabs(one)


def reach_kernel(part, waves, table, polar, result_in, result_out, changed, sems):
    _, lat = place()
    bottom = lat == 1
    rows = pl.ds(pl.multiple_of(jnp.where(bottom, 0, HALF), HALF), HALF)

    @pl.when(bottom | (lat == TOP - 1))
    def _():
        flat = waves[:, :, MORE - 128 :].reshape(WAVES, 128)
        smooth = dot(flat, table[...], 0, 0)[64 : 64 + SLABS, :WIDTH]
        masked = flat[0:1, 64 + SLABS : 65 + SLABS] > 0.5
        line = polar[1] * jnp.where(masked, smooth, 1.0)
        row = iota((HALF, WIDTH), 0)
        mine = row == jnp.where(bottom, 0, HALF - 1)
        for slab in range(SLABS):
            at = slab // LEV, slab % LEV
            changed[at] = part[at] + jnp.where(mine, line[slab : slab + 1], 0.0)
        finish(*begin(sems, (changed, result_out.at[:, :, rows])))


def exchanged(chunks):
    return lax.all_to_all(chunks, "lon", split_axis=0, concat_axis=0, tiled=True)


def moved(value, lats, north, east):
    pairs = []
    for lat, lon in [(lat, lon) for lat in lats for lon in range(LON_DEV)]:
        pairs.append((lat * LON_DEV + lon, (lat + north) * LON_DEV + (lon + east) % LON_DEV))
    return lax.ppermute(value, ("lat", "lon"), pairs)


def next_to_pole(value, outward):
    pairs = []
    for lon in range(LON_DEV):
        for polar, other in ((0, 1), (TOP, TOP - 1)):
            pair = polar * LON_DEV + lon, other * LON_DEV + lon
            pairs.append(pair if outward else pair[::-1])
    return lax.ppermute(value, ("lat", "lon"), pairs)


def local(adjoint_state, innovation, coefficients, polar_mask, wave_cutoff):
    lat = lax.axis_index("lat")
    polar = (lat == 0) | (lat == TOP)
    table = jnp.asarray(wave_tables())
    small = pltpu.SMEM((BAND,), jnp.int32)
    plain = range(1, TOP)
    table_scratch = in_vmem((WAVES, WIDE))
    halo_scratch = in_vmem((2, ROWS, 128))
    wave_scratch = [in_vmem((ROWS, WIDE)), in_vmem((128, WIDE)), halo_scratch]
    one_edge = (BAND, 128)

    def blanks(*shapes):
        return tuple(jnp.zeros(shape, jnp.float32) for shape in shapes)

    def polar_first():
        half = in_vmem(HALF_FIELD)
        send, to_polar, to_north, to_south, edge = launch(
            forward_kernel_with_blanks,
            [adjoint_state, coefficients, table, polar_mask],
            [FIRST_CHUNKS],
            [LINES, LINES, LINES, (2, *one_edge)],
            [in_vmem(FIELD), table_scratch, half, half, half, in_vmem(ACROSS), small],
            copies=6,
        )
        received = exchanged(send)
        (tiles,) = launch(closed_kernel, [coefficients], [TILES], (), [half, half], copies=2)
        send, opened = launch(
            first_respond_kernel,
            [received, tiles, wave_cutoff],
            [FIRST_CHUNKS, TILES],
            (),
            [small],
            copies=1,
            near=2,
        )
        return send, opened, to_polar, to_north, to_south, edge

    def plain_first():
        (edges,) = launch(
            edge_kernel,
            [adjoint_state, coefficients],
            [(2, *one_edge)],
            (),
            [in_vmem(FIELD)] * 3,
            copies=3,
        )
        west = moved(edges[0], plain, 0, 1)
        east = moved(edges[1], plain, 0, -1)
        to_north, to_south, to_polar = launch(
            line_kernel,
            [adjoint_state, innovation, coefficients, west, east],
            [LINES, LINES, LINES],
            (),
            [in_vmem(FIELD), in_vmem(FIELD), in_vmem(COEFF), in_vmem(one_edge), in_vmem(one_edge)],
            copies=5,
        )
        send, opened = blanks(FIRST_CHUNKS, TILES)
        return send, opened, to_polar, to_north, to_south, jnp.stack([west, east])

    send, opened, to_polar, to_north, to_south, edge = lax.cond(polar, polar_first, plain_first)
    beyond = next_to_pole(to_polar, False)

    def polar_second():
        return exchanged(send), to_north, to_south

    def plain_second():
        below = moved(to_north, range(1, TOP - 1), 1, 0)
        above = moved(to_south, range(2, TOP), -1, 0)
        return *blanks(FIRST_CHUNKS), below, above

    waves, below, above = lax.cond(polar, polar_second, plain_second)

    def polar_third():
        return tuple(launch(
            middle_kernel,
            [waves, table, polar_mask, adjoint_state, innovation, coefficients, opened, beyond],
            [CHUNKS, (2, *LINE), LINE, EDGES, ACROSS],
            [FIELD],
            [in_vmem(FIRST_CHUNKS), table_scratch, small, in_vmem(FIELD), in_vmem(FIELD), in_vmem(COEFF)]
            + [in_vmem(TILES), in_vmem(LINES), in_vmem(FIELD), *wave_scratch, halo_scratch],
            copies=14,
        ))

    def plain_third():
        return blanks(CHUNKS, (2, *LINE), LINE, EDGES, ACROSS, FIELD)

    send, to_next, next_line, edges, across, middle = lax.cond(polar, polar_third, plain_third)
    reached = next_to_pole(to_next, True)

    def polar_fourth():
        received = exchanged(send)
        again, opened = launch(
            second_respond_kernel,
            [received, wave_cutoff, polar_mask],
            [CHUNKS, TILES],
            (),
            [small, small],
            copies=2,
            near=1,
        )
        return exchanged(again), opened

    waves, opened = lax.cond(polar, polar_fourth, lambda: blanks(CHUNKS, TILES))
    reached, waves = lax.optimization_barrier((reached, waves))

    def polar_wait():
        return tuple(launch(lambda *_: None, [], (), [FIELD, HALF_FIELD, (WAVES, WIDE)], copies=1))

    def plain_fourth():
        west, east = edge[0], edge[1]
        second, lines, middle = launch(
            plain_middle_kernel,
            [adjoint_state, innovation, coefficients, west, east, below, above, reached],
            [(2, *one_edge), (2, *LINE)],
            [FIELD],
            [in_vmem(FIELD), in_vmem(FIELD), in_vmem(COEFF), in_vmem(one_edge), in_vmem(one_edge)]
            + [in_vmem(LINES), in_vmem(LINES), in_vmem((2, *LINE)), in_vmem(FIELD)],
            copies=8,
        )
        west = moved(second[0], plain, 0, 1)
        east = moved(second[1], plain, 0, -1)
        result, part, own_table = launch(
            plain_final_kernel,
            [middle, coefficients, west, east, lines, table],
            [FIELD, HALF_FIELD, (WAVES, WIDE)],
            (),
            [in_vmem(FIELD), in_vmem(COEFF), in_vmem(one_edge), in_vmem(one_edge), in_vmem((2, *LINE))],
            copies=6,
        )
        return result, part, own_table

    result, part, own_table = lax.cond(polar, polar_wait, plain_fourth)
    waves_beyond = next_to_pole(waves, True)

    def polar_fifth():
        (out,) = launch(
            final_kernel,
            [waves, table, middle, coefficients, edges, opened, next_line, across],
            (),
            [FIELD],
            [in_vmem(CHUNKS), table_scratch, in_vmem(FIELD), in_vmem(COEFF), in_vmem(EDGES)]
            + [in_vmem(TILES), in_vmem(LINE), in_vmem(ACROSS), in_vmem(FIELD), *wave_scratch],
            copies=12,
            pinned=True,
        )
        return out

    result = lax.cond(polar, polar_fifth, lambda kept=result: kept)
    (out,) = launch(
        reach_kernel,
        [part, waves_beyond, own_table, reached, result],
        (),
        [FIELD],
        [in_vmem(HALF_FIELD)],
        copies=1,
        aliases={4: 0},
        near=4,
        pinned=True,
    )
    return out


def forward_kernel_with_blanks(*refs):
    forward_kernel(*refs[:5], *refs[9:])


def solution(mesh):
    return jax.shard_map(
        local,
        mesh=mesh,
        in_specs=(
            P(None, None, "lat", "lon"),
            P(None, None, "lat", "lon"),
            P(None, None, None, "lat", "lon"),
            P("lat"),
            P("lat"),
        ),
        out_specs=P(None, None, "lat", "lon"),
        check_vma=False,
    )
```

```python
import math

import jax
import jax.numpy as jnp
import numpy as np
from jax import lax
from jax.experimental import pallas as pl
from jax.experimental.pallas import tpu as pltpu
from jax.sharding import PartitionSpec as P

NLON = 5760
KMAX = 64
WAVES = 2 * KMAX
FIELDS = 3
LEV = 12
BAND = 16
HALF = BAND // 2
LON_DEV = 16
LAT_DEV = 16
TOP = LAT_DEV - 1
WIDTH = NLON // LON_DEV
WIDE = 384
LAST = (WIDTH - 1) // 128 * 128
SLABS = FIELDS * LEV
ROWS = SLABS * BAND
SHARE = WAVES // LON_DEV
UNROLL = 12

FIELD = (FIELDS, LEV, BAND, WIDTH)
HALF_FIELD = (FIELDS, LEV, HALF, WIDTH)
COEFF = (FIELDS, 5, LEV, BAND, WIDTH)
MORE = ROWS + 64
CHUNKS = (LON_DEV, SHARE, MORE)
FIRST_CHUNKS = (LON_DEV, SHARE, MORE + 128)
LINE = (SLABS, WIDTH)
ACROSS = (40, WIDE)
LINES = (3, SLABS, WIDTH)
TILES = (2, HALF, 128)
EDGES = (3, BAND, 128)


def wave_tables():
    columns = np.concatenate([np.arange(WIDTH), [WIDTH, -1]])
    phases = (np.arange(LON_DEV)[:, None] * WIDTH + columns[None, :]) % NLON
    phases = phases[:, None, :] * np.arange(KMAX)[None, :, None] % NLON
    radians = phases * (2.0 * math.pi / NLON)
    both = np.concatenate([np.cos(radians), np.sin(radians)], axis=1)
    return np.pad(both, ((0, 0), (0, 0), (0, WIDE - WIDTH - 2))).astype(np.float32)


def split(value):
    high = value.astype(jnp.bfloat16)
    return high, (value - high.astype(jnp.float32)).astype(jnp.bfloat16)


def pair_dot(left, right, left_dim, right_dim):
    return lax.dot_general(
        left, right, (((left_dim,), (right_dim,)), ((), ())), preferred_element_type=jnp.float32
    )


def dot(left, right, left_dim, right_dim):
    (left_high, left_low), (right_high, right_low) = split(left), split(right)
    total = pair_dot(left_high, right_low, left_dim, right_dim)
    total = total + pair_dot(left_low, right_high, left_dim, right_dim)
    return total + pair_dot(left_high, right_high, left_dim, right_dim)


def iota(shape, dim):
    return lax.broadcasted_iota(jnp.int32, shape, dim)


def in_vmem(shape):
    return pltpu.VMEM(shape, jnp.float32)


def launch(kernel, operands, outs, far_outs=(), scratch=(), copies=0, aliases=None, near=0, pinned=False):
    shapes = [*outs, *far_outs]
    nbytes = sum(4 * math.prod(shape) for shape in shapes)
    nbytes += sum(4 * math.prod(operand.shape) for operand in operands)
    return pl.pallas_call(
        kernel,
        in_specs=[pl.BlockSpec(memory_space=pltpu.VMEM)] * near
        + [pl.BlockSpec(memory_space=pltpu.HBM)] * (len(operands) - near),
        out_specs=[pl.BlockSpec(memory_space=pltpu.VMEM)] * len(outs)
        + [pl.BlockSpec(memory_space=pltpu.HBM)] * len(far_outs),
        out_shape=[
            (pltpu.HBM if pinned else jax.ShapeDtypeStruct)(shape, jnp.float32) for shape in shapes
        ],
        scratch_shapes=[*scratch, pltpu.SemaphoreType.DMA((copies,))],
        input_output_aliases=aliases or {},
        compiler_params=pltpu.CompilerParams(vmem_limit_bytes=24 * 2**20),
        cost_estimate=pl.CostEstimate(flops=0, bytes_accessed=nbytes, transcendentals=0),
    )(*operands)


def begin(sems, *pairs):
    started = []
    for index, (source, target) in enumerate(pairs):
        copy = pltpu.make_async_copy(source, target, sems.at[index])
        copy.start()
        started.append(copy)
    return started


def by_field(*pairs):
    return [(source.at[field], target.at[field]) for field in range(FIELDS) for source, target in pairs]


def finish(*started):
    for copy in started:
        copy.wait()


def for_levels(field, one, carry=0):
    def some(step, carry):
        for level in range(UNROLL):
            carry = one(field, step * UNROLL + level, carry)
        return carry

    return lax.fori_loop(0, LEV // UNROLL, some, carry)


def for_slabs(one, carry=0):
    for field in range(FIELDS):
        carry = for_levels(field, one, carry)
    return carry


def lane_of(tile, slab):
    return jnp.sum(jnp.where(iota(tile.shape, 1) == slab, tile, 0.0), axis=1, keepdims=True)


def with_lane(tile, slab, column):
    return jnp.where(iota(tile.shape, 1) == slab, column, tile)


def exact_dot(value, chosen, left_dim=1, right_dim=0):
    high, low = split(value)
    chosen = chosen.astype(jnp.float32).astype(jnp.bfloat16)
    return pair_dot(high, chosen, left_dim, right_dim) + pair_dot(low, chosen, left_dim, right_dim)


def every_lane(values, lane):
    return exact_dot(values, iota((values.shape[1], 128), 0) == lane)


def own_lane(rows):
    shape = (SLABS * rows, 128)
    return iota(shape, 0) // rows == iota(shape, 1)


def tile_of(values, lane, rows, first):
    spread = jnp.where(own_lane(rows), every_lane(values, lane), 0.0)
    shape = (HALF, SLABS * rows)
    picked = iota(shape, 1) % rows == iota(shape, 0) + first
    picked = picked.astype(jnp.float32).astype(jnp.bfloat16)
    high, low = split(spread)
    return pair_dot(picked, high, 1, 0) + pair_dot(picked, low, 1, 0)


def halo_of(tile, wave_lanes, lane, weight):
    tall = jnp.concatenate([tile] * SLABS, axis=0)
    spread = exact_dot(jnp.where(own_lane(BAND), tall, 0.0), iota((128, 128), 0) >= 0)
    filtered = jnp.concatenate([weight] * SLABS, axis=0) > 0.5
    return spread * jnp.where(filtered, every_lane(wave_lanes, lane), 1.0)


def place():
    return lax.axis_index("lon"), lax.axis_index("lat")


def open_row(lat):
    return pl.multiple_of(jnp.where(lat == TOP, 0, HALF), HALF)


def row_weight(mask, first, shape):
    row = iota(shape, 0)
    weight = jnp.zeros(shape, jnp.float32)
    for r in range(shape[0]):
        weight = jnp.where(row == r, mask[first + r].astype(jnp.float32), weight)
    return weight


TILED = ACROSS[0] // 8 * (WIDE // 128)


def tile_place(index):
    row, column = index // (WIDE // 128), index % (WIDE // 128)
    return slice(8 * row, 8 * row + 8), slice(128 * column, 128 * column + 128)


def forward_kernel(
    field_in, coeff_in, table_in, mask_in,
    send,
    field, table, to_east, to_west, pole, across, mask, sems,
):
    lon, lat = place()
    top = lat == TOP
    first = open_row(lat)
    rows = pl.ds(first, HALF)
    closed = pl.ds(pl.multiple_of(HALF - first, HALF), HALF)
    field_copy, table_copy, *rest = begin(
        sems,
        (field_in, field),
        (table_in.at[lon], table),
        (coeff_in.at[:, 3, :, rows], to_east),
        (coeff_in.at[:, 4, :, rows], to_west),
        (mask_in, mask),
        (coeff_in.at[:, jnp.where(top, 1, 2), :, closed], pole),
    )
    across[...] = jnp.zeros(ACROSS, jnp.float32)
    finish(field_copy, table_copy)
    waves = dot(table[:, :WIDTH], field[...].reshape(ROWS, WIDTH), 1, 1)
    send[:, :, :ROWS] = waves.reshape(LON_DEV, SHARE, ROWS)
    finish(*rest)
    filtered = row_weight(mask, first, (HALF, 1)) > 0.5
    east = west = jnp.zeros((HALF, 128), jnp.float32)
    for slab in range(SLABS):
        at = slab // LEV, slab % LEV
        value = field[*at, rows]
        coeff = to_east[at][:, WIDTH - 1 :]
        east = with_lane(east, slab, jnp.where(filtered, coeff, coeff * value[:, WIDTH - 1 :]))
        coeff = to_west[at][:, 0:1]
        west = with_lane(west, slab, jnp.where(filtered, coeff, coeff * value[:, 0:1]))
        sign = 1.0 if at[0] == FIELDS - 1 else -1.0
        lines = pole[at]
        line = jnp.where(top, lines[HALF - 1 :], lines[0:1])
        across[slab : slab + 1, :WIDTH] = sign * line
    for target in range(LON_DEV):
        tile = jnp.where(target == (lon + 1) % LON_DEV, east, west)
        send[target, :, ROWS:MORE] = tile[:, :64]
        send[target, :, MORE:] = across[tile_place(target)] if target < TILED else tile


def closed_kernel(coeff_in, tiles, to_east, to_west, sems):
    _, lat = place()
    closed = pl.ds(pl.multiple_of(HALF - open_row(lat), HALF), HALF)
    finish(
        *begin(
            sems,
            (coeff_in.at[:, 3, :, closed], to_east),
            (coeff_in.at[:, 4, :, closed], to_west),
        )
    )
    east = west = jnp.zeros((HALF, 128), jnp.float32)
    for slab in range(SLABS):
        at = slab // LEV, slab % LEV
        east = with_lane(east, slab, to_east[at][:, WIDTH - 1 :])
        west = with_lane(west, slab, to_west[at][:, 0:1])
    tiles[0] = east
    tiles[1] = west


def responded(received, cutoff, edges):
    lon, _ = place()
    shape = (SHARE, ROWS)
    wave = (lon * SHARE + iota(shape, 0)) % KMAX
    row = iota(shape, 1) % BAND
    limit = jnp.zeros(shape, jnp.int32)
    for r in range(BAND):
        limit = jnp.where(row == r, cutoff[r], limit)
    ratio = limit.astype(jnp.float32) / jnp.maximum(wave, 1).astype(jnp.float32)
    response = jnp.where(wave <= limit, 1.0, ratio * ratio)
    response = response * jnp.where(wave == 0, 1.0 / NLON, 2.0 / NLON)
    total = received[0, :, :ROWS]
    for source in range(1, LON_DEV):
        total = total + received[source, :, :ROWS]
    blank = jnp.zeros((HALF, 64), jnp.float32)
    west = received[(lon + LON_DEV - 1) % LON_DEV, :, ROWS:MORE]
    east = received[(lon + 1) % LON_DEV, :, ROWS:MORE]
    edges[0] = jnp.concatenate([west, blank], axis=1)
    edges[1] = jnp.concatenate([east, blank], axis=1)
    return total * response


def first_respond_kernel(received, tiles, cutoff_in, send, edges, cutoff, sems):
    lon, _ = place()
    finish(*begin(sems, (cutoff_in, cutoff)))
    total = responded(received, cutoff, edges)
    for target in range(LON_DEV):
        send[target, :, :ROWS] = total
        tile = jnp.where(target == (lon + 1) % LON_DEV, tiles[0], tiles[1])
        send[target, :, ROWS:MORE] = tile[:, :64]
        send[target, :, MORE:] = received[(target + LON_DEV // 2) % LON_DEV, :, MORE:]


def second_respond_kernel(received, cutoff_in, mask_in, send, edges, cutoff, mask, sems):
    _, lat = place()
    finish(*begin(sems, (cutoff_in, cutoff), (mask_in, mask)))
    total = responded(received, cutoff, edges)
    near_row = jnp.where(lat == TOP, 0, BAND - 1)
    near = row_waves(total, near_row)
    near = with_lane(near, SLABS, mask[near_row].astype(jnp.float32))
    for target in range(LON_DEV):
        send[target, :, :ROWS] = total
        send[target, :, ROWS:] = near[:, :64]


def gather_terms(value, coeff, south_line, north_line, west_edge, east_edge):
    to_north, to_south = coeff[1] * value, coeff[2] * value
    total = coeff[0] * value
    total = total + jnp.concatenate([south_line, to_north[:-1]], axis=0)
    total = total + jnp.concatenate([to_south[1:], north_line], axis=0)
    total = total + jnp.concatenate([west_edge, (coeff[3] * value)[:, :-1]], axis=1)
    total = total + jnp.concatenate([(coeff[4] * value)[:, 1:], east_edge], axis=1)
    return total, to_north, to_south


def load_coeff(coeff, field, level):
    return [coeff[field, term, level] for term in range(5)]


def row_waves(waves, row):
    picked = iota((ROWS, 128), 0) == iota((ROWS, 128), 1) * BAND + row
    picked = picked.astype(jnp.float32).astype(jnp.bfloat16)
    high, low = split(waves)
    return pair_dot(high, picked, 1, 0) + pair_dot(low, picked, 1, 0)


def across_pole(waves, table, row):
    chosen = row_waves(waves, row)
    chosen = jnp.where(iota((WAVES, 128), 0) % 2 == 1, -chosen, chosen)
    return dot(chosen, table, 0, 0)


def whole_band(closed, opened, top):
    return jnp.where(
        top, jnp.concatenate([opened, closed], axis=0), jnp.concatenate([closed, opened], axis=0)
    )


def middle_kernel(
    waves_in, table_in, mask_in, state_in, extra_in, coeff_in, opened_in, beyond_in,
    send, to_next, next_line, edges, across, middle_out,
    waves, table, mask, state, extra, coeff_ref, opened, beyond, middle,
    filtered, opposite, halos, ends, sems,
):
    lon, lat = place()
    top = lat == TOP
    rows = pl.ds(open_row(lat), HALF)
    waves_copy, table_copy, *rest = begin(
        sems,
        (waves_in, waves),
        (table_in.at[lon], table),
        (mask_in, mask),
        (opened_in, opened),
        (beyond_in, beyond),
        *by_field((state_in.at[:, :, rows], state), (extra_in, extra), (coeff_in, coeff_ref)),
    )
    rest, fields = rest[:3], rest[3:]
    finish(waves_copy, table_copy)
    for tile in range(TILED):
        across[tile_place(tile)] = waves[tile, :, MORE:]
    flat = waves[:, :, :ROWS].reshape(WAVES, ROWS)
    filtered[...] = dot(flat, table[...], 0, 0)
    polar_row = jnp.where(top, BAND - 1, 0)
    opposite[...] = across_pole(flat, table[...], polar_row)
    finish(*rest)
    blank = jnp.zeros((HALF, 64), jnp.float32)
    sides = (lon + LON_DEV - 1) % LON_DEV, (lon + 1) % LON_DEV
    for side in range(2):
        closed = jnp.concatenate([waves[sides[side], :, ROWS:MORE], blank], axis=1)
        edges[side] = whole_band(closed, opened[side], top)
    weight = row_weight(mask, 0, (BAND, WIDTH))
    narrow = row_weight(mask, 0, (BAND, 128))
    edges[2] = narrow
    for side, lane in enumerate((WIDTH + 1 - LAST, WIDTH - LAST)):
        halos[side] = halo_of(edges[side], filtered[:, LAST:], lane, narrow)
    next_weight = jnp.where(top, weight[0:1], weight[BAND - 1 :])
    row = iota((BAND, WIDTH), 0)

    none = jnp.zeros((HALF, WIDTH), jnp.float32)

    def one(field, level, carry):
        slab = field * LEV + level
        here = pl.ds(slab, 1)
        value = whole_band(none, state[field, level], top)
        smooth = filtered[pl.ds(slab * BAND, BAND)]
        value = value + weight * (smooth[:, :WIDTH] - value)
        coeff = load_coeff(coeff_ref, field, level)
        band = pl.ds(slab * BAND, BAND)
        west, east = halos[0, band, 0:1], halos[1, band, 0:1]
        halo = beyond[2, here]
        total, north, south = gather_terms(
            value, coeff, jnp.where(top, halo, 0.0), jnp.where(top, 0.0, halo), west, east
        )
        pole = (across[here] * opposite[here])[:, :WIDTH]
        total = total + jnp.where(row == polar_row, pole, 0.0) + extra[field, level]
        middle[field, level] = total
        product = jnp.where(top, south[0:1], north[BAND - 1 :])
        near = jnp.where(top, total[0:1], total[BAND - 1 :])
        near_coeff = jnp.where(top, coeff[2][0:1], coeff[1][BAND - 1 :])
        to_next[0, here] = product
        to_next[1, here] = jnp.where(next_weight > 0.5, near_coeff, near_coeff * near)
        next_line[here] = beyond[1, here] * (beyond[0, here] + product)
        ends[0, band, : WIDTH - LAST] = (coeff[3] * total)[:, LAST:]
        ends[1, band] = (coeff[4] * total)[:, :128]
        return carry

    stored = []
    for field in range(FIELDS):
        finish(*fields[3 * field : 3 * field + 3])
        for_levels(field, one)
        stored += begin(sems.at[field : field + 1], (middle.at[field, :, rows], middle_out.at[field]))
    sums = dot(table[:, :WIDTH], middle[...].reshape(ROWS, WIDTH), 1, 1)
    send[:, :, :ROWS] = sums.reshape(LON_DEV, SHARE, ROWS)
    east_tile = tile_of(ends[0, :, : WIDTH - LAST], WIDTH - LAST - 1, BAND, open_row(lat))
    west_tile = tile_of(ends[1], 0, BAND, open_row(lat))
    for target in range(LON_DEV):
        tile = jnp.where(target == (lon + 1) % LON_DEV, east_tile, west_tile)
        send[target, :, ROWS:] = tile[:, :64]
    finish(*stored)


def final_kernel(
    waves_in, table_in, middle_in, coeff_in, edges_in, opened_in, line_in, across_in,
    out,
    waves, table, middle, coeff_ref, edges, opened, next_line, across, result,
    filtered, opposite, halos, sems,
):
    lon, lat = place()
    top = lat == TOP
    waves_copy, table_copy, *rest = begin(
        sems,
        (waves_in, waves),
        (table_in.at[lon], table),
        (edges_in, edges),
        (opened_in, opened),
        (line_in, next_line),
        (across_in, across),
        *by_field((middle_in, middle), (coeff_in, coeff_ref)),
    )
    rest, fields = rest[:4], rest[4:]
    finish(waves_copy, table_copy)
    flat = waves[:, :, :ROWS].reshape(WAVES, ROWS)
    filtered[...] = dot(flat, table[...], 0, 0)
    polar_row = jnp.where(top, BAND - 1, 0)
    opposite[...] = across_pole(flat, table[...], polar_row)
    finish(*rest)
    narrow = edges[2]
    weight = jnp.concatenate([narrow] * (WIDE // 128), axis=1)[:, :WIDTH]
    row = iota((BAND, WIDTH), 0)
    none = jnp.zeros((HALF, 128), jnp.float32)
    for side, lane in enumerate((WIDTH + 1 - LAST, WIDTH - LAST)):
        tile = jnp.where(narrow > 0.5, edges[side], whole_band(none, opened[side], top))
        halos[side] = halo_of(tile, filtered[:, LAST:], lane, narrow)

    blank = jnp.zeros((HALF, WIDTH), jnp.float32)

    def one(field, level, carry):
        slab = field * LEV + level
        here = pl.ds(slab, 1)
        value = whole_band(blank, middle[field, level], top)
        smooth = filtered[pl.ds(slab * BAND, BAND)]
        value = value + weight * (smooth[:, :WIDTH] - value)
        coeff = load_coeff(coeff_ref, field, level)
        band = pl.ds(slab * BAND, BAND)
        west, east = halos[0, band, 0:1], halos[1, band, 0:1]
        halo = next_line[here]
        total, _, _ = gather_terms(
            value, coeff, jnp.where(top, halo, 0.0), jnp.where(top, 0.0, halo), west, east
        )
        pole = (across[here] * opposite[here])[:, :WIDTH]
        result[field, level] = total + jnp.where(row == polar_row, pole, 0.0)
        return carry

    stored = []
    for field in range(FIELDS):
        finish(*fields[2 * field : 2 * field + 2])
        for_levels(field, one)
        stored += begin(sems.at[field : field + 1], (result.at[field], out.at[field]))
    finish(*stored)


def edge_kernel(field_in, coeff_in, edges, field, to_east, to_west, sems):
    finish(
        *begin(
            sems,
            (field_in, field),
            (coeff_in.at[:, 3], to_east),
            (coeff_in.at[:, 4], to_west),
        )
    )
    east = west = jnp.zeros((BAND, 128), jnp.float32)
    for slab in range(SLABS):
        at = slab // LEV, slab % LEV
        value = field[at]
        east = with_lane(east, slab, (to_east[at] * value)[:, WIDTH - 1 :])
        west = with_lane(west, slab, (to_west[at] * value)[:, 0:1])
    edges[0] = east
    edges[1] = west


def line_kernel(
    field_in, extra_in, coeff_in, west_in, east_in,
    to_north, to_south, to_polar,
    field_ref, extra, coeff_ref, west_edge, east_edge, sems,
):
    _, lat = place()
    finish(
        *begin(
            sems,
            (field_in, field_ref),
            (extra_in, extra),
            (coeff_in, coeff_ref),
            (west_in, west_edge),
            (east_in, east_edge),
        )
    )
    none = jnp.zeros((1, WIDTH), jnp.float32)

    def one(field, level, carry):
        slab = field * LEV + level
        here = pl.ds(slab, 1)
        coeff = load_coeff(coeff_ref, field, level)
        west, east = lane_of(west_edge[...], slab), lane_of(east_edge[...], slab)
        total, north, south = gather_terms(field_ref[field, level], coeff, none, none, west, east)
        total = total + extra[field, level]
        norths = total[BAND - 1 :], coeff[1][BAND - 1 :], north[BAND - 1 :]
        souths = total[0:1], coeff[2][0:1], south[0:1]
        for part in range(3):
            to_north[part, here] = norths[part]
            to_south[part, here] = souths[part]
            to_polar[part, here] = jnp.where(lat == 1, souths[part], norths[part])
        return carry

    for_slabs(one)


def plain_middle_kernel(
    state_in, extra_in, coeff_in, west_in, east_in, below_in, above_in, polar_in,
    edges, lines, middle_out,
    state, extra, coeff_ref, west_edge, east_edge, below, above, polar, middle, sems,
):
    _, lat = place()
    finish(
        *begin(
            sems,
            (state_in, state),
            (extra_in, extra),
            (coeff_in, coeff_ref),
            (west_in, west_edge),
            (east_in, east_edge),
            (below_in, below),
            (above_in, above),
            (polar_in, polar),
        )
    )

    def one(field, level, carry):
        east_tile, west_tile = carry
        slab = field * LEV + level
        here = pl.ds(slab, 1)
        coeff = load_coeff(coeff_ref, field, level)
        west, east = lane_of(west_edge[...], slab), lane_of(east_edge[...], slab)
        reached = polar[0, here]
        total, north, south = gather_terms(
            state[field, level],
            coeff,
            jnp.where(lat == 1, reached, below[2, here]),
            jnp.where(lat == TOP - 1, reached, above[2, here]),
            west,
            east,
        )
        total = total + extra[field, level]
        middle[field, level] = total
        low = below[1, here] * (below[0, here] + south[0:1])
        high = above[1, here] * (above[0, here] + north[BAND - 1 :])
        lines[0, here] = jnp.where(lat == 1, 0.0, low)
        lines[1, here] = jnp.where(lat == TOP - 1, 0.0, high)
        east_tile = with_lane(east_tile, slab, (coeff[3] * total)[:, WIDTH - 1 :])
        west_tile = with_lane(west_tile, slab, (coeff[4] * total)[:, 0:1])
        return east_tile, west_tile

    none = jnp.zeros((BAND, 128), jnp.float32)
    edges[0], edges[1] = for_slabs(one, (none, none))
    finish(*begin(sems, (middle, middle_out)))


def plain_final_kernel(
    middle_in, coeff_in, west_in, east_in, lines_in, table_in,
    out, part, table,
    middle, coeff_ref, west_edge, east_edge, lines, sems,
):
    lon, lat = place()
    finish(
        *begin(
            sems,
            (middle_in, middle),
            (coeff_in, coeff_ref),
            (west_in, west_edge),
            (east_in, east_edge),
            (lines_in, lines),
            (table_in.at[lon], table),
        )
    )

    def one(field, level, carry):
        slab = field * LEV + level
        here = pl.ds(slab, 1)
        coeff = load_coeff(coeff_ref, field, level)
        west, east = lane_of(west_edge[...], slab), lane_of(east_edge[...], slab)
        value = middle[field, level]
        total = gather_terms(value, coeff, lines[0, here], lines[1, here], west, east)[0]
        out[field, level] = total
        part[field, level] = jnp.where(lat == 1, total[:HALF], total[HALF:])
        return carry

    for_slabs(one)


def reach_kernel(part, waves, table, polar, result_in, result_out, changed, sems):
    _, lat = place()
    bottom = lat == 1
    rows = pl.ds(pl.multiple_of(jnp.where(bottom, 0, HALF), HALF), HALF)

    @pl.when(bottom | (lat == TOP - 1))
    def _():
        flat = waves[:, :, MORE - 128 :].reshape(WAVES, 128)
        smooth = dot(flat, table[...], 0, 0)[64 : 64 + SLABS, :WIDTH]
        masked = flat[0:1, 64 + SLABS : 65 + SLABS] > 0.5
        line = polar[1] * jnp.where(masked, smooth, 1.0)
        row = iota((HALF, WIDTH), 0)
        mine = row == jnp.where(bottom, 0, HALF - 1)
        for slab in range(SLABS):
            at = slab // LEV, slab % LEV
            changed[at] = part[at] + jnp.where(mine, line[slab : slab + 1], 0.0)
        finish(*begin(sems, (changed, result_out.at[:, :, rows])))


def exchanged(chunks):
    return lax.all_to_all(chunks, "lon", split_axis=0, concat_axis=0, tiled=True)


def moved(value, lats, north, east):
    pairs = []
    for lat, lon in [(lat, lon) for lat in lats for lon in range(LON_DEV)]:
        pairs.append((lat * LON_DEV + lon, (lat + north) * LON_DEV + (lon + east) % LON_DEV))
    return lax.ppermute(value, ("lat", "lon"), pairs)


def next_to_pole(value, outward):
    pairs = []
    for lon in range(LON_DEV):
        for polar, other in ((0, 1), (TOP, TOP - 1)):
            pair = polar * LON_DEV + lon, other * LON_DEV + lon
            pairs.append(pair if outward else pair[::-1])
    return lax.ppermute(value, ("lat", "lon"), pairs)


def local(adjoint_state, innovation, coefficients, polar_mask, wave_cutoff):
    lat = lax.axis_index("lat")
    polar = (lat == 0) | (lat == TOP)
    table = jnp.asarray(wave_tables())
    small = pltpu.SMEM((BAND,), jnp.int32)
    plain = range(1, TOP)
    table_scratch = in_vmem((WAVES, WIDE))
    halo_scratch = in_vmem((2, ROWS, 128))
    wave_scratch = [in_vmem((ROWS, WIDE)), in_vmem((128, WIDE)), halo_scratch]
    one_edge = (BAND, 128)

    def blanks(*shapes):
        return tuple(jnp.zeros(shape, jnp.float32) for shape in shapes)

    def polar_first():
        half = in_vmem(HALF_FIELD)
        send, to_polar, to_north, to_south, edge = launch(
            forward_kernel_with_blanks,
            [adjoint_state, coefficients, table, polar_mask],
            [FIRST_CHUNKS],
            [LINES, LINES, LINES, (2, *one_edge)],
            [in_vmem(FIELD), table_scratch, half, half, half, in_vmem(ACROSS), small],
            copies=6,
        )
        received = exchanged(send)
        (tiles,) = launch(closed_kernel, [coefficients], [TILES], (), [half, half], copies=2)
        send, opened = launch(
            first_respond_kernel,
            [received, tiles, wave_cutoff],
            [FIRST_CHUNKS, TILES],
            (),
            [small],
            copies=1,
            near=2,
        )
        return send, opened, to_polar, to_north, to_south, edge

    def plain_first():
        (edges,) = launch(
            edge_kernel,
            [adjoint_state, coefficients],
            [(2, *one_edge)],
            (),
            [in_vmem(FIELD)] * 3,
            copies=3,
        )
        west = moved(edges[0], plain, 0, 1)
        east = moved(edges[1], plain, 0, -1)
        to_north, to_south, to_polar = launch(
            line_kernel,
            [adjoint_state, innovation, coefficients, west, east],
            [LINES, LINES, LINES],
            (),
            [in_vmem(FIELD), in_vmem(FIELD), in_vmem(COEFF), in_vmem(one_edge), in_vmem(one_edge)],
            copies=5,
        )
        send, opened = blanks(FIRST_CHUNKS, TILES)
        return send, opened, to_polar, to_north, to_south, jnp.stack([west, east])

    send, opened, to_polar, to_north, to_south, edge = lax.cond(polar, polar_first, plain_first)
    beyond = next_to_pole(to_polar, False)

    def polar_second():
        return exchanged(send), to_north, to_south

    def plain_second():
        below = moved(to_north, range(1, TOP - 1), 1, 0)
        above = moved(to_south, range(2, TOP), -1, 0)
        return *blanks(FIRST_CHUNKS), below, above

    waves, below, above = lax.cond(polar, polar_second, plain_second)

    def polar_third():
        return tuple(launch(
            middle_kernel,
            [waves, table, polar_mask, adjoint_state, innovation, coefficients, opened, beyond],
            [CHUNKS, (2, *LINE), LINE, EDGES, ACROSS],
            [HALF_FIELD],
            [in_vmem(FIRST_CHUNKS), table_scratch, small, in_vmem(HALF_FIELD), in_vmem(FIELD), in_vmem(COEFF)]
            + [in_vmem(TILES), in_vmem(LINES), in_vmem(FIELD), *wave_scratch, halo_scratch],
            copies=14,
        ))

    def plain_third():
        return blanks(CHUNKS, (2, *LINE), LINE, EDGES, ACROSS, HALF_FIELD)

    send, to_next, next_line, edges, across, middle = lax.cond(polar, polar_third, plain_third)
    reached = next_to_pole(to_next, True)

    def polar_fourth():
        received = exchanged(send)
        again, opened = launch(
            second_respond_kernel,
            [received, wave_cutoff, polar_mask],
            [CHUNKS, TILES],
            (),
            [small, small],
            copies=2,
            near=1,
        )
        return exchanged(again), opened

    waves, opened = lax.cond(polar, polar_fourth, lambda: blanks(CHUNKS, TILES))
    reached, waves = lax.optimization_barrier((reached, waves))

    def polar_wait():
        return tuple(launch(lambda *_: None, [], (), [FIELD, HALF_FIELD, (WAVES, WIDE)], copies=1))

    def plain_fourth():
        west, east = edge[0], edge[1]
        second, lines, middle = launch(
            plain_middle_kernel,
            [adjoint_state, innovation, coefficients, west, east, below, above, reached],
            [(2, *one_edge), (2, *LINE)],
            [FIELD],
            [in_vmem(FIELD), in_vmem(FIELD), in_vmem(COEFF), in_vmem(one_edge), in_vmem(one_edge)]
            + [in_vmem(LINES), in_vmem(LINES), in_vmem((2, *LINE)), in_vmem(FIELD)],
            copies=8,
        )
        west = moved(second[0], plain, 0, 1)
        east = moved(second[1], plain, 0, -1)
        result, part, own_table = launch(
            plain_final_kernel,
            [middle, coefficients, west, east, lines, table],
            [FIELD, HALF_FIELD, (WAVES, WIDE)],
            (),
            [in_vmem(FIELD), in_vmem(COEFF), in_vmem(one_edge), in_vmem(one_edge), in_vmem((2, *LINE))],
            copies=6,
        )
        return result, part, own_table

    result, part, own_table = lax.cond(polar, polar_wait, plain_fourth)
    waves_beyond = next_to_pole(waves, True)

    def polar_fifth():
        (out,) = launch(
            final_kernel,
            [waves, table, middle, coefficients, edges, opened, next_line, across],
            (),
            [FIELD],
            [in_vmem(CHUNKS), table_scratch, in_vmem(HALF_FIELD), in_vmem(COEFF), in_vmem(EDGES)]
            + [in_vmem(TILES), in_vmem(LINE), in_vmem(ACROSS), in_vmem(FIELD), *wave_scratch],
            copies=12,
            pinned=True,
        )
        return out

    result = lax.cond(polar, polar_fifth, lambda kept=result: kept)
    (out,) = launch(
        reach_kernel,
        [part, waves_beyond, own_table, reached, result],
        (),
        [FIELD],
        [in_vmem(HALF_FIELD)],
        copies=1,
        aliases={4: 0},
        near=4,
        pinned=True,
    )
    return out


def forward_kernel_with_blanks(*refs):
    forward_kernel(*refs[:5], *refs[9:])


def solution(mesh):
    return jax.shard_map(
        local,
        mesh=mesh,
        in_specs=(
            P(None, None, "lat", "lon"),
            P(None, None, "lat", "lon"),
            P(None, None, None, "lat", "lon"),
            P("lat"),
            P("lat"),
        ),
        out_specs=P(None, None, "lat", "lon"),
        check_vma=False,
    )
```
